32 devices in a mesh: fsdp: 8 (over z, y), context: 2 (over x), tensor: 2 (over core).
Axes of the slice: x: 2, y: 2, z: 4, core: 2. Of those that a mesh axis runs over, the one named last changes fastest.
Arguments:
- hidden_in: bfloat16 [8, 1024, 1024], P('fsdp', 'context', 'tensor')
- cotangent: bfloat16 [8, 1024, 1024], P('fsdp', 'context', 'tensor'), may hold values from -6 to 6
- segment: int32 [8, 1024], P('fsdp', 'context'), may hold values from 0 to 2, as said below
- position: int32 [8, 1024], P('fsdp', 'context'), may hold values from 0 to 1021, as said below
- w_query: bfloat16 [1024, 2048], P('fsdp', 'tensor'), may hold values from -0.1875 to 0.1875
- w_key: bfloat16 [1024, 1024], P('fsdp', 'tensor'), may hold values from -0.1875 to 0.1875
- w_value: bfloat16 [1024, 1024], P('fsdp', 'tensor'), may hold values from -0.1875 to 0.1875
- w_output: bfloat16 [2048, 1024], P('tensor', 'fsdp'), may hold values from -1 to 1
- w_gate: bfloat16 [1024, 3072], P('fsdp', 'tensor'), may hold values from -0.1875 to 0.1875
- w_up: bfloat16 [1024, 3072], P('fsdp', 'tensor'), may hold values from -0.1875 to 0.1875
- w_down: bfloat16 [3072, 1024], P('tensor', 'fsdp'), may hold values from -0.109375 to 0.109375
- attn_gain: bfloat16 [1024], P('fsdp'), may hold values from 0.099609375 to 1.8984375
- ffn_gain: bfloat16 [1024], P('fsdp'), may hold values from 0.099609375 to 1.8984375
- query_gain: bfloat16 [128], P('fsdp'), may hold values from 0.099609375 to 1.8984375
- key_gain: bfloat16 [128], P('fsdp'), may hold values from 0.099609375 to 1.8984375
Outputs:
- block_out: bfloat16 [8, 1024, 1024], P('fsdp', 'context', 'tensor')
- grad_input: float32 [8, 1024, 1024], P('fsdp', 'context', 'tensor')
- grad_w_query: float32 [1024, 2048], P('fsdp', 'tensor')
- grad_w_key: float32 [1024, 1024], P('fsdp', 'tensor')
- grad_w_value: float32 [1024, 1024], P('fsdp', 'tensor')
- grad_w_output: float32 [2048, 1024], P('tensor', 'fsdp')
- grad_w_gate: float32 [1024, 3072], P('fsdp', 'tensor')
- grad_w_up: float32 [1024, 3072], P('fsdp', 'tensor')
- grad_w_down: float32 [3072, 1024], P('tensor', 'fsdp')
- grad_attn_gain: float32 [1024], P('fsdp')
- grad_ffn_gain: float32 [1024], P('fsdp')
- grad_query_gain: float32 [128], P('fsdp')
- grad_key_gain: float32 [128], P('fsdp')
The draws below stay inside these ranges and needn't reach their ends.
Inputs may be any that keep to these rules, and one draw needn't show every extreme that they name: `segment`: in every sequence the numbers never fall and all of 0, 1 and 2 occur; document 1 begins within the first 512 tokens (never at the first) and ends within the last 512 (never at the last); in one sequence of each draw it spans every token but the first and the last. `position`: 0 at each document's first token and rising by one along the document.
All inputs are finite; a program needn't handle non-finite values.
Results may differ from the reference program's by a relative error of at most 0.024.
Values may be sent and summed in bfloat16 or wider, within the bound.
No kernel may reach another device: no remote copies, remote signals or barrier semaphores. Data moves between devices by JAX's collectives and lax.ppermute only.
A program may use at most 192 MiB of HBM per device.

```python
import jax
import jax.numpy as jnp
from jax import lax

D = 1024
FF = 3072
HEADS = 16
KV_HEADS = 8
HEAD = 128
SEQ_LEN = 1024
TOK_DEV = 512
SEQUENCES = 8


def draw_hidden_in(key, part):
    key = jax.random.fold_in(key, 11)
    base_key, row_key, column_key = jax.random.split(key, 3)
    values = jax.random.normal(base_key, (SEQUENCES, SEQ_LEN, D), jnp.float32)
    row_scale = jnp.exp(jax.random.uniform(row_key, (SEQUENCES, SEQ_LEN, 1), jnp.float32, jnp.log(0.3), jnp.log(3.0)))
    column_scale = jnp.exp(jax.random.uniform(column_key, (1, 1, D), jnp.float32, jnp.log(0.5), jnp.log(2.0)))
    return (values * row_scale * column_scale).astype(jnp.bfloat16)


def document_bounds(key):
    first_key, last_key, pick_key = jax.random.split(key, 3)
    doc_begin = jax.random.randint(first_key, (SEQUENCES, 1), 1, TOK_DEV).astype(jnp.int32)
    doc_finish = jax.random.randint(last_key, (SEQUENCES, 1), SEQ_LEN - TOK_DEV + 1, SEQ_LEN).astype(jnp.int32)
    chosen = jax.random.randint(pick_key, (), 0, SEQUENCES).astype(jnp.int32)
    is_chosen = (jnp.arange(SEQUENCES, dtype=jnp.int32) == chosen)[:, None]
    doc_begin = jnp.where(is_chosen, jnp.int32(1), doc_begin)
    doc_finish = jnp.where(is_chosen, jnp.int32(SEQ_LEN - 1), doc_finish)
    token_index = jnp.arange(SEQ_LEN, dtype=jnp.int32)[None, :]
    return (doc_begin, doc_finish, token_index)


def draw_segment(key, part):
    doc_begin, doc_finish, token_index = document_bounds(key)
    return (token_index >= doc_begin).astype(jnp.int32) + (token_index >= doc_finish).astype(jnp.int32)


def draw_position(key, part):
    doc_begin, doc_finish, token_index = document_bounds(key)
    inside = jnp.where(token_index >= doc_begin, token_index - doc_begin, token_index)
    return jnp.where(token_index >= doc_finish, token_index - doc_finish, inside).astype(jnp.int32)


def block_scale(key, dims, cuts, smallest, top_value):
    factor_of = 1.0
    for dim, shards_of in cuts:
        heights = jax.random.uniform(jax.random.fold_in(jax.random.fold_in(key, 6), dim), (shards_of,), jnp.float32, smallest / len(cuts), top_value / len(cuts))
        factor_of = factor_of * jnp.repeat(jnp.exp(heights), dims[dim] // shards_of).reshape((-1,) + (1,) * (len(dims) - 1 - dim))
    return factor_of


def noise(stream_key, extent, scale, bound, pieces=(), kind=jnp.bfloat16):
    factor_of = block_scale(stream_key, extent, pieces, -0.22, 0.18) if pieces else 1.0
    array = jax.random.normal(stream_key, extent, jnp.float32) * scale * factor_of
    return jnp.minimum(jnp.maximum(array, -bound), bound).astype(kind)


def setup_inputs(seed: int = 0) -> dict:
    streams_of = jax.random.split(jax.random.key(seed), 16)
    hidden_in = draw_hidden_in(jax.random.fold_in(streams_of[15], 71), 0)
    cotangent = noise(streams_of[1], (SEQUENCES, SEQ_LEN, D), 1.0, 6.0, ((0, 8), (1, 2), (2, 2)))
    segment = draw_segment(jax.random.fold_in(streams_of[15], 71), 0)
    position = draw_position(jax.random.fold_in(streams_of[15], 71), 0)
    w_query = noise(streams_of[4], (D, HEADS * HEAD), D ** -0.5, 0.1875, ((0, 8), (1, 2)))
    w_key = noise(streams_of[5], (D, KV_HEADS * HEAD), D ** -0.5, 0.1875, ((0, 8), (1, 2)))
    w_value = noise(streams_of[6], (D, KV_HEADS * HEAD), D ** -0.5, 0.1875, ((0, 8), (1, 2)))
    w_output = noise(streams_of[7], (HEADS * HEAD, D), (HEADS * HEAD // 64) ** -0.5, 1.0, ((0, 2), (1, 8)))
    w_gate = noise(streams_of[8], (D, FF), D ** -0.5, 0.1875, ((0, 8), (1, 2)))
    w_up = noise(streams_of[9], (D, FF), D ** -0.5, 0.1875, ((0, 8), (1, 2)))
    w_down = noise(streams_of[10], (FF, D), FF ** -0.5, 0.109375, ((0, 2), (1, 8)))
    attn_gain = jnp.clip(1.0 + 0.18 * jax.random.normal(streams_of[11], (D,), jnp.float32), 0.099609375, 1.8984375).astype(jnp.bfloat16)
    ffn_gain = jnp.clip(1.0 + 0.18 * jax.random.normal(streams_of[12], (D,), jnp.float32), 0.099609375, 1.8984375).astype(jnp.bfloat16)
    query_gain = jnp.clip(1.0 + 0.18 * jax.random.normal(streams_of[13], (HEAD,), jnp.float32), 0.099609375, 1.8984375).astype(jnp.bfloat16)
    key_gain = jnp.clip(1.0 + 0.18 * jax.random.normal(streams_of[14], (HEAD,), jnp.float32), 0.099609375, 1.8984375).astype(jnp.bfloat16)
    return {"hidden_in": hidden_in, "cotangent": cotangent, "segment": segment, "position": position, "w_query": w_query, "w_key": w_key, "w_value": w_value, "w_output": w_output, "w_gate": w_gate, "w_up": w_up, "w_down": w_down, "attn_gain": attn_gain, "ffn_gain": ffn_gain, "query_gain": query_gain, "key_gain": key_gain}


EPS = 1e-06
THETA = 1000000.0
HIGH = lax.Precision.HIGHEST

@jax.custom_vjp
def low(v):
    return lax.optimization_barrier(v.astype(jnp.bfloat16)).astype(jnp.float32)

@jax.custom_vjp
def low_back(v):
    return v

def low_keep(v):
    return (low(v), None)

def low_pass(kept, grad):
    return (grad,)

def back_keep(v):
    return (v, None)

def back_low(kept, grad):
    return (low(grad),)
low.defvjp(low_keep, low_pass)
low_back.defvjp(back_keep, back_low)

def norm_rows(values, gain_vec):
    return values * lax.rsqrt(lax.optimization_barrier(jnp.mean(values * values, axis=-1, keepdims=True)) + EPS) * gain_vec

def rotate(values, position_row):
    half_size = HEAD // 2
    freq_table = THETA ** (-jnp.arange(half_size, dtype=jnp.float32) * 2.0 / HEAD)
    angle_table = position_row.astype(jnp.float32)[:, None] * freq_table[None, :]
    cosine_table = jnp.cos(angle_table)[:, None, :]
    sine_table = jnp.sin(angle_table)[:, None, :]
    first_half = values[..., :half_size]
    second_half = values[..., half_size:]
    return jnp.concatenate([first_half * cosine_table - second_half * sine_table, second_half * cosine_table + first_half * sine_table], axis=-1)

def one_sequence(tokens_in, segment_row, position_row, params):
    wq_mat, wk_mat, wv_mat, wo_mat, wg_mat, wu_mat, wd_mat, attn_gvec, ffn_gvec, query_gvec, key_gvec = params
    attn_in = low(norm_rows(tokens_in, attn_gvec))
    query_raw = low_back(jnp.dot(attn_in, wq_mat, precision=HIGH))
    key_raw = low_back(jnp.dot(attn_in, wk_mat, precision=HIGH))
    value_raw = low_back(jnp.dot(attn_in, wv_mat, precision=HIGH))
    query_rot = low(rotate(norm_rows(query_raw.reshape(SEQ_LEN, HEADS, HEAD), query_gvec), position_row))
    key_rot = low(rotate(norm_rows(key_raw.reshape(SEQ_LEN, KV_HEADS, HEAD), key_gvec), position_row))
    value_low = low(value_raw).reshape(SEQ_LEN, KV_HEADS, HEAD)
    query_group = query_rot.reshape(SEQ_LEN, KV_HEADS, HEADS // KV_HEADS, HEAD)
    block_rows = min(512, SEQ_LEN)
    key_index = jnp.arange(SEQ_LEN, dtype=jnp.int32)

    def attend(first_row):
        rows_query = lax.dynamic_slice_in_dim(query_group, first_row, block_rows, 0)
        rows_segment = lax.dynamic_slice_in_dim(segment_row, first_row, block_rows, 0)
        rows_index = first_row + jnp.arange(block_rows, dtype=jnp.int32)
        raw_scores = low_back(jnp.einsum('pkgd,lkd->kgpl', rows_query, key_rot, precision=HIGH) * HEAD ** (-0.5))
        allowed = (rows_segment[:, None] == segment_row[None, :]) & (key_index[None, :] <= rows_index[:, None])
        masked = jnp.where(allowed, raw_scores, -1e+30)
        probs_low = low(jax.nn.softmax(masked, axis=-1))
        return jnp.einsum('kgpl,lkd->pkgd', probs_low, value_low, precision=HIGH)
    block_starts = (jnp.arange(SEQ_LEN // block_rows) * block_rows).astype(jnp.int32)
    attn_rows = lax.map(jax.checkpoint(attend), block_starts).reshape(SEQ_LEN, HEADS * HEAD)
    attn_low = low(low_back(attn_rows))
    mid_rows = tokens_in + low_back(jnp.dot(attn_low, wo_mat, precision=HIGH))
    ffn_in = low(norm_rows(mid_rows, ffn_gvec))
    gate_pre = low_back(jnp.dot(ffn_in, wg_mat, precision=HIGH))
    up_pre = low_back(jnp.dot(ffn_in, wu_mat, precision=HIGH))
    hidden_low = low(jax.nn.silu(gate_pre) * up_pre)
    return mid_rows + low_back(jnp.dot(hidden_low, wd_mat, precision=HIGH))

def reference(hidden_in, cotangent, segment, position, w_query, w_key, w_value, w_output, w_gate, w_up, w_down, attn_gain, ffn_gain, query_gain, key_gain):
    params = (w_query.astype(jnp.float32), w_key.astype(jnp.float32), w_value.astype(jnp.float32), w_output.astype(jnp.float32), w_gate.astype(jnp.float32), w_up.astype(jnp.float32), w_down.astype(jnp.float32), attn_gain.astype(jnp.float32), ffn_gain.astype(jnp.float32), query_gain.astype(jnp.float32), key_gain.astype(jnp.float32))
    tokens_all = hidden_in.astype(jnp.float32)

    def forward(tokens_arg, params_arg):

        def per_item(sequence_item):
            return jax.checkpoint(one_sequence)(sequence_item[0], sequence_item[1], sequence_item[2], params_arg)
        return lax.map(per_item, (tokens_arg, segment, position))
    result, pullback = jax.vjp(forward, tokens_all, params)
    grad_tokens, grad_params = pullback(cotangent.astype(jnp.float32))
    return (result.astype(jnp.bfloat16), grad_tokens, grad_params[0], grad_params[1], grad_params[2], grad_params[3], grad_params[4], grad_params[5], grad_params[6], grad_params[7], grad_params[8], grad_params[9], grad_params[10])
```

```python
import jax
import jax.numpy as jnp
from jax import lax
from jax.experimental import pallas as pl
from jax.experimental.pallas import tpu as pltpu
from jax.sharding import PartitionSpec as P

EPS = 1e-06
THETA = 1000000.0


def norm_stats(values):
    return lax.rsqrt(jnp.mean(values * values, axis=-1, keepdims=True) + EPS)


def norm_back(grad_out, normed, recip_root):
    return recip_root * (grad_out - normed * jnp.mean(grad_out * normed, axis=-1, keepdims=True))


def rotary_tables(position_row, head_size):
    half_size = head_size // 2
    freq_table = THETA ** (-jnp.arange(half_size, dtype=jnp.float32) * 2.0 / head_size)
    angle_table = position_row.astype(jnp.float32)[:, None] * freq_table[None, :]
    return (jnp.cos(angle_table)[:, None, :], jnp.sin(angle_table)[:, None, :])


def rotate(values, cosine_table, sine_table, turn_sign):
    half_size = values.shape[-1] // 2
    first_half = values[..., :half_size]
    second_half = values[..., half_size:]
    turned = turn_sign * sine_table
    return jnp.concatenate(
        [
            first_half * cosine_table - second_half * turned,
            second_half * cosine_table + first_half * turned,
        ],
        axis=-1,
    )


def plain_shards(
    hidden_in,
    cotangent,
    segment,
    position,
    w_query,
    w_key,
    w_value,
    w_output,
    w_gate,
    w_up,
    w_down,
    attn_gain,
    ffn_gain,
    query_gain,
    key_gain,
):
    (
        wq_full,
        wk_full,
        wv_full,
        wo_full,
        wg_full,
        wu_full,
        wd_full,
        attn_full,
        ffn_full,
        qgain_full,
        kgain_full,
    ) = (
        lax.all_gather(w_query, "fsdp", axis=0, tiled=True),
        lax.all_gather(w_key, "fsdp", axis=0, tiled=True),
        lax.all_gather(w_value, "fsdp", axis=0, tiled=True),
        lax.all_gather(w_output, "fsdp", axis=1, tiled=True),
        lax.all_gather(w_gate, "fsdp", axis=0, tiled=True),
        lax.all_gather(w_up, "fsdp", axis=0, tiled=True),
        lax.all_gather(w_down, "fsdp", axis=1, tiled=True),
        lax.all_gather(attn_gain, "fsdp", axis=0, tiled=True),
        lax.all_gather(ffn_gain, "fsdp", axis=0, tiled=True),
        lax.all_gather(query_gain, "fsdp", axis=0, tiled=True),
        lax.all_gather(key_gain, "fsdp", axis=0, tiled=True),
    )
    rows_x, rows_dy = (
        lax.all_gather(hidden_in[0], "tensor", axis=1, tiled=True),
        lax.all_gather(cotangent[0], "tensor", axis=1, tiled=True),
    )
    tok_count = rows_x.shape[0]
    feat_part = hidden_in.shape[2]
    head_size = qgain_full.shape[0]
    q_heads = wq_full.shape[1] // head_size
    kv_heads = wk_full.shape[1] // head_size
    group_size = q_heads // kv_heads
    score_scale = head_size ** (-0.5)
    x_rows = rows_x.astype(jnp.float32)
    recip_one = norm_stats(x_rows)
    normed_one = x_rows * recip_one
    attn_gain32 = attn_full.astype(jnp.float32)
    attn_in = (normed_one * attn_gain32).astype(jnp.bfloat16)
    query_raw = jnp.dot(attn_in, wq_full, preferred_element_type=jnp.float32).reshape(
        tok_count, q_heads, head_size
    )
    key_raw = jnp.dot(attn_in, wk_full, preferred_element_type=jnp.float32).reshape(
        tok_count, kv_heads, head_size
    )
    value_raw = jnp.dot(attn_in, wv_full, preferred_element_type=jnp.float32)
    cosine_table, sine_table = rotary_tables(position[0], head_size)
    recip_query = norm_stats(query_raw)
    query_hat = query_raw * recip_query
    qgain32 = qgain_full.astype(jnp.float32)
    query_rot = rotate(query_hat * qgain32, cosine_table, sine_table, 1.0).astype(jnp.bfloat16)
    recip_key = norm_stats(key_raw)
    key_hat = key_raw * recip_key
    kgain32 = kgain_full.astype(jnp.float32)
    key_rot = rotate(key_hat * kgain32, cosine_table, sine_table, 1.0).astype(jnp.bfloat16)
    value_low = value_raw.astype(jnp.bfloat16).reshape(tok_count, kv_heads, head_size)
    key_all, value_all, segment_all = (
        lax.all_gather(key_rot, "context", axis=0, tiled=True),
        lax.all_gather(value_low, "context", axis=0, tiled=True),
        lax.all_gather(segment[0], "context", axis=0, tiled=True),
    )
    query_index = lax.axis_index("context") * tok_count + jnp.arange(tok_count, dtype=jnp.int32)
    key_index = jnp.arange(key_all.shape[0], dtype=jnp.int32)
    allowed = (segment[0][:, None] == segment_all[None, :]) & (
        key_index[None, :] <= query_index[:, None]
    )
    query_group = query_rot.reshape(tok_count, kv_heads, group_size, head_size)

    def scores_of():
        raw_scores = (
            jnp.einsum("pkgd,lkd->kgpl", query_group, key_all, preferred_element_type=jnp.float32)
            * score_scale
        )
        return jnp.where(allowed, raw_scores, -1e30)

    masked = scores_of()
    row_max = jnp.max(masked, axis=-1, keepdims=True)
    exp_terms = jnp.exp(masked - row_max)
    row_total = jnp.sum(exp_terms, axis=-1, keepdims=True)
    log_total = row_max + jnp.log(row_total)
    probs_fwd = (exp_terms / row_total).astype(jnp.bfloat16)
    attn_rows = jnp.einsum(
        "kgpl,lkd->pkgd", probs_fwd, value_all, preferred_element_type=jnp.float32
    )
    attn_low = attn_rows.reshape(tok_count, q_heads * head_size).astype(jnp.bfloat16)
    attn_sum = lax.psum(
        jnp.dot(attn_low, wo_full, preferred_element_type=jnp.float32).astype(jnp.bfloat16),
        "tensor",
    ).astype(jnp.float32)
    mid_rows = x_rows + attn_sum
    recip_two = norm_stats(mid_rows)
    normed_two = mid_rows * recip_two
    ffn_gain32 = ffn_full.astype(jnp.float32)
    ffn_in = (normed_two * ffn_gain32).astype(jnp.bfloat16)
    gate_pre = jnp.dot(ffn_in, wg_full, preferred_element_type=jnp.float32)
    up_pre = jnp.dot(ffn_in, wu_full, preferred_element_type=jnp.float32)
    gate_sig = jax.nn.sigmoid(gate_pre)
    gate_act = gate_pre * gate_sig
    hidden_low = (gate_act * up_pre).astype(jnp.bfloat16)
    ffn_rows = lax.psum_scatter(
        jnp.dot(hidden_low, wd_full, preferred_element_type=jnp.float32).astype(jnp.bfloat16),
        "tensor",
        scatter_dimension=1,
        tiled=True,
    ).astype(jnp.float32)
    feat_first = lax.axis_index("tensor") * feat_part
    mid_part = lax.dynamic_slice_in_dim(mid_rows, feat_first, feat_part, 1)
    block_out = (mid_part + ffn_rows).astype(jnp.bfloat16)[None]
    (
        wq_full,
        wk_full,
        wv_full,
        wo_full,
        wg_full,
        wu_full,
        wd_full,
        attn_full,
        ffn_full,
        qgain_full,
        kgain_full,
    ) = (
        lax.all_gather(w_query, "fsdp", axis=0, tiled=True),
        lax.all_gather(w_key, "fsdp", axis=0, tiled=True),
        lax.all_gather(w_value, "fsdp", axis=0, tiled=True),
        lax.all_gather(w_output, "fsdp", axis=1, tiled=True),
        lax.all_gather(w_gate, "fsdp", axis=0, tiled=True),
        lax.all_gather(w_up, "fsdp", axis=0, tiled=True),
        lax.all_gather(w_down, "fsdp", axis=1, tiled=True),
        lax.all_gather(attn_gain, "fsdp", axis=0, tiled=True),
        lax.all_gather(ffn_gain, "fsdp", axis=0, tiled=True),
        lax.all_gather(query_gain, "fsdp", axis=0, tiled=True),
        lax.all_gather(key_gain, "fsdp", axis=0, tiled=True),
    )
    grad_w_down = jnp.einsum("pf,pd->fd", hidden_low, rows_dy, preferred_element_type=jnp.float32)
    grad_hidden = jnp.einsum("pd,fd->pf", rows_dy, wd_full, preferred_element_type=jnp.float32)
    grad_gate = (grad_hidden * up_pre * gate_sig * (1.0 + gate_pre * (1.0 - gate_sig))).astype(
        jnp.bfloat16
    )
    grad_up_pre = (grad_hidden * gate_act).astype(jnp.bfloat16)
    grad_w_gate = jnp.einsum("pd,pf->df", ffn_in, grad_gate, preferred_element_type=jnp.float32)
    grad_w_up = jnp.einsum("pd,pf->df", ffn_in, grad_up_pre, preferred_element_type=jnp.float32)
    ffn_in_part = jnp.einsum(
        "pf,df->pd", grad_gate, wg_full, preferred_element_type=jnp.float32
    ) + jnp.einsum("pf,df->pd", grad_up_pre, wu_full, preferred_element_type=jnp.float32)
    grad_ffn_in = lax.psum(ffn_in_part.astype(jnp.bfloat16), "tensor").astype(jnp.float32)
    grad_ffn_gain = jnp.sum(grad_ffn_in * normed_two, axis=0)
    grad_mid = rows_dy.astype(jnp.float32) + norm_back(
        grad_ffn_in * ffn_gain32, normed_two, recip_two
    )
    grad_mid_low = grad_mid.astype(jnp.bfloat16)
    grad_w_output = jnp.einsum(
        "pf,pd->fd", attn_low, grad_mid_low, preferred_element_type=jnp.float32
    )
    grad_attn = jnp.einsum("pd,fd->pf", grad_mid_low, wo_full, preferred_element_type=jnp.float32)
    grad_attn = grad_attn.astype(jnp.bfloat16).reshape(tok_count, kv_heads, group_size, head_size)
    soft_probs = jnp.exp(scores_of() - log_total)
    grad_probs = jnp.einsum(
        "pkgd,lkd->kgpl", grad_attn, value_all, preferred_element_type=jnp.float32
    )
    row_delta = jnp.sum(soft_probs * grad_probs, axis=-1, keepdims=True)
    grad_scores = (soft_probs * (grad_probs - row_delta)).astype(jnp.bfloat16)
    probs_low = soft_probs.astype(jnp.bfloat16)
    grad_query = (
        jnp.einsum("kgpl,lkd->pkgd", grad_scores, key_all, preferred_element_type=jnp.float32)
        * score_scale
    )
    grad_query = grad_query.reshape(tok_count, q_heads, head_size)
    grad_key_rows = (
        jnp.einsum("kgpl,pkgd->lkd", grad_scores, query_group, preferred_element_type=jnp.float32)
        * score_scale
    )
    grad_value_rows = jnp.einsum(
        "kgpl,pkgd->lkd", probs_low, grad_attn, preferred_element_type=jnp.float32
    )
    key_value_grads = lax.psum_scatter(
        jnp.concatenate(
            [
                grad_key_rows.reshape(tok_count * lax.axis_size("context"), -1),
                grad_value_rows.reshape(tok_count * lax.axis_size("context"), -1),
            ],
            axis=1,
        ).astype(jnp.bfloat16),
        "context",
        scatter_dimension=0,
        tiled=True,
    ).astype(jnp.float32)
    kv_width = kv_heads * head_size
    grad_key = key_value_grads[:, :kv_width].reshape(tok_count, kv_heads, head_size)
    grad_value_low = key_value_grads[:, kv_width:].astype(jnp.bfloat16)
    unrot_query = rotate(grad_query, cosine_table, sine_table, -1.0)
    grad_query_gain = jnp.sum(unrot_query * query_hat, axis=(0, 1))
    grad_query_raw = (
        norm_back(unrot_query * qgain32, query_hat, recip_query)
        .astype(jnp.bfloat16)
        .reshape(tok_count, q_heads * head_size)
    )
    unrot_key = rotate(grad_key, cosine_table, sine_table, -1.0)
    grad_key_gain = jnp.sum(unrot_key * key_hat, axis=(0, 1))
    grad_key_raw = (
        norm_back(unrot_key * kgain32, key_hat, recip_key)
        .astype(jnp.bfloat16)
        .reshape(tok_count, kv_width)
    )
    grad_w_query = jnp.einsum(
        "pd,pf->df", attn_in, grad_query_raw, preferred_element_type=jnp.float32
    )
    grad_w_key = jnp.einsum("pd,pf->df", attn_in, grad_key_raw, preferred_element_type=jnp.float32)
    grad_w_value = jnp.einsum(
        "pd,pf->df", attn_in, grad_value_low, preferred_element_type=jnp.float32
    )
    attn_in_part = (
        jnp.einsum("pf,df->pd", grad_query_raw, wq_full, preferred_element_type=jnp.float32)
        + jnp.einsum("pf,df->pd", grad_key_raw, wk_full, preferred_element_type=jnp.float32)
        + jnp.einsum("pf,df->pd", grad_value_low, wv_full, preferred_element_type=jnp.float32)
    )
    grad_attn_in, grad_query_gain, grad_key_gain = (
        lax.psum(attn_in_part.astype(jnp.bfloat16), "tensor").astype(jnp.float32),
        lax.psum(grad_query_gain.astype(jnp.bfloat16), "tensor").astype(jnp.float32),
        lax.psum(grad_key_gain.astype(jnp.bfloat16), "tensor").astype(jnp.float32),
    )
    grad_attn_gain = jnp.sum(grad_attn_in * normed_one, axis=0)
    grad_input = grad_mid + norm_back(
        grad_attn_in * attn_full.astype(jnp.float32), normed_one, recip_one
    )
    grad_input_part = lax.dynamic_slice_in_dim(grad_input, feat_first, feat_part, 1)[None]
    owned = (
        lax.psum_scatter(
            grad_w_query.astype(jnp.bfloat16), "fsdp", scatter_dimension=0, tiled=True
        ).astype(jnp.float32),
        lax.psum_scatter(
            grad_w_key.astype(jnp.bfloat16), "fsdp", scatter_dimension=0, tiled=True
        ).astype(jnp.float32),
        lax.psum_scatter(
            grad_w_value.astype(jnp.bfloat16), "fsdp", scatter_dimension=0, tiled=True
        ).astype(jnp.float32),
        lax.psum_scatter(
            grad_w_output.astype(jnp.bfloat16), "fsdp", scatter_dimension=1, tiled=True
        ).astype(jnp.float32),
        lax.psum_scatter(
            grad_w_gate.astype(jnp.bfloat16), "fsdp", scatter_dimension=0, tiled=True
        ).astype(jnp.float32),
        lax.psum_scatter(
            grad_w_up.astype(jnp.bfloat16), "fsdp", scatter_dimension=0, tiled=True
        ).astype(jnp.float32),
        lax.psum_scatter(
            grad_w_down.astype(jnp.bfloat16), "fsdp", scatter_dimension=1, tiled=True
        ).astype(jnp.float32),
        lax.psum_scatter(
            grad_attn_gain.astype(jnp.bfloat16), "fsdp", scatter_dimension=0, tiled=True
        ).astype(jnp.float32),
        lax.psum_scatter(
            grad_ffn_gain.astype(jnp.bfloat16), "fsdp", scatter_dimension=0, tiled=True
        ).astype(jnp.float32),
        lax.psum_scatter(
            grad_query_gain.astype(jnp.bfloat16), "fsdp", scatter_dimension=0, tiled=True
        ).astype(jnp.float32),
        lax.psum_scatter(
            grad_key_gain.astype(jnp.bfloat16), "fsdp", scatter_dimension=0, tiled=True
        ).astype(jnp.float32),
    )
    owned = (
        lax.psum(owned[0].astype(jnp.bfloat16), "context").astype(jnp.float32),
        lax.psum(owned[1].astype(jnp.bfloat16), "context").astype(jnp.float32),
        lax.psum(owned[2].astype(jnp.bfloat16), "context").astype(jnp.float32),
        lax.psum(owned[3].astype(jnp.bfloat16), "context").astype(jnp.float32),
        lax.psum(owned[4].astype(jnp.bfloat16), "context").astype(jnp.float32),
        lax.psum(owned[5].astype(jnp.bfloat16), "context").astype(jnp.float32),
        lax.psum(owned[6].astype(jnp.bfloat16), "context").astype(jnp.float32),
        lax.psum(owned[7].astype(jnp.bfloat16), "context").astype(jnp.float32),
        lax.psum(owned[8].astype(jnp.bfloat16), "context").astype(jnp.float32),
        lax.psum(owned[9].astype(jnp.bfloat16), "context").astype(jnp.float32),
        lax.psum(owned[10].astype(jnp.bfloat16), "context").astype(jnp.float32),
    )
    return (
        block_out,
        grad_input_part,
        owned[0],
        owned[1],
        owned[2],
        owned[3],
        owned[4],
        owned[5],
        owned[6],
        owned[7],
        owned[8],
        owned[9],
        owned[10],
    )


def fence(*values):
    return lax.optimization_barrier(values)


def after(value, *earlier):
    return lax.optimization_barrier((value,) + earlier)[0]


def swap(values, axis_name):
    return lax.ppermute(values, axis_name, [(0, 1), (1, 0)])


def pick(index, zero_item, one_item):
    return jnp.where(index == 0, zero_item, one_item)


def pair_join(index, own, other, axis):
    return jnp.concatenate([pick(index, own, other), pick(index, other, own)], axis=axis)


def half_of(values, index, axis):
    half = values.shape[axis] // 2
    return lax.dynamic_slice_in_dim(values, index * half, half, axis)


def ring_pairs(fsdp_size):
    columns = fsdp_size // 2
    flip = [(i, i ^ 1) for i in range(fsdp_size)]

    def turn(step):
        return [
            (z * 2 + y, ((z + step) % columns) * 2 + y) for z in range(columns) for y in range(2)
        ]

    return columns, flip, turn


def copy_call(copies_of, scalars, operands, shapes, copy_count, spaces):
    operand_count, result_count = len(operands), len(shapes)

    def kernel(scalar_ref, *refs):
        sources = refs[:operand_count]
        targets = refs[operand_count : operand_count + result_count]
        sems = refs[operand_count + result_count]
        copies = [
            pltpu.make_async_copy(source, target, sems.at[i])
            for i, (source, target) in enumerate(copies_of(scalar_ref, sources, targets))
        ]
        for copy in copies:
            copy.start()
        for copy in copies:
            copy.wait()

    moved = sum(2 * shape.size * shape.dtype.itemsize for shape in shapes)
    return pl.pallas_call(
        kernel,
        out_shape=shapes,
        in_specs=[pl.BlockSpec(memory_space=pltpu.SMEM)]
        + [pl.BlockSpec(memory_space=spaces[0])] * operand_count,
        out_specs=[pl.BlockSpec(memory_space=spaces[1])] * result_count,
        scratch_shapes=[pltpu.SemaphoreType.DMA((copy_count,))],
        compiler_params=pltpu.CompilerParams(vmem_limit_bytes=32 * 1024 * 1024),
        cost_estimate=pl.CostEstimate(flops=0, bytes_accessed=moved, transcendentals=0),
    )(jnp.stack(scalars).astype(jnp.int32), *operands)


def pack_call(x_index, kv_heads, head_size, w_query, w_key, w_value, gain_rows):
    rows, q_columns = w_query.shape
    group_width = q_columns // (2 * kv_heads)
    wide = group_width + 2 * head_size

    def kernel(x_ref, query_ref, key_ref, value_ref, gain_ref, out_ref):
        x = x_ref[0]
        for g in range(kv_heads):
            first = g * wide
            for ref, size in ((query_ref, group_width), (key_ref, head_size), (value_ref, head_size)):
                start = pl.multiple_of((x * kv_heads + g) * size, size)
                out_ref[:rows, first : first + size] = ref[:, pl.ds(start, size)]
                first += size
        out_ref[rows:, :] = gain_ref[...]

    return pl.pallas_call(
        kernel,
        out_shape=jax.ShapeDtypeStruct(
            (rows + gain_rows.shape[0], kv_heads * wide), w_query.dtype
        ),
        in_specs=[pl.BlockSpec(memory_space=pltpu.SMEM)]
        + [pl.BlockSpec(memory_space=pltpu.VMEM)] * 4,
        out_specs=pl.BlockSpec(memory_space=pltpu.VMEM),
    )(x_index.astype(jnp.int32)[None], w_query, w_key, w_value, gain_rows)


def turn_pieces(blob):
    columns, _, turn = ring_pairs(lax.axis_size("fsdp"))
    return [blob] + [lax.ppermute(blob, "fsdp", turn(step)) for step in range(1, columns)]


def flip_pieces(values):
    return lax.ppermute(values, "fsdp", ring_pairs(lax.axis_size("fsdp"))[1])


def stack_pieces(first, rest):
    pieces = [first] + list(rest)
    shape = (len(pieces),) + pieces[0].shape
    return copy_call(
        lambda at, own, out: [(piece, out[0].at[i]) for i, piece in enumerate(own)],
        [jnp.int32(0)],
        pieces,
        [jax.ShapeDtypeStruct(shape, pieces[0].dtype)],
        len(pieces),
        (pltpu.VMEM, pl.ANY),
    )[0]


def place_rows(near, far):
    fsdp_size = lax.axis_size("fsdp")
    columns = fsdp_size // 2
    place = lax.axis_index("fsdp")
    column, side = place // 2, place % 2
    sources = [(column - step + columns) % columns for step in range(columns)]
    near_at = [source * 2 + side for source in sources]
    far_at = [source * 2 + 1 - side for source in sources]
    operands = list(near) + list(far)

    def copies_of(at, own, out):
        copies, slot = [], 0
        for ref in own:
            if len(ref.shape) == 2:
                copies.append((ref, out[0].at[at[slot]]))
                slot += 1
                continue
            for i in range(ref.shape[0]):
                copies.append((ref.at[i], out[0].at[at[slot]]))
                slot += 1
        return copies

    return copy_call(
        copies_of,
        near_at + far_at,
        operands,
        [jax.ShapeDtypeStruct((fsdp_size,) + near[0].shape[-2:], near[0].dtype)],
        fsdp_size,
        (pltpu.VMEM, pl.ANY),
    )[0]


def split_rows(grads, extra=None):
    fsdp_size = lax.axis_size("fsdp")
    columns = fsdp_size // 2
    place = lax.axis_index("fsdp")
    column, side = place // 2, place % 2
    parts = [grads] if extra is None else [grads, extra]
    rows = [part.shape[1] for part in parts]
    firsts = [0, rows[0]]
    order = [(column + step) % columns for step in range(columns)]

    def copies_of(at, own, out):
        copies = []
        for part, first, count in zip(own, firsts, rows):
            span = pl.ds(first, count)
            for i in range(columns):
                copies.append((part.at[at[i]], out[0].at[i, span]))
                copies.append((part.at[at[columns + i]], out[1].at[i, span]))
        return copies

    shape = jax.ShapeDtypeStruct((columns, sum(rows), grads.shape[-1]), jnp.bfloat16)
    return copy_call(
        copies_of,
        [c * 2 + side for c in order] + [c * 2 + 1 - side for c in order],
        parts,
        [shape, shape],
        2 * columns * len(parts),
        (pl.ANY, pltpu.VMEM),
    )


def wide_sum(*values):
    total = values[0].astype(jnp.float32)
    for value in values[1:]:
        total = total + value.astype(jnp.float32)
    return total


def turn_sums(stay, got):
    columns, _, turn = ring_pairs(lax.axis_size("fsdp"))
    return [
        lax.ppermute(
            wide_sum(stay[step], got[step]).astype(jnp.bfloat16), "fsdp", turn(step)
        )
        for step in range(1, columns)
    ]


def head_prep(raw, gain, cosine, sine):
    recip = lax.rsqrt(jnp.mean(raw * raw, axis=-1, keepdims=True) + EPS)
    hat = raw * recip
    scaled = hat * gain
    half_size = raw.shape[-1] // 2
    return hat, recip, scaled * cosine + pltpu.roll(scaled, half_size, 1) * sine


def head_back(grad, gain, cosine, sine, hat, recip):
    half_size = grad.shape[-1] // 2
    unrot = grad * cosine - pltpu.roll(grad, half_size, 1) * sine
    gain_grad = jnp.sum(unrot * hat, axis=0, keepdims=True)
    scaled = unrot * gain
    return gain_grad, recip * (scaled - hat * jnp.mean(scaled * hat, axis=-1, keepdims=True))


def nt_dot(left, right):
    return lax.dot_general(
        left, right, (((1,), (1,)), ((), ())), preferred_element_type=jnp.float32
    )


LOG2_E = 1.4426950408889634


def key_mask(segment_col, segment_row, key_rows, query_rows, diagonal):
    same = segment_col[key_rows, :] == segment_row[:, query_rows]
    if not diagonal:
        return same
    size = (key_rows.stop - key_rows.start, query_rows.stop - query_rows.start)
    key_at = lax.broadcasted_iota(jnp.int32, size, 0)
    query_at = lax.broadcasted_iota(jnp.int32, size, 1)
    return same & (key_at <= query_at)


def attend_kernel(
    group_size,
    block,
    raw_ref,
    cosine_ref,
    sine_ref,
    qgain_ref,
    kgain_ref,
    segment_col,
    segment_row,
    out_ref,
    lse_ref,
    query_scr,
    key_scr,
    value_scr,
):
    tok_count, head_size = cosine_ref.shape
    factor = head_size ** (-0.5) * LOG2_E
    blocks = [slice(i, i + block) for i in range(0, tok_count, block)]
    key_col, value_col = group_size * head_size, (group_size + 1) * head_size
    for rows in blocks:
        cosine, sine = cosine_ref[rows, :], sine_ref[rows, :]
        for h in range(group_size):
            cols = slice(h * head_size, (h + 1) * head_size)
            query_scr[rows, cols] = head_prep(raw_ref[rows, cols], qgain_ref[...], cosine, sine)[
                2
            ].astype(jnp.bfloat16)
        key_scr[rows, :] = head_prep(
            raw_ref[rows, key_col:value_col], kgain_ref[...], cosine, sine
        )[2].astype(jnp.bfloat16)
        value_scr[:, rows] = raw_ref[rows, value_col:].T.astype(jnp.bfloat16)
    for h in range(group_size):
        cols = slice(h * head_size, (h + 1) * head_size)
        for i, query_rows in enumerate(blocks):
            query = query_scr[query_rows, cols]
            total = jnp.zeros((1, block), jnp.float32)
            mixed = jnp.zeros((head_size, block), jnp.float32)
            for j, key_rows in enumerate(blocks[: i + 1]):
                scores = nt_dot(key_scr[key_rows, :], query)
                mask = key_mask(segment_col, segment_row, key_rows, query_rows, i == j)
                terms = jnp.where(mask, jnp.exp2(scores * factor), 0.0)
                total = total + jnp.sum(terms, axis=0, keepdims=True)
                mixed = mixed + jnp.dot(
                    value_scr[:, key_rows],
                    terms.astype(jnp.bfloat16),
                    preferred_element_type=jnp.float32,
                )
            out_ref[query_rows, cols] = (mixed * (1.0 / total)).T.astype(jnp.bfloat16)
            lse_ref[0, h : h + 1, query_rows] = jnp.log2(total)


def attend_back_kernel(
    group_size,
    block,
    raw_ref,
    out_ref,
    grad_ref,
    lse_ref,
    cosine_ref,
    sine_ref,
    qgain_ref,
    kgain_ref,
    segment_col,
    segment_row,
    back_ref,
    gains_ref,
    hat_scr,
    recip_scr,
    query_scr,
    key_scr,
    key_turned,
    value_scr,
    grad_key,
    grad_value,
):
    tok_count, head_size = cosine_ref.shape
    scale = head_size ** (-0.5)
    factor = scale * LOG2_E
    blocks = [slice(i, i + block) for i in range(0, tok_count, block)]
    key_col, value_col = group_size * head_size, (group_size + 1) * head_size
    head_cols = [slice(h * head_size, (h + 1) * head_size) for h in range(group_size + 1)]
    for rows in blocks:
        cosine, sine = cosine_ref[rows, :], sine_ref[rows, :]
        for h, cols in enumerate(head_cols):
            gain = qgain_ref[...] if h < group_size else kgain_ref[...]
            hat, recip, turned = head_prep(raw_ref[rows, cols], gain, cosine, sine)
            hat_scr[rows, cols] = hat
            recip_scr[rows, cols] = jnp.broadcast_to(recip, hat.shape)
            if h < group_size:
                query_scr[rows, cols] = turned.astype(jnp.bfloat16)
            else:
                key_scr[rows, :] = turned.astype(jnp.bfloat16)
                key_turned[:, rows] = turned.T.astype(jnp.bfloat16)
        value_scr[rows, :] = raw_ref[rows, value_col:].astype(jnp.bfloat16)
    query_gain_grad = jnp.zeros((1, head_size), jnp.float32)
    for h, cols in enumerate(head_cols[:group_size]):
        for i, query_rows in enumerate(blocks):
            query = query_scr[query_rows, cols]
            grad = grad_ref[query_rows, cols]
            delta = jnp.sum(
                (grad.astype(jnp.float32) * out_ref[query_rows, cols].astype(jnp.float32)).T,
                axis=0,
                keepdims=True,
            )
            lse = lse_ref[0, h : h + 1, query_rows]
            grad_query = jnp.zeros((head_size, block), jnp.float32)
            for j, key_rows in enumerate(blocks[: i + 1]):
                scores = nt_dot(key_scr[key_rows, :], query)
                mask = key_mask(segment_col, segment_row, key_rows, query_rows, i == j)
                probs = jnp.where(mask, jnp.exp2(scores * factor - lse), 0.0)
                grad_probs = nt_dot(value_scr[key_rows, :], grad)
                grad_scores = (probs * (grad_probs - delta)).astype(jnp.bfloat16)
                value_part = jnp.dot(
                    probs.astype(jnp.bfloat16), grad, preferred_element_type=jnp.float32
                )
                key_part = jnp.dot(grad_scores, query, preferred_element_type=jnp.float32)
                grad_query = grad_query + jnp.dot(
                    key_turned[:, key_rows], grad_scores, preferred_element_type=jnp.float32
                )
                if h == 0 and i == j:
                    grad_value[key_rows, :] = value_part
                    grad_key[key_rows, :] = key_part
                else:
                    grad_value[key_rows, :] += value_part
                    grad_key[key_rows, :] += key_part
            gain_grad, back = head_back(
                grad_query.T * scale,
                qgain_ref[...],
                cosine_ref[query_rows, :],
                sine_ref[query_rows, :],
                hat_scr[query_rows, cols],
                recip_scr[query_rows, cols],
            )
            query_gain_grad = query_gain_grad + gain_grad
            back_ref[query_rows, cols] = back.astype(jnp.bfloat16)
    key_gain_grad = jnp.zeros((1, head_size), jnp.float32)
    for rows in blocks:
        gain_grad, back = head_back(
            grad_key[rows, :] * scale,
            kgain_ref[...],
            cosine_ref[rows, :],
            sine_ref[rows, :],
            hat_scr[rows, head_cols[-1]],
            recip_scr[rows, head_cols[-1]],
        )
        key_gain_grad = key_gain_grad + gain_grad
        back_ref[rows, key_col:value_col] = back.astype(jnp.bfloat16)
        back_ref[rows, value_col:] = grad_value[rows, :].astype(jnp.bfloat16)
    gains_ref[0, 0:1, :] = query_gain_grad
    gains_ref[0, 1:2, :] = key_gain_grad


def attention_calls(tok_count, head_size, group_size, kv_heads):
    block = min(256, tok_count)
    wide = (group_size + 2) * head_size
    whole = pl.BlockSpec((tok_count, head_size), lambda g: (0, 0))
    gain = pl.BlockSpec((1, head_size), lambda g: (0, 0))
    common = [
        whole,
        whole,
        gain,
        gain,
        pl.BlockSpec((tok_count, 1), lambda g: (0, 0)),
        pl.BlockSpec((1, tok_count), lambda g: (0, 0)),
    ]
    raw = pl.BlockSpec((tok_count, wide), lambda g: (0, g))
    heads = pl.BlockSpec((tok_count, group_size * head_size), lambda g: (0, g))
    lse = pl.BlockSpec((1, group_size, tok_count), lambda g: (g, 0, 0))
    pairs = kv_heads * group_size * tok_count * tok_count
    low, full = jnp.bfloat16, jnp.float32
    limit = pltpu.CompilerParams(vmem_limit_bytes=44 * 1024 * 1024)

    def forward(earlier, *operands):
        count = len(earlier)
        return pl.pallas_call(
            lambda *refs: attend_kernel(group_size, block, *refs[count:]),
            grid=(kv_heads,),
            in_specs=[pl.BlockSpec(memory_space=pl.ANY)] * count + [raw] + common,
            out_specs=[heads, lse],
            out_shape=[
                jax.ShapeDtypeStruct((tok_count, kv_heads * group_size * head_size), low),
                jax.ShapeDtypeStruct((kv_heads, group_size, tok_count), full),
            ],
            scratch_shapes=[
                pltpu.VMEM((tok_count, group_size * head_size), low),
                pltpu.VMEM((tok_count, head_size), low),
                pltpu.VMEM((head_size, tok_count), low),
            ],
            compiler_params=limit,
            cost_estimate=pl.CostEstimate(
                flops=pairs, bytes_accessed=0, transcendentals=0
            ),
        )(*earlier, *operands)

    def backward(earlier, *operands):
        count = len(earlier)
        return pl.pallas_call(
            lambda *refs: attend_back_kernel(group_size, block, *refs[count:]),
            grid=(kv_heads,),
            in_specs=[pl.BlockSpec(memory_space=pl.ANY)] * count + [raw, heads, heads, lse] + common,
            out_specs=[raw, pl.BlockSpec((1, 2, head_size), lambda g: (g, 0, 0))],
            out_shape=[
                jax.ShapeDtypeStruct((tok_count, kv_heads * wide), low),
                jax.ShapeDtypeStruct((kv_heads, 2, head_size), full),
            ],
            scratch_shapes=[
                pltpu.VMEM((tok_count, (group_size + 1) * head_size), full),
                pltpu.VMEM((tok_count, (group_size + 1) * head_size), full),
                pltpu.VMEM((tok_count, group_size * head_size), low),
                pltpu.VMEM((tok_count, head_size), low),
                pltpu.VMEM((head_size, tok_count), low),
                pltpu.VMEM((tok_count, head_size), low),
                pltpu.VMEM((tok_count, head_size), full),
                pltpu.VMEM((tok_count, head_size), full),
            ],
            compiler_params=limit,
            cost_estimate=pl.CostEstimate(
                flops=pairs, bytes_accessed=0, transcendentals=0
            ),
        )(*earlier, *operands)

    return forward, backward


def sum_cores(partial_of, c_index):
    got = swap(partial_of(1 - c_index).astype(jnp.bfloat16), "tensor")
    return (partial_of(c_index) + got.astype(jnp.float32)).astype(jnp.bfloat16)


def cross_sum(mine):
    return wide_sum(mine, swap(mine, "context")).astype(jnp.bfloat16)


def sum_part(mine, x_index):
    got = swap(half_of(mine, 1 - x_index, 0), "context")
    return wide_sum(half_of(mine, x_index, 0), got)


def dot_rows(left, right):
    return jnp.dot(left, right, preferred_element_type=jnp.float32)


def dot_back(left, right):
    return jnp.einsum("pf,df->pd", left, right, preferred_element_type=jnp.float32)


def dot_grad(left, right):
    return jnp.einsum("pd,pf->df", left, right, preferred_element_type=jnp.float32)


def quarter_shards(
    hidden_in,
    cotangent,
    segment,
    position,
    w_query,
    w_key,
    w_value,
    w_output,
    w_gate,
    w_up,
    w_down,
    attn_gain,
    ffn_gain,
    query_gain,
    key_gain,
):
    x_index, c_index = lax.axis_index("context"), lax.axis_index("tensor")
    fsdp_size = lax.axis_size("fsdp")
    rows_shard = w_query.shape[0]
    model = rows_shard * fsdp_size
    head_size = query_gain.shape[0] * fsdp_size
    q_width, kv_width = w_query.shape[1] // 2, w_key.shape[1] // 2
    ff_width = w_gate.shape[1] // 2
    q_heads, kv_heads = q_width // head_size, kv_width // head_size
    group_size = q_heads // kv_heads
    group_width = group_size * head_size

    def mine(weight, axis):
        return half_of(weight, x_index, axis)

    gains = jnp.concatenate([attn_gain, ffn_gain, query_gain, key_gain])
    gain_rows = jnp.pad(gains[None], ((0, 15), (0, q_width + 2 * kv_width - gains.shape[0])))
    blob_a = pack_call(x_index, kv_heads, head_size, w_query, w_key, w_value, gain_rows)
    blob_o = mine(w_output, 0).T
    blob_g, blob_u = mine(w_gate, 1), mine(w_up, 1)
    blob_d = mine(w_down, 0).T

    def own_part(rows):
        return half_of(half_of(rows, x_index, 0), c_index, 1)

    def wide_half(weight, h):
        return half_of(weight, h, 0)

    def grouped(grads):
        return grads.astype(jnp.bfloat16).reshape(fsdp_size, rows_shard, -1)

    def stacked(pieces):
        return stack_pieces(pieces[0], pieces[1:])

    turned_a = turn_pieces(blob_a)
    far_own_a = flip_pieces(blob_a)
    hidden_got = swap(hidden_in[0], "context")
    turned_a, far_own_a, hidden_got, blob_o, blob_g, blob_u, blob_d = fence(
        turned_a, far_own_a, hidden_got, blob_o, blob_g, blob_u, blob_d
    )

    near_a = stack_pieces(turned_a[1], turned_a[2:])
    far_a = flip_pieces(near_a)
    turned_o = turn_pieces(blob_o)
    marks = jnp.stack([segment[0], position[0]])
    marks = pair_join(x_index, marks, swap(marks, "context"), 1)
    hidden_column = pair_join(x_index, hidden_in[0], hidden_got, 0)
    hidden_other = swap(hidden_column, "tensor")
    hidden_rows = pair_join(c_index, hidden_column, hidden_other, 1)
    x_rows = hidden_rows.astype(jnp.float32)
    tok_count = x_rows.shape[0]
    recip_one = norm_stats(x_rows)
    segment_all, position_all = marks[0], marks[1]
    half_size = head_size // 2
    freq_table = THETA ** (-jnp.arange(half_size, dtype=jnp.float32) * 2.0 / head_size)
    angle_table = position_all.astype(jnp.float32)[:, None] * freq_table[None, :]
    cosine_half, sine_half = jnp.cos(angle_table), jnp.sin(angle_table)
    cosine_table = jnp.concatenate([cosine_half, cosine_half], axis=1)
    sine_table = jnp.concatenate([-sine_half, sine_half], axis=1)
    (
        far_a, turned_o, hidden_rows, recip_one, cosine_table, sine_table, blob_g, turned_a,
        far_own_a, cotangent,
    ) = fence(
        far_a, turned_o, hidden_rows, recip_one, cosine_table, sine_table, blob_g, turned_a,
        far_own_a, cotangent,
    )

    near_o = stacked(turned_o)
    far_o = flip_pieces(near_o)
    turned_g = turn_pieces(blob_g)
    dy_got = swap(cotangent[0], "context")
    all_a = place_rows(turned_a, [far_own_a, far_a])
    w_qkv = all_a[:, :rows_shard].reshape(model, -1)
    gain_all = all_a[:, rows_shard].astype(jnp.float32)
    gain_part = query_gain.shape[0]
    attn_gain32 = gain_all[:, :rows_shard].reshape(model)
    ffn_gain32 = gain_all[:, rows_shard : 2 * rows_shard].reshape(model)
    qgain32 = gain_all[:, 2 * rows_shard : 2 * rows_shard + gain_part].reshape(head_size)
    kgain32 = gain_all[:, 2 * rows_shard + gain_part : 2 * rows_shard + 2 * gain_part].reshape(
        head_size
    )
    x_rows = hidden_rows.astype(jnp.float32)
    attn_in = (x_rows * recip_one * attn_gain32).astype(jnp.bfloat16)
    qkv_raw = dot_rows(attn_in, w_qkv)
    qkv_raw, far_o, near_o, turned_g, dy_got, blob_u = fence(
        qkv_raw, far_o, near_o, turned_g, dy_got, blob_u
    )

    near_g = stacked(turned_g)
    far_g = flip_pieces(near_g)
    turned_u = turn_pieces(blob_u)
    attend, attend_back = attention_calls(tok_count, head_size, group_size, kv_heads)
    shared = (
        cosine_table,
        sine_table,
        qgain32[None],
        kgain32[None],
        segment_all[:, None],
        segment_all[None, :],
    )
    attn_low, log_total = attend((), qkv_raw, *shared)
    all_o = place_rows([near_o], [far_o]).reshape(model, -1)
    attn_low, all_o, far_g, near_g, turned_u, blob_d, dy_got, cotangent = fence(
        attn_low, all_o, far_g, near_g, turned_u, blob_d, dy_got, cotangent
    )

    near_u = stacked(turned_u)
    far_u = flip_pieces(near_u)
    turned_d = turn_pieces(blob_d)
    attn_mine = sum_cores(lambda h: dot_back(attn_low, wide_half(all_o, h)), c_index)
    attn_total = cross_sum(attn_mine)
    all_g = place_rows([near_g], [far_g]).reshape(model, -1)
    dy_column = pair_join(x_index, cotangent[0], dy_got, 0)
    rows_dy = pair_join(c_index, dy_column, swap(dy_column, "tensor"), 1)
    attn_total, all_g, far_u, near_u, turned_d, rows_dy = fence(
        attn_total, all_g, far_u, near_u, turned_d, rows_dy
    )

    attn_other = swap(attn_total, "tensor")
    near_d = stacked(turned_d)
    far_d = flip_pieces(near_d)
    all_u = place_rows([near_u], [far_u]).reshape(model, -1)
    mid_rows = x_rows + pair_join(c_index, attn_total, attn_other, 1).astype(jnp.float32)
    recip_two = norm_stats(mid_rows)
    normed_two = mid_rows * recip_two
    ffn_in = (normed_two * ffn_gain32).astype(jnp.bfloat16)
    gate_pre, up_pre = dot_rows(ffn_in, all_g), dot_rows(ffn_in, all_u)
    gate_sig = jax.nn.sigmoid(gate_pre)
    hidden_low = (gate_pre * gate_sig * up_pre).astype(jnp.bfloat16)
    stay_d, away_d = split_rows(grouped(dot_grad(rows_dy, hidden_low)))
    gate_pre, up_pre, far_d, near_d, ffn_in, all_g, all_u, stay_d, away_d, hidden_low = fence(
        gate_pre, up_pre, far_d, near_d, ffn_in, all_g, all_u, stay_d, away_d, hidden_low
    )

    got_d = flip_pieces(away_d)
    gate_sig = jax.nn.sigmoid(gate_pre)
    gate_act = gate_pre * gate_sig
    all_d = place_rows([near_d], [far_d]).reshape(model, -1)
    grad_hidden = dot_rows(rows_dy, all_d)
    grad_gate = (grad_hidden * up_pre * gate_sig * (1.0 + gate_pre * (1.0 - gate_sig))).astype(
        jnp.bfloat16
    )
    grad_up_pre = (grad_hidden * gate_act).astype(jnp.bfloat16)
    ffn_mine = sum_cores(
        lambda h: dot_back(grad_gate, wide_half(all_g, h))
        + dot_back(grad_up_pre, wide_half(all_u, h)),
        c_index,
    )
    sent_d = turn_sums(after(stay_d, ffn_mine), got_d)
    stay_g, away_g = split_rows(grouped(dot_grad(ffn_in, after(grad_gate, ffn_mine))))
    got_g = flip_pieces(after(away_g, got_d))
    stay_u, away_u = split_rows(grouped(dot_grad(ffn_in, after(grad_up_pre, ffn_mine))))
    ffn_total = cross_sum(ffn_mine)
    (
        ffn_total, stay_d, got_d, sent_d, stay_g, got_g, stay_u, away_u, hidden_low, rows_dy,
        mid_rows, all_d,
    ) = fence(
        ffn_total, stay_d, got_d, sent_d, stay_g, got_g, stay_u, away_u, hidden_low, rows_dy,
        mid_rows, all_d,
    )

    def finish(stay, got, sent):
        low = wide_sum(stay[0], got[0], *sent).astype(jnp.bfloat16)
        return low, swap(low, "context")

    ffn_other = swap(ffn_total, "tensor")
    sent_g = turn_sums(stay_g, got_g)
    got_u = flip_pieces(away_u)
    grad_ffn_in = pair_join(c_index, ffn_total, ffn_other, 1).astype(jnp.float32)
    normed_two = mid_rows * recip_two
    grad_ffn_gain = jnp.sum(grad_ffn_in * normed_two, axis=0)
    grad_mid = rows_dy.astype(jnp.float32) + norm_back(
        grad_ffn_in * ffn_gain32, normed_two, recip_two
    )
    grad_mid_low = grad_mid.astype(jnp.bfloat16)
    grad_attn = dot_rows(grad_mid_low, all_o).astype(jnp.bfloat16)
    stay_o, away_o = split_rows(grouped(dot_grad(grad_mid_low, attn_low)))
    grad_qkv, head_gains = attend_back((away_o,), qkv_raw, attn_low, grad_attn, log_total, *shared)
    got_o = flip_pieces(after(away_o, got_u))
    own_d, far_d = finish(stay_d, got_d, sent_d)
    (
        sent_g, got_u, grad_qkv, head_gains, got_o, stay_o, stay_u, stay_g, got_g, attn_in,
        hidden_low, mid_rows, all_d,
    ) = fence(
        sent_g, got_u, grad_qkv, head_gains, got_o, stay_o, stay_u, stay_g, got_g, attn_in,
        hidden_low, mid_rows, all_d,
    )

    sent_u = turn_sums(stay_u, got_u)
    normed_one = x_rows * recip_one
    gain_halves = {}

    def attn_part(h):
        part = dot_back(grad_qkv, wide_half(w_qkv, h))
        gain_halves[len(gain_halves)] = jnp.sum(part * half_of(normed_one, h, 1), axis=0)
        return part

    attn_in_mine = sum_cores(attn_part, c_index)
    grad_attn_gain = pair_join(c_index, gain_halves[1], gain_halves[0], 0)
    head_gains = jnp.sum(head_gains, axis=0)
    first_device = (x_index == 0) & (c_index == 0)
    gain_block = jnp.concatenate(
        [
            grad_attn_gain.reshape(fsdp_size, rows_shard),
            jnp.where(first_device, grad_ffn_gain, 0.0).reshape(fsdp_size, rows_shard),
            head_gains[0].reshape(fsdp_size, gain_part),
            head_gains[1].reshape(fsdp_size, gain_part),
        ],
        axis=1,
    ).astype(jnp.bfloat16)
    gain_block = gain_block.astype(jnp.float32) + swap(gain_block, "tensor").astype(jnp.float32)
    gain_block = jnp.pad(
        gain_block.astype(jnp.bfloat16)[:, None],
        ((0, 0), (0, 15), (0, grad_qkv.shape[1] - gain_block.shape[1])),
    )
    stay_a, away_a = split_rows(grouped(dot_grad(attn_in, grad_qkv)), gain_block)
    got_a = flip_pieces(away_a)
    sent_o = turn_sums(after(stay_o, *sent_u), got_o)
    own_g, far_g = finish(stay_g, got_g, sent_g)
    attn_in_part = sum_part(attn_in_mine, x_index).astype(jnp.bfloat16)
    (
        sent_u, got_a, sent_o, attn_in_part, stay_a, stay_o, got_o, stay_u, got_u, hidden_low,
        mid_rows, all_d,
    ) = fence(
        sent_u, got_a, sent_o, attn_in_part, stay_a, stay_o, got_o, stay_u, got_u, hidden_low,
        mid_rows, all_d,
    )

    sent_a = turn_sums(stay_a, got_a)
    out_mine = sum_cores(lambda h: dot_back(hidden_low, wide_half(all_d, h)), c_index)
    block_out = (own_part(mid_rows) + sum_part(out_mine, x_index)).astype(jnp.bfloat16)[None]
    own_u, far_u = finish(stay_u, got_u, sent_u)
    own_o, far_o = finish(stay_o, got_o, sent_o)
    grad_attn_in = pair_join(c_index, attn_in_part, swap(attn_in_part, "tensor"), 1).astype(
        jnp.float32
    )
    normed_part = half_of(x_rows * recip_one, x_index, 0)
    grad_input = half_of(grad_mid, x_index, 0) + norm_back(
        grad_attn_in * attn_gain32, normed_part, half_of(recip_one, x_index, 0)
    )
    grad_input_part = half_of(grad_input, c_index, 1)[None]
    own_a, far_a = finish(stay_a, got_a, sent_a)
    gain_sum = own_a[rows_shard].astype(jnp.float32) + far_a[rows_shard].astype(jnp.float32)

    def outcome(own, far):
        return pair_join(x_index, own, far, 1).astype(jnp.float32)

    def outcome_columns(own, far):
        return pair_join(x_index, own.T, far.T, 0).astype(jnp.float32)

    def picked(first, size):
        wide = group_width + 2 * head_size
        starts = [g * wide + first for g in range(kv_heads)]
        own = jnp.concatenate([own_a[:rows_shard, s : s + size] for s in starts], axis=1)
        far = jnp.concatenate([far_a[:rows_shard, s : s + size] for s in starts], axis=1)
        return pair_join(x_index, own, far, 1).astype(jnp.float32)

    return (
        block_out,
        grad_input_part,
        picked(0, group_width),
        picked(group_width, head_size),
        picked(group_width + head_size, head_size),
        outcome_columns(own_o, far_o),
        outcome(own_g, far_g),
        outcome(own_u, far_u),
        outcome_columns(own_d, far_d),
        gain_sum[:rows_shard],
        gain_sum[rows_shard : 2 * rows_shard],
        gain_sum[2 * rows_shard : 2 * rows_shard + gain_part],
        gain_sum[2 * rows_shard + gain_part : 2 * rows_shard + 2 * gain_part],
    )


def fits_quarters(mesh):
    sizes = mesh.shape
    return sizes["context"] == 2 and sizes["tensor"] == 2 and sizes["fsdp"] % 2 == 0


def solution(mesh):
    in_specs = (
        P("fsdp", "context", "tensor"),
        P("fsdp", "context", "tensor"),
        P("fsdp", "context"),
        P("fsdp", "context"),
        P("fsdp", "tensor"),
        P("fsdp", "tensor"),
        P("fsdp", "tensor"),
        P("tensor", "fsdp"),
        P("fsdp", "tensor"),
        P("fsdp", "tensor"),
        P("tensor", "fsdp"),
        P("fsdp"),
        P("fsdp"),
        P("fsdp"),
        P("fsdp"),
    )
    out_specs = (
        P("fsdp", "context", "tensor"),
        P("fsdp", "context", "tensor"),
        P("fsdp", "tensor"),
        P("fsdp", "tensor"),
        P("fsdp", "tensor"),
        P("tensor", "fsdp"),
        P("fsdp", "tensor"),
        P("fsdp", "tensor"),
        P("tensor", "fsdp"),
        P("fsdp"),
        P("fsdp"),
        P("fsdp"),
        P("fsdp"),
    )
    shards = quarter_shards if fits_quarters(mesh) else plain_shards
    return jax.shard_map(shards, mesh=mesh, in_specs=in_specs, out_specs=out_specs, check_vma=False)
```

```python
import jax
import jax.numpy as jnp
from jax import lax
from jax.experimental import pallas as pl
from jax.experimental.pallas import tpu as pltpu
from jax.sharding import PartitionSpec as P

EPS = 1e-06
THETA = 1000000.0


def norm_stats(values):
    return lax.rsqrt(jnp.mean(values * values, axis=-1, keepdims=True) + EPS)


def norm_back(grad_out, normed, recip_root):
    return recip_root * (grad_out - normed * jnp.mean(grad_out * normed, axis=-1, keepdims=True))


def rotary_tables(position_row, head_size):
    half_size = head_size // 2
    freq_table = THETA ** (-jnp.arange(half_size, dtype=jnp.float32) * 2.0 / head_size)
    angle_table = position_row.astype(jnp.float32)[:, None] * freq_table[None, :]
    return (jnp.cos(angle_table)[:, None, :], jnp.sin(angle_table)[:, None, :])


def rotate(values, cosine_table, sine_table, turn_sign):
    half_size = values.shape[-1] // 2
    first_half = values[..., :half_size]
    second_half = values[..., half_size:]
    turned = turn_sign * sine_table
    return jnp.concatenate(
        [
            first_half * cosine_table - second_half * turned,
            second_half * cosine_table + first_half * turned,
        ],
        axis=-1,
    )


def plain_shards(
    hidden_in,
    cotangent,
    segment,
    position,
    w_query,
    w_key,
    w_value,
    w_output,
    w_gate,
    w_up,
    w_down,
    attn_gain,
    ffn_gain,
    query_gain,
    key_gain,
):
    (
        wq_full,
        wk_full,
        wv_full,
        wo_full,
        wg_full,
        wu_full,
        wd_full,
        attn_full,
        ffn_full,
        qgain_full,
        kgain_full,
    ) = (
        lax.all_gather(w_query, "fsdp", axis=0, tiled=True),
        lax.all_gather(w_key, "fsdp", axis=0, tiled=True),
        lax.all_gather(w_value, "fsdp", axis=0, tiled=True),
        lax.all_gather(w_output, "fsdp", axis=1, tiled=True),
        lax.all_gather(w_gate, "fsdp", axis=0, tiled=True),
        lax.all_gather(w_up, "fsdp", axis=0, tiled=True),
        lax.all_gather(w_down, "fsdp", axis=1, tiled=True),
        lax.all_gather(attn_gain, "fsdp", axis=0, tiled=True),
        lax.all_gather(ffn_gain, "fsdp", axis=0, tiled=True),
        lax.all_gather(query_gain, "fsdp", axis=0, tiled=True),
        lax.all_gather(key_gain, "fsdp", axis=0, tiled=True),
    )
    rows_x, rows_dy = (
        lax.all_gather(hidden_in[0], "tensor", axis=1, tiled=True),
        lax.all_gather(cotangent[0], "tensor", axis=1, tiled=True),
    )
    tok_count = rows_x.shape[0]
    feat_part = hidden_in.shape[2]
    head_size = qgain_full.shape[0]
    q_heads = wq_full.shape[1] // head_size
    kv_heads = wk_full.shape[1] // head_size
    group_size = q_heads // kv_heads
    score_scale = head_size ** (-0.5)
    x_rows = rows_x.astype(jnp.float32)
    recip_one = norm_stats(x_rows)
    normed_one = x_rows * recip_one
    attn_gain32 = attn_full.astype(jnp.float32)
    attn_in = (normed_one * attn_gain32).astype(jnp.bfloat16)
    query_raw = jnp.dot(attn_in, wq_full, preferred_element_type=jnp.float32).reshape(
        tok_count, q_heads, head_size
    )
    key_raw = jnp.dot(attn_in, wk_full, preferred_element_type=jnp.float32).reshape(
        tok_count, kv_heads, head_size
    )
    value_raw = jnp.dot(attn_in, wv_full, preferred_element_type=jnp.float32)
    cosine_table, sine_table = rotary_tables(position[0], head_size)
    recip_query = norm_stats(query_raw)
    query_hat = query_raw * recip_query
    qgain32 = qgain_full.astype(jnp.float32)
    query_rot = rotate(query_hat * qgain32, cosine_table, sine_table, 1.0).astype(jnp.bfloat16)
    recip_key = norm_stats(key_raw)
    key_hat = key_raw * recip_key
    kgain32 = kgain_full.astype(jnp.float32)
    key_rot = rotate(key_hat * kgain32, cosine_table, sine_table, 1.0).astype(jnp.bfloat16)
    value_low = value_raw.astype(jnp.bfloat16).reshape(tok_count, kv_heads, head_size)
    key_all, value_all, segment_all = (
        lax.all_gather(key_rot, "context", axis=0, tiled=True),
        lax.all_gather(value_low, "context", axis=0, tiled=True),
        lax.all_gather(segment[0], "context", axis=0, tiled=True),
    )
    query_index = lax.axis_index("context") * tok_count + jnp.arange(tok_count, dtype=jnp.int32)
    key_index = jnp.arange(key_all.shape[0], dtype=jnp.int32)
    allowed = (segment[0][:, None] == segment_all[None, :]) & (
        key_index[None, :] <= query_index[:, None]
    )
    query_group = query_rot.reshape(tok_count, kv_heads, group_size, head_size)

    def scores_of():
        raw_scores = (
            jnp.einsum("pkgd,lkd->kgpl", query_group, key_all, preferred_element_type=jnp.float32)
            * score_scale
        )
        return jnp.where(allowed, raw_scores, -1e30)

    masked = scores_of()
    row_max = jnp.max(masked, axis=-1, keepdims=True)
    exp_terms = jnp.exp(masked - row_max)
    row_total = jnp.sum(exp_terms, axis=-1, keepdims=True)
    log_total = row_max + jnp.log(row_total)
    probs_fwd = (exp_terms / row_total).astype(jnp.bfloat16)
    attn_rows = jnp.einsum(
        "kgpl,lkd->pkgd", probs_fwd, value_all, preferred_element_type=jnp.float32
    )
    attn_low = attn_rows.reshape(tok_count, q_heads * head_size).astype(jnp.bfloat16)
    attn_sum = lax.psum(
        jnp.dot(attn_low, wo_full, preferred_element_type=jnp.float32).astype(jnp.bfloat16),
        "tensor",
    ).astype(jnp.float32)
    mid_rows = x_rows + attn_sum
    recip_two = norm_stats(mid_rows)
    normed_two = mid_rows * recip_two
    ffn_gain32 = ffn_full.astype(jnp.float32)
    ffn_in = (normed_two * ffn_gain32).astype(jnp.bfloat16)
    gate_pre = jnp.dot(ffn_in, wg_full, preferred_element_type=jnp.float32)
    up_pre = jnp.dot(ffn_in, wu_full, preferred_element_type=jnp.float32)
    gate_sig = jax.nn.sigmoid(gate_pre)
    gate_act = gate_pre * gate_sig
    hidden_low = (gate_act * up_pre).astype(jnp.bfloat16)
    ffn_rows = lax.psum_scatter(
        jnp.dot(hidden_low, wd_full, preferred_element_type=jnp.float32).astype(jnp.bfloat16),
        "tensor",
        scatter_dimension=1,
        tiled=True,
    ).astype(jnp.float32)
    feat_first = lax.axis_index("tensor") * feat_part
    mid_part = lax.dynamic_slice_in_dim(mid_rows, feat_first, feat_part, 1)
    block_out = (mid_part + ffn_rows).astype(jnp.bfloat16)[None]
    (
        wq_full,
        wk_full,
        wv_full,
        wo_full,
        wg_full,
        wu_full,
        wd_full,
        attn_full,
        ffn_full,
        qgain_full,
        kgain_full,
    ) = (
        lax.all_gather(w_query, "fsdp", axis=0, tiled=True),
        lax.all_gather(w_key, "fsdp", axis=0, tiled=True),
        lax.all_gather(w_value, "fsdp", axis=0, tiled=True),
        lax.all_gather(w_output, "fsdp", axis=1, tiled=True),
        lax.all_gather(w_gate, "fsdp", axis=0, tiled=True),
        lax.all_gather(w_up, "fsdp", axis=0, tiled=True),
        lax.all_gather(w_down, "fsdp", axis=1, tiled=True),
        lax.all_gather(attn_gain, "fsdp", axis=0, tiled=True),
        lax.all_gather(ffn_gain, "fsdp", axis=0, tiled=True),
        lax.all_gather(query_gain, "fsdp", axis=0, tiled=True),
        lax.all_gather(key_gain, "fsdp", axis=0, tiled=True),
    )
    grad_w_down = jnp.einsum("pf,pd->fd", hidden_low, rows_dy, preferred_element_type=jnp.float32)
    grad_hidden = jnp.einsum("pd,fd->pf", rows_dy, wd_full, preferred_element_type=jnp.float32)
    grad_gate = (grad_hidden * up_pre * gate_sig * (1.0 + gate_pre * (1.0 - gate_sig))).astype(
        jnp.bfloat16
    )
    grad_up_pre = (grad_hidden * gate_act).astype(jnp.bfloat16)
    grad_w_gate = jnp.einsum("pd,pf->df", ffn_in, grad_gate, preferred_element_type=jnp.float32)
    grad_w_up = jnp.einsum("pd,pf->df", ffn_in, grad_up_pre, preferred_element_type=jnp.float32)
    ffn_in_part = jnp.einsum(
        "pf,df->pd", grad_gate, wg_full, preferred_element_type=jnp.float32
    ) + jnp.einsum("pf,df->pd", grad_up_pre, wu_full, preferred_element_type=jnp.float32)
    grad_ffn_in = lax.psum(ffn_in_part.astype(jnp.bfloat16), "tensor").astype(jnp.float32)
    grad_ffn_gain = jnp.sum(grad_ffn_in * normed_two, axis=0)
    grad_mid = rows_dy.astype(jnp.float32) + norm_back(
        grad_ffn_in * ffn_gain32, normed_two, recip_two
    )
    grad_mid_low = grad_mid.astype(jnp.bfloat16)
    grad_w_output = jnp.einsum(
        "pf,pd->fd", attn_low, grad_mid_low, preferred_element_type=jnp.float32
    )
    grad_attn = jnp.einsum("pd,fd->pf", grad_mid_low, wo_full, preferred_element_type=jnp.float32)
    grad_attn = grad_attn.astype(jnp.bfloat16).reshape(tok_count, kv_heads, group_size, head_size)
    soft_probs = jnp.exp(scores_of() - log_total)
    grad_probs = jnp.einsum(
        "pkgd,lkd->kgpl", grad_attn, value_all, preferred_element_type=jnp.float32
    )
    row_delta = jnp.sum(soft_probs * grad_probs, axis=-1, keepdims=True)
    grad_scores = (soft_probs * (grad_probs - row_delta)).astype(jnp.bfloat16)
    probs_low = soft_probs.astype(jnp.bfloat16)
    grad_query = (
        jnp.einsum("kgpl,lkd->pkgd", grad_scores, key_all, preferred_element_type=jnp.float32)
        * score_scale
    )
    grad_query = grad_query.reshape(tok_count, q_heads, head_size)
    grad_key_rows = (
        jnp.einsum("kgpl,pkgd->lkd", grad_scores, query_group, preferred_element_type=jnp.float32)
        * score_scale
    )
    grad_value_rows = jnp.einsum(
        "kgpl,pkgd->lkd", probs_low, grad_attn, preferred_element_type=jnp.float32
    )
    key_value_grads = lax.psum_scatter(
        jnp.concatenate(
            [
                grad_key_rows.reshape(tok_count * lax.axis_size("context"), -1),
                grad_value_rows.reshape(tok_count * lax.axis_size("context"), -1),
            ],
            axis=1,
        ).astype(jnp.bfloat16),
        "context",
        scatter_dimension=0,
        tiled=True,
    ).astype(jnp.float32)
    kv_width = kv_heads * head_size
    grad_key = key_value_grads[:, :kv_width].reshape(tok_count, kv_heads, head_size)
    grad_value_low = key_value_grads[:, kv_width:].astype(jnp.bfloat16)
    unrot_query = rotate(grad_query, cosine_table, sine_table, -1.0)
    grad_query_gain = jnp.sum(unrot_query * query_hat, axis=(0, 1))
    grad_query_raw = (
        norm_back(unrot_query * qgain32, query_hat, recip_query)
        .astype(jnp.bfloat16)
        .reshape(tok_count, q_heads * head_size)
    )
    unrot_key = rotate(grad_key, cosine_table, sine_table, -1.0)
    grad_key_gain = jnp.sum(unrot_key * key_hat, axis=(0, 1))
    grad_key_raw = (
        norm_back(unrot_key * kgain32, key_hat, recip_key)
        .astype(jnp.bfloat16)
        .reshape(tok_count, kv_width)
    )
    grad_w_query = jnp.einsum(
        "pd,pf->df", attn_in, grad_query_raw, preferred_element_type=jnp.float32
    )
    grad_w_key = jnp.einsum("pd,pf->df", attn_in, grad_key_raw, preferred_element_type=jnp.float32)
    grad_w_value = jnp.einsum(
        "pd,pf->df", attn_in, grad_value_low, preferred_element_type=jnp.float32
    )
    attn_in_part = (
        jnp.einsum("pf,df->pd", grad_query_raw, wq_full, preferred_element_type=jnp.float32)
        + jnp.einsum("pf,df->pd", grad_key_raw, wk_full, preferred_element_type=jnp.float32)
        + jnp.einsum("pf,df->pd", grad_value_low, wv_full, preferred_element_type=jnp.float32)
    )
    grad_attn_in, grad_query_gain, grad_key_gain = (
        lax.psum(attn_in_part.astype(jnp.bfloat16), "tensor").astype(jnp.float32),
        lax.psum(grad_query_gain.astype(jnp.bfloat16), "tensor").astype(jnp.float32),
        lax.psum(grad_key_gain.astype(jnp.bfloat16), "tensor").astype(jnp.float32),
    )
    grad_attn_gain = jnp.sum(grad_attn_in * normed_one, axis=0)
    grad_input = grad_mid + norm_back(
        grad_attn_in * attn_full.astype(jnp.float32), normed_one, recip_one
    )
    grad_input_part = lax.dynamic_slice_in_dim(grad_input, feat_first, feat_part, 1)[None]
    owned = (
        lax.psum_scatter(
            grad_w_query.astype(jnp.bfloat16), "fsdp", scatter_dimension=0, tiled=True
        ).astype(jnp.float32),
        lax.psum_scatter(
            grad_w_key.astype(jnp.bfloat16), "fsdp", scatter_dimension=0, tiled=True
        ).astype(jnp.float32),
        lax.psum_scatter(
            grad_w_value.astype(jnp.bfloat16), "fsdp", scatter_dimension=0, tiled=True
        ).astype(jnp.float32),
        lax.psum_scatter(
            grad_w_output.astype(jnp.bfloat16), "fsdp", scatter_dimension=1, tiled=True
        ).astype(jnp.float32),
        lax.psum_scatter(
            grad_w_gate.astype(jnp.bfloat16), "fsdp", scatter_dimension=0, tiled=True
        ).astype(jnp.float32),
        lax.psum_scatter(
            grad_w_up.astype(jnp.bfloat16), "fsdp", scatter_dimension=0, tiled=True
        ).astype(jnp.float32),
        lax.psum_scatter(
            grad_w_down.astype(jnp.bfloat16), "fsdp", scatter_dimension=1, tiled=True
        ).astype(jnp.float32),
        lax.psum_scatter(
            grad_attn_gain.astype(jnp.bfloat16), "fsdp", scatter_dimension=0, tiled=True
        ).astype(jnp.float32),
        lax.psum_scatter(
            grad_ffn_gain.astype(jnp.bfloat16), "fsdp", scatter_dimension=0, tiled=True
        ).astype(jnp.float32),
        lax.psum_scatter(
            grad_query_gain.astype(jnp.bfloat16), "fsdp", scatter_dimension=0, tiled=True
        ).astype(jnp.float32),
        lax.psum_scatter(
            grad_key_gain.astype(jnp.bfloat16), "fsdp", scatter_dimension=0, tiled=True
        ).astype(jnp.float32),
    )
    owned = (
        lax.psum(owned[0].astype(jnp.bfloat16), "context").astype(jnp.float32),
        lax.psum(owned[1].astype(jnp.bfloat16), "context").astype(jnp.float32),
        lax.psum(owned[2].astype(jnp.bfloat16), "context").astype(jnp.float32),
        lax.psum(owned[3].astype(jnp.bfloat16), "context").astype(jnp.float32),
        lax.psum(owned[4].astype(jnp.bfloat16), "context").astype(jnp.float32),
        lax.psum(owned[5].astype(jnp.bfloat16), "context").astype(jnp.float32),
        lax.psum(owned[6].astype(jnp.bfloat16), "context").astype(jnp.float32),
        lax.psum(owned[7].astype(jnp.bfloat16), "context").astype(jnp.float32),
        lax.psum(owned[8].astype(jnp.bfloat16), "context").astype(jnp.float32),
        lax.psum(owned[9].astype(jnp.bfloat16), "context").astype(jnp.float32),
        lax.psum(owned[10].astype(jnp.bfloat16), "context").astype(jnp.float32),
    )
    return (
        block_out,
        grad_input_part,
        owned[0],
        owned[1],
        owned[2],
        owned[3],
        owned[4],
        owned[5],
        owned[6],
        owned[7],
        owned[8],
        owned[9],
        owned[10],
    )


def fence(*values):
    return lax.optimization_barrier(values)


def after(value, *earlier):
    return lax.optimization_barrier((value,) + earlier)[0]


def swap(values, axis_name):
    return lax.ppermute(values, axis_name, [(0, 1), (1, 0)])


def pick(index, zero_item, one_item):
    return jnp.where(index == 0, zero_item, one_item)


def pair_join(index, own, other, axis):
    return jnp.concatenate([pick(index, own, other), pick(index, other, own)], axis=axis)


def half_of(values, index, axis):
    half = values.shape[axis] // 2
    return lax.dynamic_slice_in_dim(values, index * half, half, axis)


def ring_pairs(fsdp_size):
    columns = fsdp_size // 2
    flip = [(i, i ^ 1) for i in range(fsdp_size)]

    def turn(step):
        return [
            (z * 2 + y, ((z + step) % columns) * 2 + y) for z in range(columns) for y in range(2)
        ]

    return columns, flip, turn


def copy_call(copies_of, scalars, operands, shapes, copy_count, spaces):
    operand_count, result_count = len(operands), len(shapes)

    def kernel(scalar_ref, *refs):
        sources = refs[:operand_count]
        targets = refs[operand_count : operand_count + result_count]
        sems = refs[operand_count + result_count]
        copies = [
            pltpu.make_async_copy(source, target, sems.at[i])
            for i, (source, target) in enumerate(copies_of(scalar_ref, sources, targets))
        ]
        for copy in copies:
            copy.start()
        for copy in copies:
            copy.wait()

    moved = sum(2 * shape.size * shape.dtype.itemsize for shape in shapes)
    return pl.pallas_call(
        kernel,
        out_shape=shapes,
        in_specs=[pl.BlockSpec(memory_space=pltpu.SMEM)]
        + [pl.BlockSpec(memory_space=spaces[0])] * operand_count,
        out_specs=[pl.BlockSpec(memory_space=spaces[1])] * result_count,
        scratch_shapes=[pltpu.SemaphoreType.DMA((copy_count,))],
        compiler_params=pltpu.CompilerParams(vmem_limit_bytes=32 * 1024 * 1024),
        cost_estimate=pl.CostEstimate(flops=0, bytes_accessed=moved, transcendentals=0),
    )(jnp.stack(scalars).astype(jnp.int32), *operands)


def pack_call(x_index, kv_heads, head_size, w_query, w_key, w_value, gain_rows):
    rows, q_columns = w_query.shape
    group_width = q_columns // (2 * kv_heads)
    wide = group_width + 2 * head_size

    def kernel(x_ref, query_ref, key_ref, value_ref, gain_ref, out_ref):
        x = x_ref[0]
        for g in range(kv_heads):
            first = g * wide
            for ref, size in ((query_ref, group_width), (key_ref, head_size), (value_ref, head_size)):
                start = pl.multiple_of((x * kv_heads + g) * size, size)
                out_ref[:rows, first : first + size] = ref[:, pl.ds(start, size)]
                first += size
        out_ref[rows:, :] = gain_ref[...]

    return pl.pallas_call(
        kernel,
        out_shape=jax.ShapeDtypeStruct(
            (rows + gain_rows.shape[0], kv_heads * wide), w_query.dtype
        ),
        in_specs=[pl.BlockSpec(memory_space=pltpu.SMEM)]
        + [pl.BlockSpec(memory_space=pltpu.VMEM)] * 4,
        out_specs=pl.BlockSpec(memory_space=pltpu.VMEM),
    )(x_index.astype(jnp.int32)[None], w_query, w_key, w_value, gain_rows)


def turn_pieces(blob):
    columns, _, turn = ring_pairs(lax.axis_size("fsdp"))
    return [blob] + [lax.ppermute(blob, "fsdp", turn(step)) for step in range(1, columns)]


def flip_pieces(values):
    return lax.ppermute(values, "fsdp", ring_pairs(lax.axis_size("fsdp"))[1])


def stack_pieces(first, rest):
    pieces = [first] + list(rest)
    shape = (len(pieces),) + pieces[0].shape
    return copy_call(
        lambda at, own, out: [(piece, out[0].at[i]) for i, piece in enumerate(own)],
        [jnp.int32(0)],
        pieces,
        [jax.ShapeDtypeStruct(shape, pieces[0].dtype)],
        len(pieces),
        (pltpu.VMEM, pl.ANY),
    )[0]


def place_rows(near, far):
    fsdp_size = lax.axis_size("fsdp")
    columns = fsdp_size // 2
    place = lax.axis_index("fsdp")
    column, side = place // 2, place % 2
    sources = [(column - step + columns) % columns for step in range(columns)]
    near_at = [source * 2 + side for source in sources]
    far_at = [source * 2 + 1 - side for source in sources]
    operands = list(near) + list(far)

    def copies_of(at, own, out):
        copies, slot = [], 0
        for ref in own:
            if len(ref.shape) == 2:
                copies.append((ref, out[0].at[at[slot]]))
                slot += 1
                continue
            for i in range(ref.shape[0]):
                copies.append((ref.at[i], out[0].at[at[slot]]))
                slot += 1
        return copies

    return copy_call(
        copies_of,
        near_at + far_at,
        operands,
        [jax.ShapeDtypeStruct((fsdp_size,) + near[0].shape[-2:], near[0].dtype)],
        fsdp_size,
        (pltpu.VMEM, pl.ANY),
    )[0]


def split_rows(grads, extra=None, apart=False):
    fsdp_size = lax.axis_size("fsdp")
    columns = fsdp_size // 2
    place = lax.axis_index("fsdp")
    column, side = place // 2, place % 2
    parts = [grads] if extra is None else [grads, extra]
    rows = [part.shape[1] for part in parts]
    firsts = [0, rows[0]]
    order = [(column + step) % columns for step in range(columns)]

    def copies_of(at, own, out):
        copies = []
        for part, first, count in zip(own, firsts, rows):
            span = pl.ds(first, count)
            for i in range(columns):
                copies.append((part.at[at[i]], out[0].at[i, span]))
                if apart:
                    target = out[2].at[span] if i == 0 else out[1].at[i - 1, span]
                else:
                    target = out[1].at[i, span]
                copies.append((part.at[at[columns + i]], target))
        return copies

    def shape(*lead):
        return jax.ShapeDtypeStruct(lead + (sum(rows), grads.shape[-1]), jnp.bfloat16)

    away_shapes = [shape(columns - 1), shape()] if apart else [shape(columns)]
    return copy_call(
        copies_of,
        [c * 2 + side for c in order] + [c * 2 + 1 - side for c in order],
        parts,
        [shape(columns)] + away_shapes,
        2 * columns * len(parts),
        (pl.ANY, pltpu.VMEM),
    )


def wide_sum(*values):
    total = values[0].astype(jnp.float32)
    for value in values[1:]:
        total = total + value.astype(jnp.float32)
    return total


def turn_sums(stay, got):
    lacking = stay.shape[0] - got.shape[0]
    columns, _, turn = ring_pairs(lax.axis_size("fsdp"))
    return [
        lax.ppermute(
            wide_sum(stay[step], got[step - lacking]).astype(jnp.bfloat16), "fsdp", turn(step)
        )
        for step in range(1, columns)
    ]


def head_prep(raw, gain, cosine, sine):
    recip = lax.rsqrt(jnp.mean(raw * raw, axis=-1, keepdims=True) + EPS)
    hat = raw * recip
    scaled = hat * gain
    half_size = raw.shape[-1] // 2
    return hat, recip, scaled * cosine + pltpu.roll(scaled, half_size, 1) * sine


def head_back(grad, gain, cosine, sine, hat, recip):
    half_size = grad.shape[-1] // 2
    unrot = grad * cosine - pltpu.roll(grad, half_size, 1) * sine
    gain_grad = jnp.sum(unrot * hat, axis=0, keepdims=True)
    scaled = unrot * gain
    return gain_grad, recip * (scaled - hat * jnp.mean(scaled * hat, axis=-1, keepdims=True))


def nt_dot(left, right):
    return lax.dot_general(
        left, right, (((1,), (1,)), ((), ())), preferred_element_type=jnp.float32
    )


LOG2_E = 1.4426950408889634


def key_mask(segment_col, segment_row, key_rows, query_rows, diagonal):
    same = segment_col[key_rows, :] == segment_row[:, query_rows]
    if not diagonal:
        return same
    size = (key_rows.stop - key_rows.start, query_rows.stop - query_rows.start)
    key_at = lax.broadcasted_iota(jnp.int32, size, 0)
    query_at = lax.broadcasted_iota(jnp.int32, size, 1)
    return same & (key_at <= query_at)


def attend_kernel(
    group_size,
    block,
    raw_ref,
    cosine_ref,
    sine_ref,
    qgain_ref,
    kgain_ref,
    segment_col,
    segment_row,
    out_ref,
    lse_ref,
    query_scr,
    key_scr,
    value_scr,
):
    tok_count, head_size = cosine_ref.shape
    factor = head_size ** (-0.5) * LOG2_E
    blocks = [slice(i, i + block) for i in range(0, tok_count, block)]
    key_col, value_col = group_size * head_size, (group_size + 1) * head_size
    for rows in blocks:
        cosine, sine = cosine_ref[rows, :], sine_ref[rows, :]
        for h in range(group_size):
            cols = slice(h * head_size, (h + 1) * head_size)
            query_scr[rows, cols] = head_prep(raw_ref[rows, cols], qgain_ref[...], cosine, sine)[
                2
            ].astype(jnp.bfloat16)
        key_scr[rows, :] = head_prep(
            raw_ref[rows, key_col:value_col], kgain_ref[...], cosine, sine
        )[2].astype(jnp.bfloat16)
        value_scr[:, rows] = raw_ref[rows, value_col:].T.astype(jnp.bfloat16)
    for h in range(group_size):
        cols = slice(h * head_size, (h + 1) * head_size)
        for i, query_rows in enumerate(blocks):
            query = query_scr[query_rows, cols]
            total = jnp.zeros((1, block), jnp.float32)
            mixed = jnp.zeros((head_size, block), jnp.float32)
            for j, key_rows in enumerate(blocks[: i + 1]):
                scores = nt_dot(key_scr[key_rows, :], query)
                mask = key_mask(segment_col, segment_row, key_rows, query_rows, i == j)
                terms = jnp.where(mask, jnp.exp2(scores * factor), 0.0)
                total = total + jnp.sum(terms, axis=0, keepdims=True)
                mixed = mixed + jnp.dot(
                    value_scr[:, key_rows],
                    terms.astype(jnp.bfloat16),
                    preferred_element_type=jnp.float32,
                )
            out_ref[query_rows, cols] = (mixed * (1.0 / total)).T.astype(jnp.bfloat16)
            lse_ref[0, h : h + 1, query_rows] = jnp.log2(total)


def attend_back_kernel(
    group_size,
    block,
    raw_ref,
    out_ref,
    grad_ref,
    lse_ref,
    cosine_ref,
    sine_ref,
    qgain_ref,
    kgain_ref,
    segment_col,
    segment_row,
    back_ref,
    gains_ref,
    hat_scr,
    recip_scr,
    query_scr,
    key_scr,
    key_turned,
    value_scr,
    grad_key,
    grad_value,
):
    tok_count, head_size = cosine_ref.shape
    scale = head_size ** (-0.5)
    factor = scale * LOG2_E
    blocks = [slice(i, i + block) for i in range(0, tok_count, block)]
    key_col, value_col = group_size * head_size, (group_size + 1) * head_size
    head_cols = [slice(h * head_size, (h + 1) * head_size) for h in range(group_size + 1)]
    for rows in blocks:
        cosine, sine = cosine_ref[rows, :], sine_ref[rows, :]
        for h, cols in enumerate(head_cols):
            gain = qgain_ref[...] if h < group_size else kgain_ref[...]
            hat, recip, turned = head_prep(raw_ref[rows, cols], gain, cosine, sine)
            hat_scr[rows, cols] = hat
            recip_scr[rows, cols] = jnp.broadcast_to(recip, hat.shape)
            if h < group_size:
                query_scr[rows, cols] = turned.astype(jnp.bfloat16)
            else:
                key_scr[rows, :] = turned.astype(jnp.bfloat16)
                key_turned[:, rows] = turned.T.astype(jnp.bfloat16)
        value_scr[rows, :] = raw_ref[rows, value_col:].astype(jnp.bfloat16)
    query_gain_grad = jnp.zeros((1, head_size), jnp.float32)
    for h, cols in enumerate(head_cols[:group_size]):
        for i, query_rows in enumerate(blocks):
            query = query_scr[query_rows, cols]
            grad = grad_ref[query_rows, cols]
            delta = jnp.sum(
                (grad.astype(jnp.float32) * out_ref[query_rows, cols].astype(jnp.float32)).T,
                axis=0,
                keepdims=True,
            )
            lse = lse_ref[0, h : h + 1, query_rows]
            grad_query = jnp.zeros((head_size, block), jnp.float32)
            for j, key_rows in enumerate(blocks[: i + 1]):
                scores = nt_dot(key_scr[key_rows, :], query)
                mask = key_mask(segment_col, segment_row, key_rows, query_rows, i == j)
                probs = jnp.where(mask, jnp.exp2(scores * factor - lse), 0.0)
                grad_probs = nt_dot(value_scr[key_rows, :], grad)
                grad_scores = (probs * (grad_probs - delta)).astype(jnp.bfloat16)
                value_part = jnp.dot(
                    probs.astype(jnp.bfloat16), grad, preferred_element_type=jnp.float32
                )
                key_part = jnp.dot(grad_scores, query, preferred_element_type=jnp.float32)
                grad_query = grad_query + jnp.dot(
                    key_turned[:, key_rows], grad_scores, preferred_element_type=jnp.float32
                )
                if h == 0 and i == j:
                    grad_value[key_rows, :] = value_part
                    grad_key[key_rows, :] = key_part
                else:
                    grad_value[key_rows, :] += value_part
                    grad_key[key_rows, :] += key_part
            gain_grad, back = head_back(
                grad_query.T * scale,
                qgain_ref[...],
                cosine_ref[query_rows, :],
                sine_ref[query_rows, :],
                hat_scr[query_rows, cols],
                recip_scr[query_rows, cols],
            )
            query_gain_grad = query_gain_grad + gain_grad
            back_ref[query_rows, cols] = back.astype(jnp.bfloat16)
    key_gain_grad = jnp.zeros((1, head_size), jnp.float32)
    for rows in blocks:
        gain_grad, back = head_back(
            grad_key[rows, :] * scale,
            kgain_ref[...],
            cosine_ref[rows, :],
            sine_ref[rows, :],
            hat_scr[rows, head_cols[-1]],
            recip_scr[rows, head_cols[-1]],
        )
        key_gain_grad = key_gain_grad + gain_grad
        back_ref[rows, key_col:value_col] = back.astype(jnp.bfloat16)
        back_ref[rows, value_col:] = grad_value[rows, :].astype(jnp.bfloat16)
    gains_ref[0, 0:1, :] = query_gain_grad
    gains_ref[0, 1:2, :] = key_gain_grad


def attention_calls(tok_count, head_size, group_size, first, kv_heads):
    block = min(256, tok_count)
    wide = (group_size + 2) * head_size
    whole = pl.BlockSpec((tok_count, head_size), lambda g: (0, 0))
    gain = pl.BlockSpec((1, head_size), lambda g: (0, 0))
    common = [
        whole,
        whole,
        gain,
        gain,
        pl.BlockSpec((tok_count, 1), lambda g: (0, 0)),
        pl.BlockSpec((1, tok_count), lambda g: (0, 0)),
    ]
    raw = pl.BlockSpec((tok_count, wide), lambda g: (0, first + g))
    heads = pl.BlockSpec((tok_count, group_size * head_size), lambda g: (0, first + g))
    lse = pl.BlockSpec((1, group_size, tok_count), lambda g: (first + g, 0, 0))
    raw_out = pl.BlockSpec((tok_count, wide), lambda g: (0, g))
    heads_out = pl.BlockSpec((tok_count, group_size * head_size), lambda g: (0, g))
    lse_out = pl.BlockSpec((1, group_size, tok_count), lambda g: (g, 0, 0))
    pairs = kv_heads * group_size * tok_count * tok_count
    low, full = jnp.bfloat16, jnp.float32
    limit = pltpu.CompilerParams(vmem_limit_bytes=44 * 1024 * 1024)

    def forward(earlier, *operands):
        count = len(earlier)
        return pl.pallas_call(
            lambda *refs: attend_kernel(group_size, block, *refs[count:]),
            grid=(kv_heads,),
            in_specs=[pl.BlockSpec(memory_space=pl.ANY)] * count + [raw] + common,
            out_specs=[heads_out, lse_out],
            out_shape=[
                jax.ShapeDtypeStruct((tok_count, kv_heads * group_size * head_size), low),
                jax.ShapeDtypeStruct((kv_heads, group_size, tok_count), full),
            ],
            scratch_shapes=[
                pltpu.VMEM((tok_count, group_size * head_size), low),
                pltpu.VMEM((tok_count, head_size), low),
                pltpu.VMEM((head_size, tok_count), low),
            ],
            compiler_params=limit,
            cost_estimate=pl.CostEstimate(
                flops=pairs, bytes_accessed=0, transcendentals=0
            ),
        )(*earlier, *operands)

    def backward(earlier, *operands):
        count = len(earlier)
        return pl.pallas_call(
            lambda *refs: attend_back_kernel(group_size, block, *refs[count:]),
            grid=(kv_heads,),
            in_specs=[pl.BlockSpec(memory_space=pl.ANY)] * count + [raw, heads, heads, lse] + common,
            out_specs=[raw_out, pl.BlockSpec((1, 2, head_size), lambda g: (g, 0, 0))],
            out_shape=[
                jax.ShapeDtypeStruct((tok_count, kv_heads * wide), low),
                jax.ShapeDtypeStruct((kv_heads, 2, head_size), full),
            ],
            scratch_shapes=[
                pltpu.VMEM((tok_count, (group_size + 1) * head_size), full),
                pltpu.VMEM((tok_count, (group_size + 1) * head_size), full),
                pltpu.VMEM((tok_count, group_size * head_size), low),
                pltpu.VMEM((tok_count, head_size), low),
                pltpu.VMEM((head_size, tok_count), low),
                pltpu.VMEM((tok_count, head_size), low),
                pltpu.VMEM((tok_count, head_size), full),
                pltpu.VMEM((tok_count, head_size), full),
            ],
            compiler_params=limit,
            cost_estimate=pl.CostEstimate(
                flops=pairs, bytes_accessed=0, transcendentals=0
            ),
        )(*earlier, *operands)

    return forward, backward


def sum_cores(partial_of, c_index):
    got = swap(partial_of(1 - c_index).astype(jnp.bfloat16), "tensor")
    return (partial_of(c_index) + got.astype(jnp.float32)).astype(jnp.bfloat16)


def cross_sum(mine):
    return wide_sum(mine, swap(mine, "context")).astype(jnp.bfloat16)


def sum_part(mine, x_index):
    got = swap(half_of(mine, 1 - x_index, 0), "context")
    return wide_sum(half_of(mine, x_index, 0), got)


def dot_rows(left, right):
    return jnp.dot(left, right, preferred_element_type=jnp.float32)


def dot_back(left, right):
    return jnp.einsum("pf,df->pd", left, right, preferred_element_type=jnp.float32)


def dot_grad(left, right):
    return jnp.einsum("pd,pf->df", left, right, preferred_element_type=jnp.float32)


def quarter_shards(
    hidden_in,
    cotangent,
    segment,
    position,
    w_query,
    w_key,
    w_value,
    w_output,
    w_gate,
    w_up,
    w_down,
    attn_gain,
    ffn_gain,
    query_gain,
    key_gain,
):
    x_index, c_index = lax.axis_index("context"), lax.axis_index("tensor")
    fsdp_size = lax.axis_size("fsdp")
    rows_shard = w_query.shape[0]
    model = rows_shard * fsdp_size
    head_size = query_gain.shape[0] * fsdp_size
    q_width, kv_width = w_query.shape[1] // 2, w_key.shape[1] // 2
    ff_width = w_gate.shape[1] // 2
    q_heads, kv_heads = q_width // head_size, kv_width // head_size
    group_size = q_heads // kv_heads
    group_width = group_size * head_size

    def mine(weight, axis):
        return half_of(weight, x_index, axis)

    gains = jnp.concatenate([attn_gain, ffn_gain, query_gain, key_gain])
    gain_rows = jnp.pad(gains[None], ((0, 15), (0, q_width + 2 * kv_width - gains.shape[0])))
    blob_a = pack_call(x_index, kv_heads, head_size, w_query, w_key, w_value, gain_rows)
    blob_o = mine(w_output, 0).T
    blob_g, blob_u = mine(w_gate, 1), mine(w_up, 1)
    blob_d = mine(w_down, 0).T

    def own_part(rows):
        return half_of(half_of(rows, x_index, 0), c_index, 1)

    def wide_half(weight, h):
        return half_of(weight, h, 0)

    def grouped(grads):
        return grads.astype(jnp.bfloat16).reshape(fsdp_size, rows_shard, -1)

    def stacked(pieces):
        return stack_pieces(pieces[0], pieces[1:])

    turned_a = turn_pieces(blob_a)
    far_own_a = flip_pieces(blob_a)
    hidden_got = swap(hidden_in[0], "context")
    last = len(turned_a) // 2
    far_a = [
        far_own_a if step == 0 else None if step == last else flip_pieces(piece)
        for step, piece in enumerate(turned_a)
    ]
    far_a.pop(last)
    turned_a, far_a, hidden_got, blob_o, blob_g, blob_u, blob_d = fence(
        turned_a, far_a, hidden_got, blob_o, blob_g, blob_u, blob_d
    )

    far_last = flip_pieces(turned_a[last])
    turned_o = turn_pieces(blob_o)
    marks = jnp.stack([segment[0], position[0]])
    marks_got = swap(marks, "context")
    hidden_column = pair_join(x_index, hidden_in[0], hidden_got, 0)
    hidden_other = swap(hidden_column, "tensor")
    hidden_rows = pair_join(c_index, hidden_column, hidden_other, 1)
    x_rows = hidden_rows.astype(jnp.float32)
    tok_count = x_rows.shape[0]
    recip_one = norm_stats(x_rows)
    far_a, far_last, turned_o, hidden_rows, recip_one, marks_got, blob_g, turned_a, cotangent = (
        fence(
            far_a, far_last, turned_o, hidden_rows, recip_one, marks_got, blob_g, turned_a,
            cotangent,
        )
    )

    near_o = stacked(turned_o)
    far_o = flip_pieces(near_o)
    turned_g = turn_pieces(blob_g)
    dy_got = swap(cotangent[0], "context")
    marks = pair_join(x_index, marks, marks_got, 1)
    segment_all, position_all = marks[0], marks[1]
    half_size = head_size // 2
    freq_table = THETA ** (-jnp.arange(half_size, dtype=jnp.float32) * 2.0 / head_size)
    angle_table = position_all.astype(jnp.float32)[:, None] * freq_table[None, :]
    cosine_half, sine_half = jnp.cos(angle_table), jnp.sin(angle_table)
    cosine_table = jnp.concatenate([cosine_half, cosine_half], axis=1)
    sine_table = jnp.concatenate([-sine_half, sine_half], axis=1)
    all_a = place_rows(turned_a, far_a[:last] + [far_last] + far_a[last:])
    w_qkv = all_a[:, :rows_shard].reshape(model, -1)
    gain_all = all_a[:, rows_shard].astype(jnp.float32)
    gain_part = query_gain.shape[0]
    attn_gain32 = gain_all[:, :rows_shard].reshape(model)
    ffn_gain32 = gain_all[:, rows_shard : 2 * rows_shard].reshape(model)
    qgain32 = gain_all[:, 2 * rows_shard : 2 * rows_shard + gain_part].reshape(head_size)
    kgain32 = gain_all[:, 2 * rows_shard + gain_part : 2 * rows_shard + 2 * gain_part].reshape(
        head_size
    )
    x_rows = hidden_rows.astype(jnp.float32)
    attn_in = (x_rows * recip_one * attn_gain32).astype(jnp.bfloat16)
    qkv_raw = dot_rows(attn_in, w_qkv)
    qkv_raw, far_o, near_o, turned_g, dy_got, blob_u, cosine_table, sine_table = fence(
        qkv_raw, far_o, near_o, turned_g, dy_got, blob_u, cosine_table, sine_table
    )

    near_g = stacked(turned_g)
    far_g = flip_pieces(near_g)
    turned_u = turn_pieces(blob_u)
    shared = (
        cosine_table,
        sine_table,
        qgain32[None],
        kgain32[None],
        segment_all[:, None],
        segment_all[None, :],
    )
    attend, _ = attention_calls(tok_count, head_size, group_size, 0, kv_heads)
    attn_low, log_total = attend((), qkv_raw, *shared)
    all_o = place_rows([near_o], [far_o]).reshape(model, -1)
    attn_low, all_o, far_g, near_g, turned_u, blob_d, dy_got, cotangent = fence(
        attn_low, all_o, far_g, near_g, turned_u, blob_d, dy_got, cotangent
    )

    near_u = stacked(turned_u)
    far_u = flip_pieces(near_u)
    turned_d = turn_pieces(blob_d)
    attn_mine = sum_cores(lambda h: dot_back(attn_low, wide_half(all_o, h)), c_index)
    attn_total = cross_sum(attn_mine)
    all_g = place_rows([near_g], [far_g]).reshape(model, -1)
    dy_column = pair_join(x_index, cotangent[0], dy_got, 0)
    rows_dy = pair_join(c_index, dy_column, swap(dy_column, "tensor"), 1)
    all_u = place_rows([near_u], [far_u]).reshape(model, -1)
    far_own_d = flip_pieces(after(blob_d, far_u))
    attn_total, all_g, all_u, turned_d, far_own_d, rows_dy = fence(
        attn_total, all_g, all_u, turned_d, far_own_d, rows_dy
    )

    attn_other = swap(attn_total, "tensor")
    near_d = stack_pieces(turned_d[1], turned_d[2:])
    far_d = flip_pieces(near_d)
    mid_rows = x_rows + pair_join(c_index, attn_total, attn_other, 1).astype(jnp.float32)
    recip_two = norm_stats(mid_rows)
    normed_two = mid_rows * recip_two
    ffn_in = (normed_two * ffn_gain32).astype(jnp.bfloat16)
    gate_pre, up_pre = dot_rows(ffn_in, all_g), dot_rows(ffn_in, all_u)
    gate_sig = jax.nn.sigmoid(gate_pre)
    hidden_low = (gate_pre * gate_sig * up_pre).astype(jnp.bfloat16)
    stay_d, away_d, apart_d = split_rows(grouped(dot_grad(rows_dy, hidden_low)), apart=True)
    gate_pre, up_pre, far_d, near_d, ffn_in, all_g, all_u, stay_d, away_d, apart_d, hidden_low = fence(
        gate_pre, up_pre, far_d, near_d, ffn_in, all_g, all_u, stay_d, away_d, apart_d, hidden_low
    )

    got_d = flip_pieces(away_d)
    gate_sig = jax.nn.sigmoid(gate_pre)
    gate_act = gate_pre * gate_sig
    all_d = place_rows([turned_d[0], near_d], [far_own_d, far_d]).reshape(model, -1)
    grad_hidden = dot_rows(rows_dy, all_d)
    grad_gate = (grad_hidden * up_pre * gate_sig * (1.0 + gate_pre * (1.0 - gate_sig))).astype(
        jnp.bfloat16
    )
    grad_up_pre = (grad_hidden * gate_act).astype(jnp.bfloat16)
    ffn_mine = sum_cores(
        lambda h: dot_back(grad_gate, wide_half(all_g, h))
        + dot_back(grad_up_pre, wide_half(all_u, h)),
        c_index,
    )
    ffn_total = cross_sum(ffn_mine)
    sent_d = turn_sums(after(stay_d, ffn_mine), got_d)
    stay_g, away_g, apart_g = split_rows(
        grouped(dot_grad(ffn_in, after(grad_gate, ffn_mine))), apart=True
    )
    got_g = flip_pieces(after(away_g, got_d))
    stay_u, away_u, apart_u = split_rows(
        grouped(dot_grad(ffn_in, after(grad_up_pre, ffn_mine))), apart=True
    )
    late_hidden = after(hidden_low, ffn_mine)
    out_away = dot_back(late_hidden, wide_half(all_d, 1 - c_index)).astype(jnp.bfloat16)
    out_stay = dot_back(late_hidden, wide_half(all_d, c_index))
    (
        ffn_total, stay_d, apart_d, sent_d, stay_g, got_g, apart_g, stay_u, away_u, apart_u,
        out_away, out_stay, rows_dy, mid_rows,
    ) = fence(
        ffn_total, stay_d, apart_d, sent_d, stay_g, got_g, apart_g, stay_u, away_u, apart_u,
        out_away, out_stay, rows_dy, mid_rows,
    )

    def finish(stay, got, sent, earlier=()):
        low = wide_sum(stay[0], got, *sent).astype(jnp.bfloat16)
        return low, swap(after(low, *earlier), "context")

    ffn_other = swap(ffn_total, "tensor")
    got_u = flip_pieces(away_u)
    sent_g = turn_sums(stay_g, got_g)
    out_other = swap(after(out_away, ffn_other), "tensor")
    out_mine = wide_sum(out_stay, out_other).astype(jnp.bfloat16)
    grad_ffn_in = pair_join(c_index, ffn_total, ffn_other, 1).astype(jnp.float32)
    normed_two = mid_rows * recip_two
    grad_ffn_gain = jnp.sum(grad_ffn_in * normed_two, axis=0)
    grad_mid = rows_dy.astype(jnp.float32) + norm_back(
        grad_ffn_in * ffn_gain32, normed_two, recip_two
    )
    grad_mid_low = grad_mid.astype(jnp.bfloat16)
    grad_attn = dot_rows(grad_mid_low, all_o).astype(jnp.bfloat16)
    stay_o, away_o = split_rows(grouped(dot_grad(grad_mid_low, attn_low)))
    (
        got_u, stay_u, sent_g, stay_g, sent_d, stay_d, grad_attn, away_o, stay_o, apart_d, apart_g,
        apart_u, attn_in, mid_rows, out_mine,
    ) = fence(
        got_u, stay_u, sent_g, stay_g, sent_d, stay_d, grad_attn, away_o, stay_o, apart_d, apart_g,
        apart_u, attn_in, mid_rows, out_mine,
    )

    got_o = flip_pieces(away_o)
    sent_u = turn_sums(stay_u, got_u)
    half_heads = kv_heads // 2
    _, back_first = attention_calls(tok_count, head_size, group_size, 0, half_heads)
    _, back_second = attention_calls(tok_count, head_size, group_size, half_heads, half_heads)
    back_a, gains_a = back_first((), qkv_raw, attn_low, grad_attn, log_total, *shared)
    stay_a, away_a = split_rows(grouped(dot_grad(attn_in, back_a)))
    got_own_d = flip_pieces(apart_d)
    (
        got_o, stay_o, sent_u, stay_u, sent_g, stay_g, back_a, gains_a, stay_a, away_a, grad_attn,
        attn_in, mid_rows, out_mine, got_own_d, stay_d, sent_d, apart_g, apart_u,
    ) = fence(
        got_o, stay_o, sent_u, stay_u, sent_g, stay_g, back_a, gains_a, stay_a, away_a, grad_attn,
        attn_in, mid_rows, out_mine, got_own_d, stay_d, sent_d, apart_g, apart_u,
    )

    got_a = flip_pieces(away_a)
    sent_o = turn_sums(stay_o, got_o)
    back_b, gains_b = back_second((), qkv_raw, attn_low, grad_attn, log_total, *shared)
    out_got = swap(half_of(out_mine, 1 - x_index, 0), "context")
    (
        got_a, stay_a, sent_o, stay_o, got_o, back_a, back_b, gains_a, gains_b, attn_in, mid_rows,
        out_mine, out_got, apart_g, apart_u, got_own_d, stay_d, sent_d, stay_u, sent_u, stay_g, sent_g,
    ) = fence(
        got_a, stay_a, sent_o, stay_o, got_o, back_a, back_b, gains_a, gains_b, attn_in, mid_rows,
        out_mine, out_got, apart_g, apart_u, got_own_d, stay_d, sent_d, stay_u, sent_u, stay_g, sent_g,
    )

    got_own_g = flip_pieces(apart_g)
    got_own_u = flip_pieces(apart_u)
    own_o, far_o = finish(stay_o, got_o[0], sent_o)
    own_d, far_d = finish(stay_d, got_own_d, sent_d)
    back = jnp.concatenate([back_a, back_b], axis=1)
    normed_one = x_rows * recip_one
    gain_halves = {}

    def attn_part(h):
        part = dot_back(back, wide_half(w_qkv, h))
        gain_halves[len(gain_halves)] = jnp.sum(part * half_of(normed_one, h, 1), axis=0)
        return part

    attn_in_mine = sum_cores(attn_part, c_index)
    grad_attn_gain = pair_join(c_index, gain_halves[1], gain_halves[0], 0)
    head_gains = jnp.sum(gains_a, axis=0) + jnp.sum(gains_b, axis=0)
    first_device = (x_index == 0) & (c_index == 0)
    gain_block = jnp.concatenate(
        [
            grad_attn_gain.reshape(fsdp_size, rows_shard),
            jnp.where(first_device, grad_ffn_gain, 0.0).reshape(fsdp_size, rows_shard),
            head_gains[0].reshape(fsdp_size, gain_part),
            head_gains[1].reshape(fsdp_size, gain_part),
        ],
        axis=1,
    ).astype(jnp.bfloat16)
    gain_block = gain_block.astype(jnp.float32) + swap(gain_block, "tensor").astype(jnp.float32)
    gain_block = jnp.pad(
        gain_block.astype(jnp.bfloat16)[:, None],
        ((0, 0), (0, 15), (0, back_b.shape[1] - gain_block.shape[1])),
    )
    stay_b, away_b = split_rows(grouped(dot_grad(attn_in, back_b)), gain_block)
    (
        stay_a, got_a, attn_in_mine, stay_b, away_b, mid_rows, out_mine, out_got, got_own_g,
        got_own_u, stay_g, sent_g, stay_u, sent_u, own_o, far_o, own_d, far_d,
    ) = fence(
        stay_a, got_a, attn_in_mine, stay_b, away_b, mid_rows, out_mine, out_got, got_own_g,
        got_own_u, stay_g, sent_g, stay_u, sent_u, own_o, far_o, own_d, far_d,
    )

    got_b = flip_pieces(away_b)
    sent_a = turn_sums(stay_a, got_a)
    attn_in_part = sum_part(attn_in_mine, x_index).astype(jnp.bfloat16)
    (
        got_b, stay_b, stay_a, got_a, sent_a, attn_in_part, got_own_g, stay_g, sent_g, got_own_u,
        stay_u, sent_u, mid_rows, out_mine, out_got,
    ) = fence(
        got_b, stay_b, stay_a, got_a, sent_a, attn_in_part, got_own_g, stay_g, sent_g, got_own_u,
        stay_u, sent_u, mid_rows, out_mine, out_got,
    )

    out_part = wide_sum(half_of(out_mine, x_index, 0), out_got)
    block_out = (own_part(mid_rows) + out_part).astype(jnp.bfloat16)[None]
    sent_b = turn_sums(stay_b, got_b)
    attn_in_other = swap(attn_in_part, "tensor")
    own_a, far_a = finish(stay_a, got_a[0], sent_a)
    own_g, far_g = finish(stay_g, got_own_g, sent_g, (far_a,))
    grad_attn_in = pair_join(c_index, attn_in_part, attn_in_other, 1).astype(jnp.float32)
    normed_part = half_of(x_rows * recip_one, x_index, 0)
    grad_input = half_of(grad_mid, x_index, 0) + norm_back(
        grad_attn_in * attn_gain32, normed_part, half_of(recip_one, x_index, 0)
    )
    grad_input_part = half_of(grad_input, c_index, 1)[None]
    (
        sent_b, stay_b, got_b, own_a, far_a, own_g, far_g, grad_input_part, block_out, got_own_u,
        stay_u, sent_u,
    ) = fence(
        sent_b, stay_b, got_b, own_a, far_a, own_g, far_g, grad_input_part, block_out, got_own_u,
        stay_u, sent_u,
    )

    own_u, far_u = finish(stay_u, got_own_u, sent_u)
    own_b, far_b = finish(stay_b, got_b[0], sent_b)
    gain_sum = own_b[rows_shard].astype(jnp.float32) + far_b[rows_shard].astype(jnp.float32)

    def outcome(own, far):
        return pair_join(x_index, own, far, 1).astype(jnp.float32)

    def outcome_columns(own, far):
        return pair_join(x_index, own.T, far.T, 0).astype(jnp.float32)

    def picked(first, size):
        wide = group_width + 2 * head_size
        starts = [g * wide + first for g in range(kv_heads // 2)]

        def columns(halves):
            return jnp.concatenate(
                [half[:rows_shard, s : s + size] for half in halves for s in starts], axis=1
            )

        return pair_join(x_index, columns((own_a, own_b)), columns((far_a, far_b)), 1).astype(
            jnp.float32
        )

    return (
        block_out,
        grad_input_part,
        picked(0, group_width),
        picked(group_width, head_size),
        picked(group_width + head_size, head_size),
        outcome_columns(own_o, far_o),
        outcome(own_g, far_g),
        outcome(own_u, far_u),
        outcome_columns(own_d, far_d),
        gain_sum[:rows_shard],
        gain_sum[rows_shard : 2 * rows_shard],
        gain_sum[2 * rows_shard : 2 * rows_shard + gain_part],
        gain_sum[2 * rows_shard + gain_part : 2 * rows_shard + 2 * gain_part],
    )


def fits_quarters(mesh):
    sizes = mesh.shape
    return sizes["context"] == 2 and sizes["tensor"] == 2 and sizes["fsdp"] % 2 == 0


def solution(mesh):
    in_specs = (
        P("fsdp", "context", "tensor"),
        P("fsdp", "context", "tensor"),
        P("fsdp", "context"),
        P("fsdp", "context"),
        P("fsdp", "tensor"),
        P("fsdp", "tensor"),
        P("fsdp", "tensor"),
        P("tensor", "fsdp"),
        P("fsdp", "tensor"),
        P("fsdp", "tensor"),
        P("tensor", "fsdp"),
        P("fsdp"),
        P("fsdp"),
        P("fsdp"),
        P("fsdp"),
    )
    out_specs = (
        P("fsdp", "context", "tensor"),
        P("fsdp", "context", "tensor"),
        P("fsdp", "tensor"),
        P("fsdp", "tensor"),
        P("fsdp", "tensor"),
        P("tensor", "fsdp"),
        P("fsdp", "tensor"),
        P("fsdp", "tensor"),
        P("tensor", "fsdp"),
        P("fsdp"),
        P("fsdp"),
        P("fsdp"),
        P("fsdp"),
    )
    shards = quarter_shards if fits_quarters(mesh) else plain_shards
    return jax.shard_map(shards, mesh=mesh, in_specs=in_specs, out_specs=out_specs, check_vma=False)
```

```python
import jax
import jax.numpy as jnp
from jax import lax
from jax.experimental import pallas as pl
from jax.experimental.pallas import tpu as pltpu
from jax.sharding import PartitionSpec as P

EPS = 1e-06
THETA = 1000000.0


def norm_stats(values):
    return lax.rsqrt(jnp.mean(values * values, axis=-1, keepdims=True) + EPS)


def norm_back(grad_out, normed, recip_root):
    return recip_root * (grad_out - normed * jnp.mean(grad_out * normed, axis=-1, keepdims=True))


def rotary_tables(position_row, head_size):
    half_size = head_size // 2
    freq_table = THETA ** (-jnp.arange(half_size, dtype=jnp.float32) * 2.0 / head_size)
    angle_table = position_row.astype(jnp.float32)[:, None] * freq_table[None, :]
    return (jnp.cos(angle_table)[:, None, :], jnp.sin(angle_table)[:, None, :])


def rotate(values, cosine_table, sine_table, turn_sign):
    half_size = values.shape[-1] // 2
    first_half = values[..., :half_size]
    second_half = values[..., half_size:]
    turned = turn_sign * sine_table
    return jnp.concatenate(
        [
            first_half * cosine_table - second_half * turned,
            second_half * cosine_table + first_half * turned,
        ],
        axis=-1,
    )


def plain_shards(
    hidden_in,
    cotangent,
    segment,
    position,
    w_query,
    w_key,
    w_value,
    w_output,
    w_gate,
    w_up,
    w_down,
    attn_gain,
    ffn_gain,
    query_gain,
    key_gain,
):
    (
        wq_full,
        wk_full,
        wv_full,
        wo_full,
        wg_full,
        wu_full,
        wd_full,
        attn_full,
        ffn_full,
        qgain_full,
        kgain_full,
    ) = (
        lax.all_gather(w_query, "fsdp", axis=0, tiled=True),
        lax.all_gather(w_key, "fsdp", axis=0, tiled=True),
        lax.all_gather(w_value, "fsdp", axis=0, tiled=True),
        lax.all_gather(w_output, "fsdp", axis=1, tiled=True),
        lax.all_gather(w_gate, "fsdp", axis=0, tiled=True),
        lax.all_gather(w_up, "fsdp", axis=0, tiled=True),
        lax.all_gather(w_down, "fsdp", axis=1, tiled=True),
        lax.all_gather(attn_gain, "fsdp", axis=0, tiled=True),
        lax.all_gather(ffn_gain, "fsdp", axis=0, tiled=True),
        lax.all_gather(query_gain, "fsdp", axis=0, tiled=True),
        lax.all_gather(key_gain, "fsdp", axis=0, tiled=True),
    )
    rows_x, rows_dy = (
        lax.all_gather(hidden_in[0], "tensor", axis=1, tiled=True),
        lax.all_gather(cotangent[0], "tensor", axis=1, tiled=True),
    )
    tok_count = rows_x.shape[0]
    feat_part = hidden_in.shape[2]
    head_size = qgain_full.shape[0]
    q_heads = wq_full.shape[1] // head_size
    kv_heads = wk_full.shape[1] // head_size
    group_size = q_heads // kv_heads
    score_scale = head_size ** (-0.5)
    x_rows = rows_x.astype(jnp.float32)
    recip_one = norm_stats(x_rows)
    normed_one = x_rows * recip_one
    attn_gain32 = attn_full.astype(jnp.float32)
    attn_in = (normed_one * attn_gain32).astype(jnp.bfloat16)
    query_raw = jnp.dot(attn_in, wq_full, preferred_element_type=jnp.float32).reshape(
        tok_count, q_heads, head_size
    )
    key_raw = jnp.dot(attn_in, wk_full, preferred_element_type=jnp.float32).reshape(
        tok_count, kv_heads, head_size
    )
    value_raw = jnp.dot(attn_in, wv_full, preferred_element_type=jnp.float32)
    cosine_table, sine_table = rotary_tables(position[0], head_size)
    recip_query = norm_stats(query_raw)
    query_hat = query_raw * recip_query
    qgain32 = qgain_full.astype(jnp.float32)
    query_rot = rotate(query_hat * qgain32, cosine_table, sine_table, 1.0).astype(jnp.bfloat16)
    recip_key = norm_stats(key_raw)
    key_hat = key_raw * recip_key
    kgain32 = kgain_full.astype(jnp.float32)
    key_rot = rotate(key_hat * kgain32, cosine_table, sine_table, 1.0).astype(jnp.bfloat16)
    value_low = value_raw.astype(jnp.bfloat16).reshape(tok_count, kv_heads, head_size)
    key_all, value_all, segment_all = (
        lax.all_gather(key_rot, "context", axis=0, tiled=True),
        lax.all_gather(value_low, "context", axis=0, tiled=True),
        lax.all_gather(segment[0], "context", axis=0, tiled=True),
    )
    query_index = lax.axis_index("context") * tok_count + jnp.arange(tok_count, dtype=jnp.int32)
    key_index = jnp.arange(key_all.shape[0], dtype=jnp.int32)
    allowed = (segment[0][:, None] == segment_all[None, :]) & (
        key_index[None, :] <= query_index[:, None]
    )
    query_group = query_rot.reshape(tok_count, kv_heads, group_size, head_size)

    def scores_of():
        raw_scores = (
            jnp.einsum("pkgd,lkd->kgpl", query_group, key_all, preferred_element_type=jnp.float32)
            * score_scale
        )
        return jnp.where(allowed, raw_scores, -1e30)

    masked = scores_of()
    row_max = jnp.max(masked, axis=-1, keepdims=True)
    exp_terms = jnp.exp(masked - row_max)
    row_total = jnp.sum(exp_terms, axis=-1, keepdims=True)
    log_total = row_max + jnp.log(row_total)
    probs_fwd = (exp_terms / row_total).astype(jnp.bfloat16)
    attn_rows = jnp.einsum(
        "kgpl,lkd->pkgd", probs_fwd, value_all, preferred_element_type=jnp.float32
    )
    attn_low = attn_rows.reshape(tok_count, q_heads * head_size).astype(jnp.bfloat16)
    attn_sum = lax.psum(
        jnp.dot(attn_low, wo_full, preferred_element_type=jnp.float32).astype(jnp.bfloat16),
        "tensor",
    ).astype(jnp.float32)
    mid_rows = x_rows + attn_sum
    recip_two = norm_stats(mid_rows)
    normed_two = mid_rows * recip_two
    ffn_gain32 = ffn_full.astype(jnp.float32)
    ffn_in = (normed_two * ffn_gain32).astype(jnp.bfloat16)
    gate_pre = jnp.dot(ffn_in, wg_full, preferred_element_type=jnp.float32)
    up_pre = jnp.dot(ffn_in, wu_full, preferred_element_type=jnp.float32)
    gate_sig = jax.nn.sigmoid(gate_pre)
    gate_act = gate_pre * gate_sig
    hidden_low = (gate_act * up_pre).astype(jnp.bfloat16)
    ffn_rows = lax.psum_scatter(
        jnp.dot(hidden_low, wd_full, preferred_element_type=jnp.float32).astype(jnp.bfloat16),
        "tensor",
        scatter_dimension=1,
        tiled=True,
    ).astype(jnp.float32)
    feat_first = lax.axis_index("tensor") * feat_part
    mid_part = lax.dynamic_slice_in_dim(mid_rows, feat_first, feat_part, 1)
    block_out = (mid_part + ffn_rows).astype(jnp.bfloat16)[None]
    (
        wq_full,
        wk_full,
        wv_full,
        wo_full,
        wg_full,
        wu_full,
        wd_full,
        attn_full,
        ffn_full,
        qgain_full,
        kgain_full,
    ) = (
        lax.all_gather(w_query, "fsdp", axis=0, tiled=True),
        lax.all_gather(w_key, "fsdp", axis=0, tiled=True),
        lax.all_gather(w_value, "fsdp", axis=0, tiled=True),
        lax.all_gather(w_output, "fsdp", axis=1, tiled=True),
        lax.all_gather(w_gate, "fsdp", axis=0, tiled=True),
        lax.all_gather(w_up, "fsdp", axis=0, tiled=True),
        lax.all_gather(w_down, "fsdp", axis=1, tiled=True),
        lax.all_gather(attn_gain, "fsdp", axis=0, tiled=True),
        lax.all_gather(ffn_gain, "fsdp", axis=0, tiled=True),
        lax.all_gather(query_gain, "fsdp", axis=0, tiled=True),
        lax.all_gather(key_gain, "fsdp", axis=0, tiled=True),
    )
    grad_w_down = jnp.einsum("pf,pd->fd", hidden_low, rows_dy, preferred_element_type=jnp.float32)
    grad_hidden = jnp.einsum("pd,fd->pf", rows_dy, wd_full, preferred_element_type=jnp.float32)
    grad_gate = (grad_hidden * up_pre * gate_sig * (1.0 + gate_pre * (1.0 - gate_sig))).astype(
        jnp.bfloat16
    )
    grad_up_pre = (grad_hidden * gate_act).astype(jnp.bfloat16)
    grad_w_gate = jnp.einsum("pd,pf->df", ffn_in, grad_gate, preferred_element_type=jnp.float32)
    grad_w_up = jnp.einsum("pd,pf->df", ffn_in, grad_up_pre, preferred_element_type=jnp.float32)
    ffn_in_part = jnp.einsum(
        "pf,df->pd", grad_gate, wg_full, preferred_element_type=jnp.float32
    ) + jnp.einsum("pf,df->pd", grad_up_pre, wu_full, preferred_element_type=jnp.float32)
    grad_ffn_in = lax.psum(ffn_in_part.astype(jnp.bfloat16), "tensor").astype(jnp.float32)
    grad_ffn_gain = jnp.sum(grad_ffn_in * normed_two, axis=0)
    grad_mid = rows_dy.astype(jnp.float32) + norm_back(
        grad_ffn_in * ffn_gain32, normed_two, recip_two
    )
    grad_mid_low = grad_mid.astype(jnp.bfloat16)
    grad_w_output = jnp.einsum(
        "pf,pd->fd", attn_low, grad_mid_low, preferred_element_type=jnp.float32
    )
    grad_attn = jnp.einsum("pd,fd->pf", grad_mid_low, wo_full, preferred_element_type=jnp.float32)
    grad_attn = grad_attn.astype(jnp.bfloat16).reshape(tok_count, kv_heads, group_size, head_size)
    soft_probs = jnp.exp(scores_of() - log_total)
    grad_probs = jnp.einsum(
        "pkgd,lkd->kgpl", grad_attn, value_all, preferred_element_type=jnp.float32
    )
    row_delta = jnp.sum(soft_probs * grad_probs, axis=-1, keepdims=True)
    grad_scores = (soft_probs * (grad_probs - row_delta)).astype(jnp.bfloat16)
    probs_low = soft_probs.astype(jnp.bfloat16)
    grad_query = (
        jnp.einsum("kgpl,lkd->pkgd", grad_scores, key_all, preferred_element_type=jnp.float32)
        * score_scale
    )
    grad_query = grad_query.reshape(tok_count, q_heads, head_size)
    grad_key_rows = (
        jnp.einsum("kgpl,pkgd->lkd", grad_scores, query_group, preferred_element_type=jnp.float32)
        * score_scale
    )
    grad_value_rows = jnp.einsum(
        "kgpl,pkgd->lkd", probs_low, grad_attn, preferred_element_type=jnp.float32
    )
    key_value_grads = lax.psum_scatter(
        jnp.concatenate(
            [
                grad_key_rows.reshape(tok_count * lax.axis_size("context"), -1),
                grad_value_rows.reshape(tok_count * lax.axis_size("context"), -1),
            ],
            axis=1,
        ).astype(jnp.bfloat16),
        "context",
        scatter_dimension=0,
        tiled=True,
    ).astype(jnp.float32)
    kv_width = kv_heads * head_size
    grad_key = key_value_grads[:, :kv_width].reshape(tok_count, kv_heads, head_size)
    grad_value_low = key_value_grads[:, kv_width:].astype(jnp.bfloat16)
    unrot_query = rotate(grad_query, cosine_table, sine_table, -1.0)
    grad_query_gain = jnp.sum(unrot_query * query_hat, axis=(0, 1))
    grad_query_raw = (
        norm_back(unrot_query * qgain32, query_hat, recip_query)
        .astype(jnp.bfloat16)
        .reshape(tok_count, q_heads * head_size)
    )
    unrot_key = rotate(grad_key, cosine_table, sine_table, -1.0)
    grad_key_gain = jnp.sum(unrot_key * key_hat, axis=(0, 1))
    grad_key_raw = (
        norm_back(unrot_key * kgain32, key_hat, recip_key)
        .astype(jnp.bfloat16)
        .reshape(tok_count, kv_width)
    )
    grad_w_query = jnp.einsum(
        "pd,pf->df", attn_in, grad_query_raw, preferred_element_type=jnp.float32
    )
    grad_w_key = jnp.einsum("pd,pf->df", attn_in, grad_key_raw, preferred_element_type=jnp.float32)
    grad_w_value = jnp.einsum(
        "pd,pf->df", attn_in, grad_value_low, preferred_element_type=jnp.float32
    )
    attn_in_part = (
        jnp.einsum("pf,df->pd", grad_query_raw, wq_full, preferred_element_type=jnp.float32)
        + jnp.einsum("pf,df->pd", grad_key_raw, wk_full, preferred_element_type=jnp.float32)
        + jnp.einsum("pf,df->pd", grad_value_low, wv_full, preferred_element_type=jnp.float32)
    )
    grad_attn_in, grad_query_gain, grad_key_gain = (
        lax.psum(attn_in_part.astype(jnp.bfloat16), "tensor").astype(jnp.float32),
        lax.psum(grad_query_gain.astype(jnp.bfloat16), "tensor").astype(jnp.float32),
        lax.psum(grad_key_gain.astype(jnp.bfloat16), "tensor").astype(jnp.float32),
    )
    grad_attn_gain = jnp.sum(grad_attn_in * normed_one, axis=0)
    grad_input = grad_mid + norm_back(
        grad_attn_in * attn_full.astype(jnp.float32), normed_one, recip_one
    )
    grad_input_part = lax.dynamic_slice_in_dim(grad_input, feat_first, feat_part, 1)[None]
    owned = (
        lax.psum_scatter(
            grad_w_query.astype(jnp.bfloat16), "fsdp", scatter_dimension=0, tiled=True
        ).astype(jnp.float32),
        lax.psum_scatter(
            grad_w_key.astype(jnp.bfloat16), "fsdp", scatter_dimension=0, tiled=True
        ).astype(jnp.float32),
        lax.psum_scatter(
            grad_w_value.astype(jnp.bfloat16), "fsdp", scatter_dimension=0, tiled=True
        ).astype(jnp.float32),
        lax.psum_scatter(
            grad_w_output.astype(jnp.bfloat16), "fsdp", scatter_dimension=1, tiled=True
        ).astype(jnp.float32),
        lax.psum_scatter(
            grad_w_gate.astype(jnp.bfloat16), "fsdp", scatter_dimension=0, tiled=True
        ).astype(jnp.float32),
        lax.psum_scatter(
            grad_w_up.astype(jnp.bfloat16), "fsdp", scatter_dimension=0, tiled=True
        ).astype(jnp.float32),
        lax.psum_scatter(
            grad_w_down.astype(jnp.bfloat16), "fsdp", scatter_dimension=1, tiled=True
        ).astype(jnp.float32),
        lax.psum_scatter(
            grad_attn_gain.astype(jnp.bfloat16), "fsdp", scatter_dimension=0, tiled=True
        ).astype(jnp.float32),
        lax.psum_scatter(
            grad_ffn_gain.astype(jnp.bfloat16), "fsdp", scatter_dimension=0, tiled=True
        ).astype(jnp.float32),
        lax.psum_scatter(
            grad_query_gain.astype(jnp.bfloat16), "fsdp", scatter_dimension=0, tiled=True
        ).astype(jnp.float32),
        lax.psum_scatter(
            grad_key_gain.astype(jnp.bfloat16), "fsdp", scatter_dimension=0, tiled=True
        ).astype(jnp.float32),
    )
    owned = (
        lax.psum(owned[0].astype(jnp.bfloat16), "context").astype(jnp.float32),
        lax.psum(owned[1].astype(jnp.bfloat16), "context").astype(jnp.float32),
        lax.psum(owned[2].astype(jnp.bfloat16), "context").astype(jnp.float32),
        lax.psum(owned[3].astype(jnp.bfloat16), "context").astype(jnp.float32),
        lax.psum(owned[4].astype(jnp.bfloat16), "context").astype(jnp.float32),
        lax.psum(owned[5].astype(jnp.bfloat16), "context").astype(jnp.float32),
        lax.psum(owned[6].astype(jnp.bfloat16), "context").astype(jnp.float32),
        lax.psum(owned[7].astype(jnp.bfloat16), "context").astype(jnp.float32),
        lax.psum(owned[8].astype(jnp.bfloat16), "context").astype(jnp.float32),
        lax.psum(owned[9].astype(jnp.bfloat16), "context").astype(jnp.float32),
        lax.psum(owned[10].astype(jnp.bfloat16), "context").astype(jnp.float32),
    )
    return (
        block_out,
        grad_input_part,
        owned[0],
        owned[1],
        owned[2],
        owned[3],
        owned[4],
        owned[5],
        owned[6],
        owned[7],
        owned[8],
        owned[9],
        owned[10],
    )


def fence(*values):
    return lax.optimization_barrier(values)


def after(value, *earlier):
    return lax.optimization_barrier((value,) + earlier)[0]


def swap(values, axis_name):
    return lax.ppermute(values, axis_name, [(0, 1), (1, 0)])


def pick(index, zero_item, one_item):
    return jnp.where(index == 0, zero_item, one_item)


def pair_join(index, own, other, axis):
    return jnp.concatenate([pick(index, own, other), pick(index, other, own)], axis=axis)


def half_of(values, index, axis):
    half = values.shape[axis] // 2
    return lax.dynamic_slice_in_dim(values, index * half, half, axis)


def ring_pairs(fsdp_size):
    columns = fsdp_size // 2
    flip = [(i, i ^ 1) for i in range(fsdp_size)]

    def turn(step):
        return [
            (z * 2 + y, ((z + step) % columns) * 2 + y) for z in range(columns) for y in range(2)
        ]

    return columns, flip, turn


def copy_call(copies_of, scalars, operands, shapes, copy_count, spaces):
    operand_count, result_count = len(operands), len(shapes)

    def kernel(scalar_ref, *refs):
        sources = refs[:operand_count]
        targets = refs[operand_count : operand_count + result_count]
        sems = refs[operand_count + result_count]
        copies = [
            pltpu.make_async_copy(source, target, sems.at[i])
            for i, (source, target) in enumerate(copies_of(scalar_ref, sources, targets))
        ]
        for copy in copies:
            copy.start()
        for copy in copies:
            copy.wait()

    moved = sum(2 * shape.size * shape.dtype.itemsize for shape in shapes)
    return pl.pallas_call(
        kernel,
        out_shape=shapes,
        in_specs=[pl.BlockSpec(memory_space=pltpu.SMEM)]
        + [pl.BlockSpec(memory_space=spaces[0])] * operand_count,
        out_specs=[pl.BlockSpec(memory_space=spaces[1])] * result_count,
        scratch_shapes=[pltpu.SemaphoreType.DMA((copy_count,))],
        compiler_params=pltpu.CompilerParams(vmem_limit_bytes=32 * 1024 * 1024),
        cost_estimate=pl.CostEstimate(flops=0, bytes_accessed=moved, transcendentals=0),
    )(jnp.stack(scalars).astype(jnp.int32), *operands)


def pack_call(x_index, kv_heads, head_size, w_query, w_key, w_value, gain_rows):
    rows, q_columns = w_query.shape
    group_width = q_columns // (2 * kv_heads)
    wide = group_width + 2 * head_size

    def kernel(x_ref, query_ref, key_ref, value_ref, gain_ref, out_ref):
        x = x_ref[0]
        for g in range(kv_heads):
            first = g * wide
            for ref, size in ((query_ref, group_width), (key_ref, head_size), (value_ref, head_size)):
                start = pl.multiple_of((x * kv_heads + g) * size, size)
                out_ref[:rows, first : first + size] = ref[:, pl.ds(start, size)]
                first += size
        out_ref[rows:, :] = gain_ref[...]

    return pl.pallas_call(
        kernel,
        out_shape=jax.ShapeDtypeStruct(
            (rows + gain_rows.shape[0], kv_heads * wide), w_query.dtype
        ),
        in_specs=[pl.BlockSpec(memory_space=pltpu.SMEM)]
        + [pl.BlockSpec(memory_space=pltpu.VMEM)] * 4,
        out_specs=pl.BlockSpec(memory_space=pltpu.VMEM),
    )(x_index.astype(jnp.int32)[None], w_query, w_key, w_value, gain_rows)


def turn_pieces(blob):
    columns, _, turn = ring_pairs(lax.axis_size("fsdp"))
    return [blob] + [lax.ppermute(blob, "fsdp", turn(step)) for step in range(1, columns)]


def flip_pieces(values):
    return lax.ppermute(values, "fsdp", ring_pairs(lax.axis_size("fsdp"))[1])


def stack_pieces(first, rest):
    pieces = [first] + list(rest)
    shape = (len(pieces),) + pieces[0].shape
    return copy_call(
        lambda at, own, out: [(piece, out[0].at[i]) for i, piece in enumerate(own)],
        [jnp.int32(0)],
        pieces,
        [jax.ShapeDtypeStruct(shape, pieces[0].dtype)],
        len(pieces),
        (pltpu.VMEM, pl.ANY),
    )[0]


def place_rows(near, far):
    fsdp_size = lax.axis_size("fsdp")
    columns = fsdp_size // 2
    place = lax.axis_index("fsdp")
    column, side = place // 2, place % 2
    sources = [(column - step + columns) % columns for step in range(columns)]
    near_at = [source * 2 + side for source in sources]
    far_at = [source * 2 + 1 - side for source in sources]
    operands = list(near) + list(far)

    def copies_of(at, own, out):
        copies, slot = [], 0
        for ref in own:
            if len(ref.shape) == 2:
                copies.append((ref, out[0].at[at[slot]]))
                slot += 1
                continue
            for i in range(ref.shape[0]):
                copies.append((ref.at[i], out[0].at[at[slot]]))
                slot += 1
        return copies

    return copy_call(
        copies_of,
        near_at + far_at,
        operands,
        [jax.ShapeDtypeStruct((fsdp_size,) + near[0].shape[-2:], near[0].dtype)],
        fsdp_size,
        (pltpu.VMEM, pl.ANY),
    )[0]


def split_rows(grads, extra=None, apart=False):
    fsdp_size = lax.axis_size("fsdp")
    columns = fsdp_size // 2
    place = lax.axis_index("fsdp")
    column, side = place // 2, place % 2
    parts = [grads] if extra is None else [grads, extra]
    rows = [part.shape[1] for part in parts]
    firsts = [0, rows[0]]
    order = [(column + step) % columns for step in range(columns)]

    def copies_of(at, own, out):
        copies = []
        for part, first, count in zip(own, firsts, rows):
            span = pl.ds(first, count)
            for i in range(columns):
                copies.append((part.at[at[i]], out[0].at[i, span]))
                if apart:
                    target = out[2].at[span] if i == 0 else out[1].at[i - 1, span]
                else:
                    target = out[1].at[i, span]
                copies.append((part.at[at[columns + i]], target))
        return copies

    def shape(*lead):
        return jax.ShapeDtypeStruct(lead + (sum(rows), grads.shape[-1]), jnp.bfloat16)

    away_shapes = [shape(columns - 1), shape()] if apart else [shape(columns)]
    return copy_call(
        copies_of,
        [c * 2 + side for c in order] + [c * 2 + 1 - side for c in order],
        parts,
        [shape(columns)] + away_shapes,
        2 * columns * len(parts),
        (pl.ANY, pltpu.VMEM),
    )


def wide_sum(*values):
    total = values[0].astype(jnp.float32)
    for value in values[1:]:
        total = total + value.astype(jnp.float32)
    return total


def turn_sums(stay, got):
    lacking = stay.shape[0] - got.shape[0]
    columns, _, turn = ring_pairs(lax.axis_size("fsdp"))
    return [
        lax.ppermute(
            wide_sum(stay[step], got[step - lacking]).astype(jnp.bfloat16), "fsdp", turn(step)
        )
        for step in range(1, columns)
    ]


def head_prep(raw, gain, cosine, sine):
    recip = lax.rsqrt(jnp.mean(raw * raw, axis=-1, keepdims=True) + EPS)
    hat = raw * recip
    scaled = hat * gain
    half_size = raw.shape[-1] // 2
    return hat, recip, scaled * cosine + pltpu.roll(scaled, half_size, 1) * sine


def head_back(grad, gain, cosine, sine, hat, recip):
    half_size = grad.shape[-1] // 2
    unrot = grad * cosine - pltpu.roll(grad, half_size, 1) * sine
    gain_grad = jnp.sum(unrot * hat, axis=0, keepdims=True)
    scaled = unrot * gain
    return gain_grad, recip * (scaled - hat * jnp.mean(scaled * hat, axis=-1, keepdims=True))


def nt_dot(left, right):
    return lax.dot_general(
        left, right, (((1,), (1,)), ((), ())), preferred_element_type=jnp.float32
    )


LOG2_E = 1.4426950408889634


def key_mask(segment_col, segment_row, key_rows, query_rows, diagonal):
    same = segment_col[key_rows, :] == segment_row[:, query_rows]
    if not diagonal:
        return same
    size = (key_rows.stop - key_rows.start, query_rows.stop - query_rows.start)
    key_at = lax.broadcasted_iota(jnp.int32, size, 0)
    query_at = lax.broadcasted_iota(jnp.int32, size, 1)
    return same & (key_at <= query_at)


def attend_kernel(
    group_size,
    block,
    raw_ref,
    cosine_ref,
    sine_ref,
    qgain_ref,
    kgain_ref,
    segment_col,
    segment_row,
    out_ref,
    lse_ref,
    query_scr,
    key_scr,
    value_scr,
):
    tok_count, head_size = cosine_ref.shape
    factor = head_size ** (-0.5) * LOG2_E
    blocks = [slice(i, i + block) for i in range(0, tok_count, block)]
    key_col, value_col = group_size * head_size, (group_size + 1) * head_size
    for rows in blocks:
        cosine, sine = cosine_ref[rows, :], sine_ref[rows, :]
        for h in range(group_size):
            cols = slice(h * head_size, (h + 1) * head_size)
            query_scr[rows, cols] = head_prep(raw_ref[rows, cols], qgain_ref[...], cosine, sine)[
                2
            ].astype(jnp.bfloat16)
        key_scr[rows, :] = head_prep(
            raw_ref[rows, key_col:value_col], kgain_ref[...], cosine, sine
        )[2].astype(jnp.bfloat16)
        value_scr[:, rows] = raw_ref[rows, value_col:].T.astype(jnp.bfloat16)
    for h in range(group_size):
        cols = slice(h * head_size, (h + 1) * head_size)
        for i, query_rows in enumerate(blocks):
            query = query_scr[query_rows, cols]
            total = jnp.zeros((1, block), jnp.float32)
            mixed = jnp.zeros((head_size, block), jnp.float32)
            for j, key_rows in enumerate(blocks[: i + 1]):
                scores = nt_dot(key_scr[key_rows, :], query)
                mask = key_mask(segment_col, segment_row, key_rows, query_rows, i == j)
                terms = jnp.where(mask, jnp.exp2(scores * factor), 0.0)
                total = total + jnp.sum(terms, axis=0, keepdims=True)
                mixed = mixed + jnp.dot(
                    value_scr[:, key_rows],
                    terms.astype(jnp.bfloat16),
                    preferred_element_type=jnp.float32,
                )
            out_ref[query_rows, cols] = (mixed * (1.0 / total)).T.astype(jnp.bfloat16)
            lse_ref[0, h : h + 1, query_rows] = jnp.log2(total)


def attend_back_kernel(
    group_size,
    block,
    raw_ref,
    out_ref,
    grad_ref,
    lse_ref,
    cosine_ref,
    sine_ref,
    qgain_ref,
    kgain_ref,
    segment_col,
    segment_row,
    back_ref,
    gains_ref,
    hat_scr,
    recip_scr,
    query_scr,
    key_scr,
    key_turned,
    value_scr,
    grad_key,
    grad_value,
):
    tok_count, head_size = cosine_ref.shape
    scale = head_size ** (-0.5)
    factor = scale * LOG2_E
    blocks = [slice(i, i + block) for i in range(0, tok_count, block)]
    key_col, value_col = group_size * head_size, (group_size + 1) * head_size
    head_cols = [slice(h * head_size, (h + 1) * head_size) for h in range(group_size + 1)]
    for rows in blocks:
        cosine, sine = cosine_ref[rows, :], sine_ref[rows, :]
        for h, cols in enumerate(head_cols):
            gain = qgain_ref[...] if h < group_size else kgain_ref[...]
            hat, recip, turned = head_prep(raw_ref[rows, cols], gain, cosine, sine)
            hat_scr[rows, cols] = hat
            recip_scr[rows, cols] = jnp.broadcast_to(recip, hat.shape)
            if h < group_size:
                query_scr[rows, cols] = turned.astype(jnp.bfloat16)
            else:
                key_scr[rows, :] = turned.astype(jnp.bfloat16)
                key_turned[:, rows] = turned.T.astype(jnp.bfloat16)
        value_scr[rows, :] = raw_ref[rows, value_col:].astype(jnp.bfloat16)
    query_gain_grad = jnp.zeros((1, head_size), jnp.float32)
    for h, cols in enumerate(head_cols[:group_size]):
        for i, query_rows in enumerate(blocks):
            query = query_scr[query_rows, cols]
            grad = grad_ref[query_rows, cols]
            delta = jnp.sum(
                (grad.astype(jnp.float32) * out_ref[query_rows, cols].astype(jnp.float32)).T,
                axis=0,
                keepdims=True,
            )
            lse = lse_ref[0, h : h + 1, query_rows]
            grad_query = jnp.zeros((head_size, block), jnp.float32)
            for j, key_rows in enumerate(blocks[: i + 1]):
                scores = nt_dot(key_scr[key_rows, :], query)
                mask = key_mask(segment_col, segment_row, key_rows, query_rows, i == j)
                probs = jnp.where(mask, jnp.exp2(scores * factor - lse), 0.0)
                grad_probs = nt_dot(value_scr[key_rows, :], grad)
                grad_scores = (probs * (grad_probs - delta)).astype(jnp.bfloat16)
                value_part = jnp.dot(
                    probs.astype(jnp.bfloat16), grad, preferred_element_type=jnp.float32
                )
                key_part = jnp.dot(grad_scores, query, preferred_element_type=jnp.float32)
                grad_query = grad_query + jnp.dot(
                    key_turned[:, key_rows], grad_scores, preferred_element_type=jnp.float32
                )
                if h == 0 and i == j:
                    grad_value[key_rows, :] = value_part
                    grad_key[key_rows, :] = key_part
                else:
                    grad_value[key_rows, :] += value_part
                    grad_key[key_rows, :] += key_part
            gain_grad, back = head_back(
                grad_query.T * scale,
                qgain_ref[...],
                cosine_ref[query_rows, :],
                sine_ref[query_rows, :],
                hat_scr[query_rows, cols],
                recip_scr[query_rows, cols],
            )
            query_gain_grad = query_gain_grad + gain_grad
            back_ref[query_rows, cols] = back.astype(jnp.bfloat16)
    key_gain_grad = jnp.zeros((1, head_size), jnp.float32)
    for rows in blocks:
        gain_grad, back = head_back(
            grad_key[rows, :] * scale,
            kgain_ref[...],
            cosine_ref[rows, :],
            sine_ref[rows, :],
            hat_scr[rows, head_cols[-1]],
            recip_scr[rows, head_cols[-1]],
        )
        key_gain_grad = key_gain_grad + gain_grad
        back_ref[rows, key_col:value_col] = back.astype(jnp.bfloat16)
        back_ref[rows, value_col:] = grad_value[rows, :].astype(jnp.bfloat16)
    gains_ref[0, 0:1, :] = query_gain_grad
    gains_ref[0, 1:2, :] = key_gain_grad


def attention_calls(tok_count, head_size, group_size, first, kv_heads):
    block = min(256, tok_count)
    wide = (group_size + 2) * head_size
    whole = pl.BlockSpec((tok_count, head_size), lambda g: (0, 0))
    gain = pl.BlockSpec((1, head_size), lambda g: (0, 0))
    common = [
        whole,
        whole,
        gain,
        gain,
        pl.BlockSpec((tok_count, 1), lambda g: (0, 0)),
        pl.BlockSpec((1, tok_count), lambda g: (0, 0)),
    ]
    raw = pl.BlockSpec((tok_count, wide), lambda g: (0, first + g))
    heads = pl.BlockSpec((tok_count, group_size * head_size), lambda g: (0, first + g))
    lse = pl.BlockSpec((1, group_size, tok_count), lambda g: (first + g, 0, 0))
    raw_out = pl.BlockSpec((tok_count, wide), lambda g: (0, g))
    heads_out = pl.BlockSpec((tok_count, group_size * head_size), lambda g: (0, g))
    lse_out = pl.BlockSpec((1, group_size, tok_count), lambda g: (g, 0, 0))
    pairs = kv_heads * group_size * tok_count * tok_count
    low, full = jnp.bfloat16, jnp.float32
    limit = pltpu.CompilerParams(vmem_limit_bytes=44 * 1024 * 1024)

    def forward(earlier, *operands):
        count = len(earlier)
        return pl.pallas_call(
            lambda *refs: attend_kernel(group_size, block, *refs[count:]),
            grid=(kv_heads,),
            in_specs=[pl.BlockSpec(memory_space=pl.ANY)] * count + [raw] + common,
            out_specs=[heads_out, lse_out],
            out_shape=[
                jax.ShapeDtypeStruct((tok_count, kv_heads * group_size * head_size), low),
                jax.ShapeDtypeStruct((kv_heads, group_size, tok_count), full),
            ],
            scratch_shapes=[
                pltpu.VMEM((tok_count, group_size * head_size), low),
                pltpu.VMEM((tok_count, head_size), low),
                pltpu.VMEM((head_size, tok_count), low),
            ],
            compiler_params=limit,
            cost_estimate=pl.CostEstimate(
                flops=pairs, bytes_accessed=0, transcendentals=0
            ),
        )(*earlier, *operands)

    def backward(earlier, *operands):
        count = len(earlier)
        return pl.pallas_call(
            lambda *refs: attend_back_kernel(group_size, block, *refs[count:]),
            grid=(kv_heads,),
            in_specs=[pl.BlockSpec(memory_space=pl.ANY)] * count + [raw, heads, heads, lse] + common,
            out_specs=[raw_out, pl.BlockSpec((1, 2, head_size), lambda g: (g, 0, 0))],
            out_shape=[
                jax.ShapeDtypeStruct((tok_count, kv_heads * wide), low),
                jax.ShapeDtypeStruct((kv_heads, 2, head_size), full),
            ],
            scratch_shapes=[
                pltpu.VMEM((tok_count, (group_size + 1) * head_size), full),
                pltpu.VMEM((tok_count, (group_size + 1) * head_size), full),
                pltpu.VMEM((tok_count, group_size * head_size), low),
                pltpu.VMEM((tok_count, head_size), low),
                pltpu.VMEM((head_size, tok_count), low),
                pltpu.VMEM((tok_count, head_size), low),
                pltpu.VMEM((tok_count, head_size), full),
                pltpu.VMEM((tok_count, head_size), full),
            ],
            compiler_params=limit,
            cost_estimate=pl.CostEstimate(
                flops=pairs, bytes_accessed=0, transcendentals=0
            ),
        )(*earlier, *operands)

    return forward, backward


def sum_cores(partial_of, c_index):
    got = swap(partial_of(1 - c_index).astype(jnp.bfloat16), "tensor")
    return (partial_of(c_index) + got.astype(jnp.float32)).astype(jnp.bfloat16)


def cross_sum(mine):
    return wide_sum(mine, swap(mine, "context")).astype(jnp.bfloat16)


def sum_part(mine, x_index):
    got = swap(half_of(mine, 1 - x_index, 0), "context")
    return wide_sum(half_of(mine, x_index, 0), got)


def dot_rows(left, right):
    return jnp.dot(left, right, preferred_element_type=jnp.float32)


def dot_back(left, right):
    return jnp.einsum("pf,df->pd", left, right, preferred_element_type=jnp.float32)


def dot_grad(left, right):
    return jnp.einsum("pd,pf->df", left, right, preferred_element_type=jnp.float32)


def quarter_shards(
    hidden_in,
    cotangent,
    segment,
    position,
    w_query,
    w_key,
    w_value,
    w_output,
    w_gate,
    w_up,
    w_down,
    attn_gain,
    ffn_gain,
    query_gain,
    key_gain,
):
    x_index, c_index = lax.axis_index("context"), lax.axis_index("tensor")
    fsdp_size = lax.axis_size("fsdp")
    rows_shard = w_query.shape[0]
    model = rows_shard * fsdp_size
    head_size = query_gain.shape[0] * fsdp_size
    q_width, kv_width = w_query.shape[1] // 2, w_key.shape[1] // 2
    ff_width = w_gate.shape[1] // 2
    q_heads, kv_heads = q_width // head_size, kv_width // head_size
    group_size = q_heads // kv_heads
    group_width = group_size * head_size

    def mine(weight, axis):
        return half_of(weight, x_index, axis)

    gains = jnp.concatenate([attn_gain, ffn_gain, query_gain, key_gain])
    gain_rows = jnp.pad(gains[None], ((0, 15), (0, q_width + 2 * kv_width - gains.shape[0])))
    blob_a = pack_call(x_index, kv_heads, head_size, w_query, w_key, w_value, gain_rows)
    blob_o = mine(w_output, 0).T
    blob_g, blob_u = mine(w_gate, 1), mine(w_up, 1)
    blob_d = mine(w_down, 0).T

    def own_part(rows):
        return half_of(half_of(rows, x_index, 0), c_index, 1)

    def wide_half(weight, h):
        return half_of(weight, h, 0)

    def grouped(grads):
        return grads.astype(jnp.bfloat16).reshape(fsdp_size, rows_shard, -1)

    def stacked(pieces):
        return stack_pieces(pieces[0], pieces[1:])

    hidden_other = swap(hidden_in[0], "tensor")
    hidden_other, blob_a = fence(hidden_other, blob_a)

    turned_a = turn_pieces(blob_a)
    far_own_a = flip_pieces(blob_a)
    hidden_wide = pair_join(c_index, hidden_in[0], hidden_other, 1)
    hidden_got = swap(hidden_wide, "context")
    last = len(turned_a) // 2
    far_a = [
        far_own_a if step == 0 else None if step == last else flip_pieces(piece)
        for step, piece in enumerate(turned_a)
    ]
    far_a.pop(last)
    turned_a, far_a, hidden_wide, hidden_got, blob_o, blob_g, blob_u, blob_d = fence(
        turned_a, far_a, hidden_wide, hidden_got, blob_o, blob_g, blob_u, blob_d
    )

    far_last = flip_pieces(turned_a[last])
    turned_o = turn_pieces(blob_o)
    marks = jnp.stack([segment[0], position[0]])
    marks_got = swap(marks, "context")
    hidden_rows = pair_join(x_index, hidden_wide, hidden_got, 0)
    x_rows = hidden_rows.astype(jnp.float32)
    tok_count = x_rows.shape[0]
    recip_one = norm_stats(x_rows)
    far_a, far_last, turned_o, hidden_rows, recip_one, marks_got, blob_g, turned_a, cotangent = (
        fence(
            far_a, far_last, turned_o, hidden_rows, recip_one, marks_got, blob_g, turned_a,
            cotangent,
        )
    )

    near_o = stacked(turned_o)
    far_o = flip_pieces(near_o)
    turned_g = turn_pieces(blob_g)
    dy_got = swap(cotangent[0], "context")
    marks = pair_join(x_index, marks, marks_got, 1)
    segment_all, position_all = marks[0], marks[1]
    half_size = head_size // 2
    freq_table = THETA ** (-jnp.arange(half_size, dtype=jnp.float32) * 2.0 / head_size)
    angle_table = position_all.astype(jnp.float32)[:, None] * freq_table[None, :]
    cosine_half, sine_half = jnp.cos(angle_table), jnp.sin(angle_table)
    cosine_table = jnp.concatenate([cosine_half, cosine_half], axis=1)
    sine_table = jnp.concatenate([-sine_half, sine_half], axis=1)
    all_a = place_rows(turned_a, far_a[:last] + [far_last] + far_a[last:])
    w_qkv = all_a[:, :rows_shard].reshape(model, -1)
    gain_all = all_a[:, rows_shard].astype(jnp.float32)
    gain_part = query_gain.shape[0]
    attn_gain32 = gain_all[:, :rows_shard].reshape(model)
    ffn_gain32 = gain_all[:, rows_shard : 2 * rows_shard].reshape(model)
    qgain32 = gain_all[:, 2 * rows_shard : 2 * rows_shard + gain_part].reshape(head_size)
    kgain32 = gain_all[:, 2 * rows_shard + gain_part : 2 * rows_shard + 2 * gain_part].reshape(
        head_size
    )
    x_rows = hidden_rows.astype(jnp.float32)
    attn_in = (x_rows * recip_one * attn_gain32).astype(jnp.bfloat16)
    qkv_raw = dot_rows(attn_in, w_qkv)
    qkv_raw, far_o, near_o, turned_g, dy_got, blob_u, cosine_table, sine_table = fence(
        qkv_raw, far_o, near_o, turned_g, dy_got, blob_u, cosine_table, sine_table
    )

    near_g = stacked(turned_g)
    far_g = flip_pieces(near_g)
    turned_u = turn_pieces(blob_u)
    shared = (
        cosine_table,
        sine_table,
        qgain32[None],
        kgain32[None],
        segment_all[:, None],
        segment_all[None, :],
    )
    attend, _ = attention_calls(tok_count, head_size, group_size, 0, kv_heads)
    attn_low, log_total = attend((), qkv_raw, *shared)
    all_o = place_rows([near_o], [far_o]).reshape(model, -1)
    attn_low, all_o, far_g, near_g, turned_u, blob_d, dy_got, cotangent = fence(
        attn_low, all_o, far_g, near_g, turned_u, blob_d, dy_got, cotangent
    )

    attn_mine = sum_cores(lambda h: dot_back(attn_low, wide_half(all_o, h)), c_index)
    near_u = stack_pieces(after(turned_u[0], attn_mine), turned_u[1:])
    far_u = flip_pieces(near_u)
    turned_d = turn_pieces(blob_d)
    attn_total = cross_sum(attn_mine)
    all_g = place_rows([near_g], [far_g]).reshape(model, -1)
    dy_column = pair_join(x_index, cotangent[0], dy_got, 0)
    rows_dy = pair_join(c_index, dy_column, swap(dy_column, "tensor"), 1)
    all_u = place_rows([near_u], [far_u]).reshape(model, -1)
    far_own_d = flip_pieces(after(blob_d, far_u))
    attn_total, all_g, all_u, turned_d, far_own_d, rows_dy = fence(
        attn_total, all_g, all_u, turned_d, far_own_d, rows_dy
    )

    attn_other = swap(attn_total, "tensor")
    near_d = stack_pieces(turned_d[1], turned_d[2:])
    far_d = flip_pieces(near_d)
    mid_rows = x_rows + pair_join(c_index, attn_total, attn_other, 1).astype(jnp.float32)
    recip_two = norm_stats(mid_rows)
    normed_two = mid_rows * recip_two
    ffn_in = (normed_two * ffn_gain32).astype(jnp.bfloat16)
    gate_pre, up_pre = dot_rows(ffn_in, all_g), dot_rows(ffn_in, all_u)
    gate_sig = jax.nn.sigmoid(gate_pre)
    hidden_low = (gate_pre * gate_sig * up_pre).astype(jnp.bfloat16)
    stay_d, away_d, apart_d = split_rows(grouped(dot_grad(rows_dy, hidden_low)), apart=True)
    gate_pre, up_pre, far_d, near_d, ffn_in, all_g, all_u, stay_d, away_d, apart_d, hidden_low = fence(
        gate_pre, up_pre, far_d, near_d, ffn_in, all_g, all_u, stay_d, away_d, apart_d, hidden_low
    )

    got_d = flip_pieces(away_d)
    gate_sig = jax.nn.sigmoid(gate_pre)
    gate_act = gate_pre * gate_sig
    all_d = place_rows([turned_d[0], near_d], [far_own_d, far_d]).reshape(model, -1)
    grad_hidden = dot_rows(rows_dy, all_d)
    grad_gate = (grad_hidden * up_pre * gate_sig * (1.0 + gate_pre * (1.0 - gate_sig))).astype(
        jnp.bfloat16
    )
    grad_up_pre = (grad_hidden * gate_act).astype(jnp.bfloat16)
    ffn_mine = sum_cores(
        lambda h: dot_back(grad_gate, wide_half(all_g, h))
        + dot_back(grad_up_pre, wide_half(all_u, h)),
        c_index,
    )
    ffn_total = cross_sum(ffn_mine)
    sent_d = turn_sums(after(stay_d, ffn_mine), got_d)
    stay_g, away_g, apart_g = split_rows(
        grouped(dot_grad(ffn_in, after(grad_gate, ffn_mine))), apart=True
    )
    got_g = flip_pieces(after(away_g, got_d))
    stay_u, away_u, apart_u = split_rows(
        grouped(dot_grad(ffn_in, after(grad_up_pre, ffn_mine))), apart=True
    )
    late_hidden = after(hidden_low, ffn_mine)
    out_away = dot_back(late_hidden, wide_half(all_d, 1 - c_index)).astype(jnp.bfloat16)
    out_stay = dot_back(late_hidden, wide_half(all_d, c_index))
    (
        ffn_total, stay_d, apart_d, sent_d, stay_g, got_g, apart_g, stay_u, away_u, apart_u,
        out_away, out_stay, rows_dy, mid_rows,
    ) = fence(
        ffn_total, stay_d, apart_d, sent_d, stay_g, got_g, apart_g, stay_u, away_u, apart_u,
        out_away, out_stay, rows_dy, mid_rows,
    )

    def finish(stay, got, sent, earlier=()):
        low = wide_sum(stay[0], got, *sent).astype(jnp.bfloat16)
        return low, swap(after(low, *earlier), "context")

    ffn_other = swap(ffn_total, "tensor")
    got_u = flip_pieces(away_u)
    sent_g = turn_sums(stay_g, got_g)
    out_other = swap(after(out_away, ffn_other), "tensor")
    out_mine = wide_sum(out_stay, out_other).astype(jnp.bfloat16)
    grad_ffn_in = pair_join(c_index, ffn_total, ffn_other, 1).astype(jnp.float32)
    normed_two = mid_rows * recip_two
    grad_ffn_gain = jnp.sum(grad_ffn_in * normed_two, axis=0)
    grad_mid = rows_dy.astype(jnp.float32) + norm_back(
        grad_ffn_in * ffn_gain32, normed_two, recip_two
    )
    grad_mid_low = grad_mid.astype(jnp.bfloat16)
    grad_attn = dot_rows(grad_mid_low, all_o).astype(jnp.bfloat16)
    stay_o, away_o = split_rows(grouped(dot_grad(grad_mid_low, attn_low)))
    (
        got_u, stay_u, sent_g, stay_g, sent_d, stay_d, grad_attn, away_o, stay_o, apart_d, apart_g,
        apart_u, attn_in, mid_rows, out_mine,
    ) = fence(
        got_u, stay_u, sent_g, stay_g, sent_d, stay_d, grad_attn, away_o, stay_o, apart_d, apart_g,
        apart_u, attn_in, mid_rows, out_mine,
    )

    got_o = flip_pieces(away_o)
    sent_u = turn_sums(stay_u, got_u)
    half_heads = kv_heads // 2
    _, back_first = attention_calls(tok_count, head_size, group_size, 0, half_heads)
    _, back_second = attention_calls(tok_count, head_size, group_size, half_heads, half_heads)
    back_a, gains_a = back_first((), qkv_raw, attn_low, grad_attn, log_total, *shared)
    stay_a, away_a = split_rows(grouped(dot_grad(attn_in, back_a)))
    got_own_d = flip_pieces(apart_d)
    (
        got_o, stay_o, sent_u, stay_u, sent_g, stay_g, back_a, gains_a, stay_a, away_a, grad_attn,
        attn_in, mid_rows, out_mine, got_own_d, stay_d, sent_d, apart_g, apart_u,
    ) = fence(
        got_o, stay_o, sent_u, stay_u, sent_g, stay_g, back_a, gains_a, stay_a, away_a, grad_attn,
        attn_in, mid_rows, out_mine, got_own_d, stay_d, sent_d, apart_g, apart_u,
    )

    got_a = flip_pieces(away_a)
    sent_o = turn_sums(stay_o, got_o)
    back_b, gains_b = back_second((), qkv_raw, attn_low, grad_attn, log_total, *shared)
    out_got = swap(half_of(out_mine, 1 - x_index, 0), "context")
    (
        got_a, stay_a, sent_o, stay_o, got_o, back_a, back_b, gains_a, gains_b, attn_in, mid_rows,
        out_mine, out_got, apart_g, apart_u, got_own_d, stay_d, sent_d, stay_u, sent_u, stay_g, sent_g,
    ) = fence(
        got_a, stay_a, sent_o, stay_o, got_o, back_a, back_b, gains_a, gains_b, attn_in, mid_rows,
        out_mine, out_got, apart_g, apart_u, got_own_d, stay_d, sent_d, stay_u, sent_u, stay_g, sent_g,
    )

    got_own_g = flip_pieces(apart_g)
    got_own_u = flip_pieces(apart_u)
    own_o, far_o = finish(stay_o, got_o[0], sent_o)
    own_d, far_d = finish(stay_d, got_own_d, sent_d)
    back = jnp.concatenate([back_a, back_b], axis=1)
    normed_one = x_rows * recip_one
    gain_halves = {}

    def attn_part(h):
        part = dot_back(back, wide_half(w_qkv, h))
        gain_halves[len(gain_halves)] = jnp.sum(part * half_of(normed_one, h, 1), axis=0)
        return part

    attn_in_mine = sum_cores(attn_part, c_index)
    grad_attn_gain = pair_join(c_index, gain_halves[1], gain_halves[0], 0)
    head_gains = jnp.sum(gains_a, axis=0) + jnp.sum(gains_b, axis=0)
    first_device = (x_index == 0) & (c_index == 0)
    gain_block = jnp.concatenate(
        [
            grad_attn_gain.reshape(fsdp_size, rows_shard),
            jnp.where(first_device, grad_ffn_gain, 0.0).reshape(fsdp_size, rows_shard),
            head_gains[0].reshape(fsdp_size, gain_part),
            head_gains[1].reshape(fsdp_size, gain_part),
        ],
        axis=1,
    ).astype(jnp.bfloat16)
    gain_block = gain_block.astype(jnp.float32) + swap(gain_block, "tensor").astype(jnp.float32)
    gain_block = jnp.pad(
        gain_block.astype(jnp.bfloat16)[:, None],
        ((0, 0), (0, 15), (0, back_b.shape[1] - gain_block.shape[1])),
    )
    stay_b, away_b = split_rows(grouped(dot_grad(attn_in, back_b)), gain_block)
    (
        stay_a, got_a, attn_in_mine, stay_b, away_b, mid_rows, out_mine, out_got, got_own_g,
        got_own_u, stay_g, sent_g, stay_u, sent_u, own_o, far_o, own_d, far_d,
    ) = fence(
        stay_a, got_a, attn_in_mine, stay_b, away_b, mid_rows, out_mine, out_got, got_own_g,
        got_own_u, stay_g, sent_g, stay_u, sent_u, own_o, far_o, own_d, far_d,
    )

    got_b = flip_pieces(away_b)
    sent_a = turn_sums(stay_a, got_a)
    attn_in_part = sum_part(attn_in_mine, x_index).astype(jnp.bfloat16)
    (
        got_b, stay_b, stay_a, got_a, sent_a, attn_in_part, got_own_g, stay_g, sent_g, got_own_u,
        stay_u, sent_u, mid_rows, out_mine, out_got,
    ) = fence(
        got_b, stay_b, stay_a, got_a, sent_a, attn_in_part, got_own_g, stay_g, sent_g, got_own_u,
        stay_u, sent_u, mid_rows, out_mine, out_got,
    )

    out_part = wide_sum(half_of(out_mine, x_index, 0), out_got)
    block_out = (own_part(mid_rows) + out_part).astype(jnp.bfloat16)[None]
    sent_b = turn_sums(stay_b, got_b)
    attn_in_other = swap(attn_in_part, "tensor")
    own_a, far_a = finish(stay_a, got_a[0], sent_a)
    own_g, far_g = finish(stay_g, got_own_g, sent_g, (far_a,))
    grad_attn_in = pair_join(c_index, attn_in_part, attn_in_other, 1).astype(jnp.float32)
    normed_part = half_of(x_rows * recip_one, x_index, 0)
    grad_input = half_of(grad_mid, x_index, 0) + norm_back(
        grad_attn_in * attn_gain32, normed_part, half_of(recip_one, x_index, 0)
    )
    grad_input_part = half_of(grad_input, c_index, 1)[None]
    (
        sent_b, stay_b, got_b, own_a, far_a, own_g, far_g, grad_input_part, block_out, got_own_u,
        stay_u, sent_u,
    ) = fence(
        sent_b, stay_b, got_b, own_a, far_a, own_g, far_g, grad_input_part, block_out, got_own_u,
        stay_u, sent_u,
    )

    own_u, far_u = finish(stay_u, got_own_u, sent_u)
    own_b, far_b = finish(stay_b, got_b[0], sent_b)
    gain_sum = own_b[rows_shard].astype(jnp.float32) + far_b[rows_shard].astype(jnp.float32)

    def outcome(own, far):
        return pair_join(x_index, own, far, 1).astype(jnp.float32)

    def outcome_columns(own, far):
        return pair_join(x_index, own.T, far.T, 0).astype(jnp.float32)

    def picked(first, size):
        wide = group_width + 2 * head_size
        starts = [g * wide + first for g in range(kv_heads // 2)]

        def columns(halves):
            return jnp.concatenate(
                [half[:rows_shard, s : s + size] for half in halves for s in starts], axis=1
            )

        return pair_join(x_index, columns((own_a, own_b)), columns((far_a, far_b)), 1).astype(
            jnp.float32
        )

    return (
        block_out,
        grad_input_part,
        picked(0, group_width),
        picked(group_width, head_size),
        picked(group_width + head_size, head_size),
        outcome_columns(own_o, far_o),
        outcome(own_g, far_g),
        outcome(own_u, far_u),
        outcome_columns(own_d, far_d),
        gain_sum[:rows_shard],
        gain_sum[rows_shard : 2 * rows_shard],
        gain_sum[2 * rows_shard : 2 * rows_shard + gain_part],
        gain_sum[2 * rows_shard + gain_part : 2 * rows_shard + 2 * gain_part],
    )


def fits_quarters(mesh):
    sizes = mesh.shape
    return sizes["context"] == 2 and sizes["tensor"] == 2 and sizes["fsdp"] % 2 == 0


def solution(mesh):
    in_specs = (
        P("fsdp", "context", "tensor"),
        P("fsdp", "context", "tensor"),
        P("fsdp", "context"),
        P("fsdp", "context"),
        P("fsdp", "tensor"),
        P("fsdp", "tensor"),
        P("fsdp", "tensor"),
        P("tensor", "fsdp"),
        P("fsdp", "tensor"),
        P("fsdp", "tensor"),
        P("tensor", "fsdp"),
        P("fsdp"),
        P("fsdp"),
        P("fsdp"),
        P("fsdp"),
    )
    out_specs = (
        P("fsdp", "context", "tensor"),
        P("fsdp", "context", "tensor"),
        P("fsdp", "tensor"),
        P("fsdp", "tensor"),
        P("fsdp", "tensor"),
        P("tensor", "fsdp"),
        P("fsdp", "tensor"),
        P("fsdp", "tensor"),
        P("tensor", "fsdp"),
        P("fsdp"),
        P("fsdp"),
        P("fsdp"),
        P("fsdp"),
    )
    shards = quarter_shards if fits_quarters(mesh) else plain_shards
    return jax.shard_map(shards, mesh=mesh, in_specs=in_specs, out_specs=out_specs, check_vma=False)
```

```python
import jax
import jax.numpy as jnp
from jax import lax
from jax.experimental import pallas as pl
from jax.experimental.pallas import tpu as pltpu
from jax.sharding import PartitionSpec as P

EPS = 1e-06
THETA = 1000000.0


def norm_stats(values):
    return lax.rsqrt(jnp.mean(values * values, axis=-1, keepdims=True) + EPS)


def norm_back(grad_out, normed, recip_root):
    return recip_root * (grad_out - normed * jnp.mean(grad_out * normed, axis=-1, keepdims=True))


def rotary_tables(position_row, head_size):
    half_size = head_size // 2
    freq_table = THETA ** (-jnp.arange(half_size, dtype=jnp.float32) * 2.0 / head_size)
    angle_table = position_row.astype(jnp.float32)[:, None] * freq_table[None, :]
    return (jnp.cos(angle_table)[:, None, :], jnp.sin(angle_table)[:, None, :])


def rotate(values, cosine_table, sine_table, turn_sign):
    half_size = values.shape[-1] // 2
    first_half = values[..., :half_size]
    second_half = values[..., half_size:]
    turned = turn_sign * sine_table
    return jnp.concatenate(
        [
            first_half * cosine_table - second_half * turned,
            second_half * cosine_table + first_half * turned,
        ],
        axis=-1,
    )


def plain_shards(
    hidden_in,
    cotangent,
    segment,
    position,
    w_query,
    w_key,
    w_value,
    w_output,
    w_gate,
    w_up,
    w_down,
    attn_gain,
    ffn_gain,
    query_gain,
    key_gain,
):
    (
        wq_full,
        wk_full,
        wv_full,
        wo_full,
        wg_full,
        wu_full,
        wd_full,
        attn_full,
        ffn_full,
        qgain_full,
        kgain_full,
    ) = (
        lax.all_gather(w_query, "fsdp", axis=0, tiled=True),
        lax.all_gather(w_key, "fsdp", axis=0, tiled=True),
        lax.all_gather(w_value, "fsdp", axis=0, tiled=True),
        lax.all_gather(w_output, "fsdp", axis=1, tiled=True),
        lax.all_gather(w_gate, "fsdp", axis=0, tiled=True),
        lax.all_gather(w_up, "fsdp", axis=0, tiled=True),
        lax.all_gather(w_down, "fsdp", axis=1, tiled=True),
        lax.all_gather(attn_gain, "fsdp", axis=0, tiled=True),
        lax.all_gather(ffn_gain, "fsdp", axis=0, tiled=True),
        lax.all_gather(query_gain, "fsdp", axis=0, tiled=True),
        lax.all_gather(key_gain, "fsdp", axis=0, tiled=True),
    )
    rows_x, rows_dy = (
        lax.all_gather(hidden_in[0], "tensor", axis=1, tiled=True),
        lax.all_gather(cotangent[0], "tensor", axis=1, tiled=True),
    )
    tok_count = rows_x.shape[0]
    feat_part = hidden_in.shape[2]
    head_size = qgain_full.shape[0]
    q_heads = wq_full.shape[1] // head_size
    kv_heads = wk_full.shape[1] // head_size
    group_size = q_heads // kv_heads
    score_scale = head_size ** (-0.5)
    x_rows = rows_x.astype(jnp.float32)
    recip_one = norm_stats(x_rows)
    normed_one = x_rows * recip_one
    attn_gain32 = attn_full.astype(jnp.float32)
    attn_in = (normed_one * attn_gain32).astype(jnp.bfloat16)
    query_raw = jnp.dot(attn_in, wq_full, preferred_element_type=jnp.float32).reshape(
        tok_count, q_heads, head_size
    )
    key_raw = jnp.dot(attn_in, wk_full, preferred_element_type=jnp.float32).reshape(
        tok_count, kv_heads, head_size
    )
    value_raw = jnp.dot(attn_in, wv_full, preferred_element_type=jnp.float32)
    cosine_table, sine_table = rotary_tables(position[0], head_size)
    recip_query = norm_stats(query_raw)
    query_hat = query_raw * recip_query
    qgain32 = qgain_full.astype(jnp.float32)
    query_rot = rotate(query_hat * qgain32, cosine_table, sine_table, 1.0).astype(jnp.bfloat16)
    recip_key = norm_stats(key_raw)
    key_hat = key_raw * recip_key
    kgain32 = kgain_full.astype(jnp.float32)
    key_rot = rotate(key_hat * kgain32, cosine_table, sine_table, 1.0).astype(jnp.bfloat16)
    value_low = value_raw.astype(jnp.bfloat16).reshape(tok_count, kv_heads, head_size)
    key_all, value_all, segment_all = (
        lax.all_gather(key_rot, "context", axis=0, tiled=True),
        lax.all_gather(value_low, "context", axis=0, tiled=True),
        lax.all_gather(segment[0], "context", axis=0, tiled=True),
    )
    query_index = lax.axis_index("context") * tok_count + jnp.arange(tok_count, dtype=jnp.int32)
    key_index = jnp.arange(key_all.shape[0], dtype=jnp.int32)
    allowed = (segment[0][:, None] == segment_all[None, :]) & (
        key_index[None, :] <= query_index[:, None]
    )
    query_group = query_rot.reshape(tok_count, kv_heads, group_size, head_size)

    def scores_of():
        raw_scores = (
            jnp.einsum("pkgd,lkd->kgpl", query_group, key_all, preferred_element_type=jnp.float32)
            * score_scale
        )
        return jnp.where(allowed, raw_scores, -1e30)

    masked = scores_of()
    row_max = jnp.max(masked, axis=-1, keepdims=True)
    exp_terms = jnp.exp(masked - row_max)
    row_total = jnp.sum(exp_terms, axis=-1, keepdims=True)
    log_total = row_max + jnp.log(row_total)
    probs_fwd = (exp_terms / row_total).astype(jnp.bfloat16)
    attn_rows = jnp.einsum(
        "kgpl,lkd->pkgd", probs_fwd, value_all, preferred_element_type=jnp.float32
    )
    attn_low = attn_rows.reshape(tok_count, q_heads * head_size).astype(jnp.bfloat16)
    attn_sum = lax.psum(
        jnp.dot(attn_low, wo_full, preferred_element_type=jnp.float32).astype(jnp.bfloat16),
        "tensor",
    ).astype(jnp.float32)
    mid_rows = x_rows + attn_sum
    recip_two = norm_stats(mid_rows)
    normed_two = mid_rows * recip_two
    ffn_gain32 = ffn_full.astype(jnp.float32)
    ffn_in = (normed_two * ffn_gain32).astype(jnp.bfloat16)
    gate_pre = jnp.dot(ffn_in, wg_full, preferred_element_type=jnp.float32)
    up_pre = jnp.dot(ffn_in, wu_full, preferred_element_type=jnp.float32)
    gate_sig = jax.nn.sigmoid(gate_pre)
    gate_act = gate_pre * gate_sig
    hidden_low = (gate_act * up_pre).astype(jnp.bfloat16)
    ffn_rows = lax.psum_scatter(
        jnp.dot(hidden_low, wd_full, preferred_element_type=jnp.float32).astype(jnp.bfloat16),
        "tensor",
        scatter_dimension=1,
        tiled=True,
    ).astype(jnp.float32)
    feat_first = lax.axis_index("tensor") * feat_part
    mid_part = lax.dynamic_slice_in_dim(mid_rows, feat_first, feat_part, 1)
    block_out = (mid_part + ffn_rows).astype(jnp.bfloat16)[None]
    (
        wq_full,
        wk_full,
        wv_full,
        wo_full,
        wg_full,
        wu_full,
        wd_full,
        attn_full,
        ffn_full,
        qgain_full,
        kgain_full,
    ) = (
        lax.all_gather(w_query, "fsdp", axis=0, tiled=True),
        lax.all_gather(w_key, "fsdp", axis=0, tiled=True),
        lax.all_gather(w_value, "fsdp", axis=0, tiled=True),
        lax.all_gather(w_output, "fsdp", axis=1, tiled=True),
        lax.all_gather(w_gate, "fsdp", axis=0, tiled=True),
        lax.all_gather(w_up, "fsdp", axis=0, tiled=True),
        lax.all_gather(w_down, "fsdp", axis=1, tiled=True),
        lax.all_gather(attn_gain, "fsdp", axis=0, tiled=True),
        lax.all_gather(ffn_gain, "fsdp", axis=0, tiled=True),
        lax.all_gather(query_gain, "fsdp", axis=0, tiled=True),
        lax.all_gather(key_gain, "fsdp", axis=0, tiled=True),
    )
    grad_w_down = jnp.einsum("pf,pd->fd", hidden_low, rows_dy, preferred_element_type=jnp.float32)
    grad_hidden = jnp.einsum("pd,fd->pf", rows_dy, wd_full, preferred_element_type=jnp.float32)
    grad_gate = (grad_hidden * up_pre * gate_sig * (1.0 + gate_pre * (1.0 - gate_sig))).astype(
        jnp.bfloat16
    )
    grad_up_pre = (grad_hidden * gate_act).astype(jnp.bfloat16)
    grad_w_gate = jnp.einsum("pd,pf->df", ffn_in, grad_gate, preferred_element_type=jnp.float32)
    grad_w_up = jnp.einsum("pd,pf->df", ffn_in, grad_up_pre, preferred_element_type=jnp.float32)
    ffn_in_part = jnp.einsum(
        "pf,df->pd", grad_gate, wg_full, preferred_element_type=jnp.float32
    ) + jnp.einsum("pf,df->pd", grad_up_pre, wu_full, preferred_element_type=jnp.float32)
    grad_ffn_in = lax.psum(ffn_in_part.astype(jnp.bfloat16), "tensor").astype(jnp.float32)
    grad_ffn_gain = jnp.sum(grad_ffn_in * normed_two, axis=0)
    grad_mid = rows_dy.astype(jnp.float32) + norm_back(
        grad_ffn_in * ffn_gain32, normed_two, recip_two
    )
    grad_mid_low = grad_mid.astype(jnp.bfloat16)
    grad_w_output = jnp.einsum(
        "pf,pd->fd", attn_low, grad_mid_low, preferred_element_type=jnp.float32
    )
    grad_attn = jnp.einsum("pd,fd->pf", grad_mid_low, wo_full, preferred_element_type=jnp.float32)
    grad_attn = grad_attn.astype(jnp.bfloat16).reshape(tok_count, kv_heads, group_size, head_size)
    soft_probs = jnp.exp(scores_of() - log_total)
    grad_probs = jnp.einsum(
        "pkgd,lkd->kgpl", grad_attn, value_all, preferred_element_type=jnp.float32
    )
    row_delta = jnp.sum(soft_probs * grad_probs, axis=-1, keepdims=True)
    grad_scores = (soft_probs * (grad_probs - row_delta)).astype(jnp.bfloat16)
    probs_low = soft_probs.astype(jnp.bfloat16)
    grad_query = (
        jnp.einsum("kgpl,lkd->pkgd", grad_scores, key_all, preferred_element_type=jnp.float32)
        * score_scale
    )
    grad_query = grad_query.reshape(tok_count, q_heads, head_size)
    grad_key_rows = (
        jnp.einsum("kgpl,pkgd->lkd", grad_scores, query_group, preferred_element_type=jnp.float32)
        * score_scale
    )
    grad_value_rows = jnp.einsum(
        "kgpl,pkgd->lkd", probs_low, grad_attn, preferred_element_type=jnp.float32
    )
    key_value_grads = lax.psum_scatter(
        jnp.concatenate(
            [
                grad_key_rows.reshape(tok_count * lax.axis_size("context"), -1),
                grad_value_rows.reshape(tok_count * lax.axis_size("context"), -1),
            ],
            axis=1,
        ).astype(jnp.bfloat16),
        "context",
        scatter_dimension=0,
        tiled=True,
    ).astype(jnp.float32)
    kv_width = kv_heads * head_size
    grad_key = key_value_grads[:, :kv_width].reshape(tok_count, kv_heads, head_size)
    grad_value_low = key_value_grads[:, kv_width:].astype(jnp.bfloat16)
    unrot_query = rotate(grad_query, cosine_table, sine_table, -1.0)
    grad_query_gain = jnp.sum(unrot_query * query_hat, axis=(0, 1))
    grad_query_raw = (
        norm_back(unrot_query * qgain32, query_hat, recip_query)
        .astype(jnp.bfloat16)
        .reshape(tok_count, q_heads * head_size)
    )
    unrot_key = rotate(grad_key, cosine_table, sine_table, -1.0)
    grad_key_gain = jnp.sum(unrot_key * key_hat, axis=(0, 1))
    grad_key_raw = (
        norm_back(unrot_key * kgain32, key_hat, recip_key)
        .astype(jnp.bfloat16)
        .reshape(tok_count, kv_width)
    )
    grad_w_query = jnp.einsum(
        "pd,pf->df", attn_in, grad_query_raw, preferred_element_type=jnp.float32
    )
    grad_w_key = jnp.einsum("pd,pf->df", attn_in, grad_key_raw, preferred_element_type=jnp.float32)
    grad_w_value = jnp.einsum(
        "pd,pf->df", attn_in, grad_value_low, preferred_element_type=jnp.float32
    )
    attn_in_part = (
        jnp.einsum("pf,df->pd", grad_query_raw, wq_full, preferred_element_type=jnp.float32)
        + jnp.einsum("pf,df->pd", grad_key_raw, wk_full, preferred_element_type=jnp.float32)
        + jnp.einsum("pf,df->pd", grad_value_low, wv_full, preferred_element_type=jnp.float32)
    )
    grad_attn_in, grad_query_gain, grad_key_gain = (
        lax.psum(attn_in_part.astype(jnp.bfloat16), "tensor").astype(jnp.float32),
        lax.psum(grad_query_gain.astype(jnp.bfloat16), "tensor").astype(jnp.float32),
        lax.psum(grad_key_gain.astype(jnp.bfloat16), "tensor").astype(jnp.float32),
    )
    grad_attn_gain = jnp.sum(grad_attn_in * normed_one, axis=0)
    grad_input = grad_mid + norm_back(
        grad_attn_in * attn_full.astype(jnp.float32), normed_one, recip_one
    )
    grad_input_part = lax.dynamic_slice_in_dim(grad_input, feat_first, feat_part, 1)[None]
    owned = (
        lax.psum_scatter(
            grad_w_query.astype(jnp.bfloat16), "fsdp", scatter_dimension=0, tiled=True
        ).astype(jnp.float32),
        lax.psum_scatter(
            grad_w_key.astype(jnp.bfloat16), "fsdp", scatter_dimension=0, tiled=True
        ).astype(jnp.float32),
        lax.psum_scatter(
            grad_w_value.astype(jnp.bfloat16), "fsdp", scatter_dimension=0, tiled=True
        ).astype(jnp.float32),
        lax.psum_scatter(
            grad_w_output.astype(jnp.bfloat16), "fsdp", scatter_dimension=1, tiled=True
        ).astype(jnp.float32),
        lax.psum_scatter(
            grad_w_gate.astype(jnp.bfloat16), "fsdp", scatter_dimension=0, tiled=True
        ).astype(jnp.float32),
        lax.psum_scatter(
            grad_w_up.astype(jnp.bfloat16), "fsdp", scatter_dimension=0, tiled=True
        ).astype(jnp.float32),
        lax.psum_scatter(
            grad_w_down.astype(jnp.bfloat16), "fsdp", scatter_dimension=1, tiled=True
        ).astype(jnp.float32),
        lax.psum_scatter(
            grad_attn_gain.astype(jnp.bfloat16), "fsdp", scatter_dimension=0, tiled=True
        ).astype(jnp.float32),
        lax.psum_scatter(
            grad_ffn_gain.astype(jnp.bfloat16), "fsdp", scatter_dimension=0, tiled=True
        ).astype(jnp.float32),
        lax.psum_scatter(
            grad_query_gain.astype(jnp.bfloat16), "fsdp", scatter_dimension=0, tiled=True
        ).astype(jnp.float32),
        lax.psum_scatter(
            grad_key_gain.astype(jnp.bfloat16), "fsdp", scatter_dimension=0, tiled=True
        ).astype(jnp.float32),
    )
    owned = (
        lax.psum(owned[0].astype(jnp.bfloat16), "context").astype(jnp.float32),
        lax.psum(owned[1].astype(jnp.bfloat16), "context").astype(jnp.float32),
        lax.psum(owned[2].astype(jnp.bfloat16), "context").astype(jnp.float32),
        lax.psum(owned[3].astype(jnp.bfloat16), "context").astype(jnp.float32),
        lax.psum(owned[4].astype(jnp.bfloat16), "context").astype(jnp.float32),
        lax.psum(owned[5].astype(jnp.bfloat16), "context").astype(jnp.float32),
        lax.psum(owned[6].astype(jnp.bfloat16), "context").astype(jnp.float32),
        lax.psum(owned[7].astype(jnp.bfloat16), "context").astype(jnp.float32),
        lax.psum(owned[8].astype(jnp.bfloat16), "context").astype(jnp.float32),
        lax.psum(owned[9].astype(jnp.bfloat16), "context").astype(jnp.float32),
        lax.psum(owned[10].astype(jnp.bfloat16), "context").astype(jnp.float32),
    )
    return (
        block_out,
        grad_input_part,
        owned[0],
        owned[1],
        owned[2],
        owned[3],
        owned[4],
        owned[5],
        owned[6],
        owned[7],
        owned[8],
        owned[9],
        owned[10],
    )


def fence(*values):
    return lax.optimization_barrier(values)


def after(value, *earlier):
    return lax.optimization_barrier((value,) + earlier)[0]


def swap(values, axis_name):
    return lax.ppermute(values, axis_name, [(0, 1), (1, 0)])


def pick(index, zero_item, one_item):
    return jnp.where(index == 0, zero_item, one_item)


def pair_join(index, own, other, axis):
    return jnp.concatenate([pick(index, own, other), pick(index, other, own)], axis=axis)


def half_of(values, index, axis):
    half = values.shape[axis] // 2
    return lax.dynamic_slice_in_dim(values, index * half, half, axis)


def ring_pairs(fsdp_size):
    columns = fsdp_size // 2
    flip = [(i, i ^ 1) for i in range(fsdp_size)]

    def turn(step):
        return [
            (z * 2 + y, ((z + step) % columns) * 2 + y) for z in range(columns) for y in range(2)
        ]

    return columns, flip, turn


def copy_call(copies_of, scalars, operands, shapes, copy_count, spaces):
    operand_count, result_count = len(operands), len(shapes)

    def kernel(scalar_ref, *refs):
        sources = refs[:operand_count]
        targets = refs[operand_count : operand_count + result_count]
        sems = refs[operand_count + result_count]
        copies = [
            pltpu.make_async_copy(source, target, sems.at[i])
            for i, (source, target) in enumerate(copies_of(scalar_ref, sources, targets))
        ]
        for copy in copies:
            copy.start()
        for copy in copies:
            copy.wait()

    moved = sum(2 * shape.size * shape.dtype.itemsize for shape in shapes)
    return pl.pallas_call(
        kernel,
        out_shape=shapes,
        in_specs=[pl.BlockSpec(memory_space=pltpu.SMEM)]
        + [pl.BlockSpec(memory_space=spaces[0])] * operand_count,
        out_specs=[pl.BlockSpec(memory_space=spaces[1])] * result_count,
        scratch_shapes=[pltpu.SemaphoreType.DMA((copy_count,))],
        compiler_params=pltpu.CompilerParams(vmem_limit_bytes=32 * 1024 * 1024),
        cost_estimate=pl.CostEstimate(flops=0, bytes_accessed=moved, transcendentals=0),
    )(jnp.stack(scalars).astype(jnp.int32), *operands)


def pack_call(x_index, kv_heads, head_size, w_query, w_key, w_value, gain_rows):
    rows, q_columns = w_query.shape
    group_width = q_columns // (2 * kv_heads)
    wide = group_width + 2 * head_size

    def kernel(x_ref, query_ref, key_ref, value_ref, gain_ref, out_ref):
        x = x_ref[0]
        for g in range(kv_heads):
            first = g * wide
            for ref, size in ((query_ref, group_width), (key_ref, head_size), (value_ref, head_size)):
                start = pl.multiple_of((x * kv_heads + g) * size, size)
                out_ref[:rows, first : first + size] = ref[:, pl.ds(start, size)]
                first += size
        out_ref[rows:, :] = gain_ref[...]

    return pl.pallas_call(
        kernel,
        out_shape=jax.ShapeDtypeStruct(
            (rows + gain_rows.shape[0], kv_heads * wide), w_query.dtype
        ),
        in_specs=[pl.BlockSpec(memory_space=pltpu.SMEM)]
        + [pl.BlockSpec(memory_space=pltpu.VMEM)] * 4,
        out_specs=pl.BlockSpec(memory_space=pltpu.VMEM),
    )(x_index.astype(jnp.int32)[None], w_query, w_key, w_value, gain_rows)


def turn_pieces(blob):
    columns, _, turn = ring_pairs(lax.axis_size("fsdp"))
    return [blob] + [lax.ppermute(blob, "fsdp", turn(step)) for step in range(1, columns)]


def flip_pieces(values):
    return lax.ppermute(values, "fsdp", ring_pairs(lax.axis_size("fsdp"))[1])


def stack_pieces(first, rest):
    pieces = [first] + list(rest)
    shape = (len(pieces),) + pieces[0].shape
    return copy_call(
        lambda at, own, out: [(piece, out[0].at[i]) for i, piece in enumerate(own)],
        [jnp.int32(0)],
        pieces,
        [jax.ShapeDtypeStruct(shape, pieces[0].dtype)],
        len(pieces),
        (pltpu.VMEM, pl.ANY),
    )[0]


def place_rows(near, far):
    fsdp_size = lax.axis_size("fsdp")
    columns = fsdp_size // 2
    place = lax.axis_index("fsdp")
    column, side = place // 2, place % 2
    sources = [(column - step + columns) % columns for step in range(columns)]
    near_at = [source * 2 + side for source in sources]
    far_at = [source * 2 + 1 - side for source in sources]
    operands = list(near) + list(far)

    def copies_of(at, own, out):
        copies, slot = [], 0
        for ref in own:
            if len(ref.shape) == 2:
                copies.append((ref, out[0].at[at[slot]]))
                slot += 1
                continue
            for i in range(ref.shape[0]):
                copies.append((ref.at[i], out[0].at[at[slot]]))
                slot += 1
        return copies

    return copy_call(
        copies_of,
        near_at + far_at,
        operands,
        [jax.ShapeDtypeStruct((fsdp_size,) + near[0].shape[-2:], near[0].dtype)],
        fsdp_size,
        (pltpu.VMEM, pl.ANY),
    )[0]


def split_rows(grads, extra=None, apart=False):
    fsdp_size = lax.axis_size("fsdp")
    columns = fsdp_size // 2
    place = lax.axis_index("fsdp")
    column, side = place // 2, place % 2
    parts = [grads] if extra is None else [grads, extra]
    rows = [part.shape[1] for part in parts]
    firsts = [0, rows[0]]
    order = [(column + step) % columns for step in range(columns)]

    def copies_of(at, own, out):
        copies = []
        for part, first, count in zip(own, firsts, rows):
            span = pl.ds(first, count)
            for i in range(columns):
                copies.append((part.at[at[i]], out[0].at[i, span]))
                if apart:
                    target = out[2].at[span] if i == 0 else out[1].at[i - 1, span]
                else:
                    target = out[1].at[i, span]
                copies.append((part.at[at[columns + i]], target))
        return copies

    def shape(*lead):
        return jax.ShapeDtypeStruct(lead + (sum(rows), grads.shape[-1]), jnp.bfloat16)

    away_shapes = [shape(columns - 1), shape()] if apart else [shape(columns)]
    return copy_call(
        copies_of,
        [c * 2 + side for c in order] + [c * 2 + 1 - side for c in order],
        parts,
        [shape(columns)] + away_shapes,
        2 * columns * len(parts),
        (pl.ANY, pltpu.VMEM),
    )


def wide_sum(*values):
    total = values[0].astype(jnp.float32)
    for value in values[1:]:
        total = total + value.astype(jnp.float32)
    return total


def turn_sums(stay, got):
    lacking = stay.shape[0] - got.shape[0]
    columns, _, turn = ring_pairs(lax.axis_size("fsdp"))
    return [
        lax.ppermute(
            wide_sum(stay[step], got[step - lacking]).astype(jnp.bfloat16), "fsdp", turn(step)
        )
        for step in range(1, columns)
    ]


def head_prep(raw, gain, cosine, sine):
    recip = lax.rsqrt(jnp.mean(raw * raw, axis=-1, keepdims=True) + EPS)
    hat = raw * recip
    scaled = hat * gain
    half_size = raw.shape[-1] // 2
    return hat, recip, scaled * cosine + pltpu.roll(scaled, half_size, 1) * sine


def head_back(grad, gain, cosine, sine, hat, recip):
    half_size = grad.shape[-1] // 2
    unrot = grad * cosine - pltpu.roll(grad, half_size, 1) * sine
    gain_grad = jnp.sum(unrot * hat, axis=0, keepdims=True)
    scaled = unrot * gain
    return gain_grad, recip * (scaled - hat * jnp.mean(scaled * hat, axis=-1, keepdims=True))


def nt_dot(left, right):
    return lax.dot_general(
        left, right, (((1,), (1,)), ((), ())), preferred_element_type=jnp.float32
    )


LOG2_E = 1.4426950408889634


def key_mask(segment_col, segment_row, key_rows, query_rows, diagonal):
    same = segment_col[key_rows, :] == segment_row[:, query_rows]
    if not diagonal:
        return same
    size = (key_rows.stop - key_rows.start, query_rows.stop - query_rows.start)
    key_at = lax.broadcasted_iota(jnp.int32, size, 0)
    query_at = lax.broadcasted_iota(jnp.int32, size, 1)
    return same & (key_at <= query_at)


def attend_kernel(
    group_size,
    block,
    raw_ref,
    cosine_ref,
    sine_ref,
    qgain_ref,
    kgain_ref,
    segment_col,
    segment_row,
    out_ref,
    lse_ref,
    query_scr,
    key_scr,
    value_scr,
):
    tok_count, head_size = cosine_ref.shape
    factor = head_size ** (-0.5) * LOG2_E
    blocks = [slice(i, i + block) for i in range(0, tok_count, block)]
    key_col, value_col = group_size * head_size, (group_size + 1) * head_size
    for rows in blocks:
        cosine, sine = cosine_ref[rows, :], sine_ref[rows, :]
        for h in range(group_size):
            cols = slice(h * head_size, (h + 1) * head_size)
            query_scr[rows, cols] = head_prep(raw_ref[rows, cols], qgain_ref[...], cosine, sine)[
                2
            ].astype(jnp.bfloat16)
        key_scr[rows, :] = head_prep(
            raw_ref[rows, key_col:value_col], kgain_ref[...], cosine, sine
        )[2].astype(jnp.bfloat16)
        value_scr[:, rows] = raw_ref[rows, value_col:].T.astype(jnp.bfloat16)
    for h in range(group_size):
        cols = slice(h * head_size, (h + 1) * head_size)
        for i, query_rows in enumerate(blocks):
            query = query_scr[query_rows, cols]
            total = jnp.zeros((1, block), jnp.float32)
            mixed = jnp.zeros((head_size, block), jnp.float32)
            for j, key_rows in enumerate(blocks[: i + 1]):
                scores = nt_dot(key_scr[key_rows, :], query)
                mask = key_mask(segment_col, segment_row, key_rows, query_rows, i == j)
                terms = jnp.where(mask, jnp.exp2(scores * factor), 0.0)
                total = total + jnp.sum(terms, axis=0, keepdims=True)
                mixed = mixed + jnp.dot(
                    value_scr[:, key_rows],
                    terms.astype(jnp.bfloat16),
                    preferred_element_type=jnp.float32,
                )
            out_ref[query_rows, cols] = (mixed * (1.0 / total)).T.astype(jnp.bfloat16)
            lse_ref[0, h : h + 1, query_rows] = jnp.log2(total)


def attend_back_kernel(
    group_size,
    block,
    raw_ref,
    out_ref,
    grad_ref,
    lse_ref,
    cosine_ref,
    sine_ref,
    qgain_ref,
    kgain_ref,
    segment_col,
    segment_row,
    back_ref,
    gains_ref,
    hat_scr,
    recip_scr,
    query_scr,
    key_scr,
    key_turned,
    value_scr,
    grad_key,
    grad_value,
):
    tok_count, head_size = cosine_ref.shape
    scale = head_size ** (-0.5)
    factor = scale * LOG2_E
    blocks = [slice(i, i + block) for i in range(0, tok_count, block)]
    key_col, value_col = group_size * head_size, (group_size + 1) * head_size
    head_cols = [slice(h * head_size, (h + 1) * head_size) for h in range(group_size + 1)]
    for rows in blocks:
        cosine, sine = cosine_ref[rows, :], sine_ref[rows, :]
        for h, cols in enumerate(head_cols):
            gain = qgain_ref[...] if h < group_size else kgain_ref[...]
            hat, recip, turned = head_prep(raw_ref[rows, cols], gain, cosine, sine)
            hat_scr[rows, cols] = hat
            recip_scr[rows, cols] = jnp.broadcast_to(recip, hat.shape)
            if h < group_size:
                query_scr[rows, cols] = turned.astype(jnp.bfloat16)
            else:
                key_scr[rows, :] = turned.astype(jnp.bfloat16)
                key_turned[:, rows] = turned.T.astype(jnp.bfloat16)
        value_scr[rows, :] = raw_ref[rows, value_col:].astype(jnp.bfloat16)
    query_gain_grad = jnp.zeros((1, head_size), jnp.float32)
    for h, cols in enumerate(head_cols[:group_size]):
        for i, query_rows in enumerate(blocks):
            query = query_scr[query_rows, cols]
            grad = grad_ref[query_rows, cols]
            delta = jnp.sum(
                (grad.astype(jnp.float32) * out_ref[query_rows, cols].astype(jnp.float32)).T,
                axis=0,
                keepdims=True,
            )
            lse = lse_ref[0, h : h + 1, query_rows]
            grad_query = jnp.zeros((head_size, block), jnp.float32)
            for j, key_rows in enumerate(blocks[: i + 1]):
                scores = nt_dot(key_scr[key_rows, :], query)
                mask = key_mask(segment_col, segment_row, key_rows, query_rows, i == j)
                probs = jnp.where(mask, jnp.exp2(scores * factor - lse), 0.0)
                grad_probs = nt_dot(value_scr[key_rows, :], grad)
                grad_scores = (probs * (grad_probs - delta)).astype(jnp.bfloat16)
                value_part = jnp.dot(
                    probs.astype(jnp.bfloat16), grad, preferred_element_type=jnp.float32
                )
                key_part = jnp.dot(grad_scores, query, preferred_element_type=jnp.float32)
                grad_query = grad_query + jnp.dot(
                    key_turned[:, key_rows], grad_scores, preferred_element_type=jnp.float32
                )
                if h == 0 and i == j:
                    grad_value[key_rows, :] = value_part
                    grad_key[key_rows, :] = key_part
                else:
                    grad_value[key_rows, :] += value_part
                    grad_key[key_rows, :] += key_part
            gain_grad, back = head_back(
                grad_query.T * scale,
                qgain_ref[...],
                cosine_ref[query_rows, :],
                sine_ref[query_rows, :],
                hat_scr[query_rows, cols],
                recip_scr[query_rows, cols],
            )
            query_gain_grad = query_gain_grad + gain_grad
            back_ref[query_rows, cols] = back.astype(jnp.bfloat16)
    key_gain_grad = jnp.zeros((1, head_size), jnp.float32)
    for rows in blocks:
        gain_grad, back = head_back(
            grad_key[rows, :] * scale,
            kgain_ref[...],
            cosine_ref[rows, :],
            sine_ref[rows, :],
            hat_scr[rows, head_cols[-1]],
            recip_scr[rows, head_cols[-1]],
        )
        key_gain_grad = key_gain_grad + gain_grad
        back_ref[rows, key_col:value_col] = back.astype(jnp.bfloat16)
        back_ref[rows, value_col:] = grad_value[rows, :].astype(jnp.bfloat16)
    gains_ref[0, 0:1, :] = query_gain_grad
    gains_ref[0, 1:2, :] = key_gain_grad


def attention_calls(tok_count, head_size, group_size, first, kv_heads):
    block = min(256, tok_count)
    wide = (group_size + 2) * head_size
    whole = pl.BlockSpec((tok_count, head_size), lambda g: (0, 0))
    gain = pl.BlockSpec((1, head_size), lambda g: (0, 0))
    common = [
        whole,
        whole,
        gain,
        gain,
        pl.BlockSpec((tok_count, 1), lambda g: (0, 0)),
        pl.BlockSpec((1, tok_count), lambda g: (0, 0)),
    ]
    raw = pl.BlockSpec((tok_count, wide), lambda g: (0, first + g))
    heads = pl.BlockSpec((tok_count, group_size * head_size), lambda g: (0, first + g))
    lse = pl.BlockSpec((1, group_size, tok_count), lambda g: (first + g, 0, 0))
    raw_out = pl.BlockSpec((tok_count, wide), lambda g: (0, g))
    heads_out = pl.BlockSpec((tok_count, group_size * head_size), lambda g: (0, g))
    lse_out = pl.BlockSpec((1, group_size, tok_count), lambda g: (g, 0, 0))
    pairs = kv_heads * group_size * tok_count * tok_count
    low, full = jnp.bfloat16, jnp.float32
    limit = pltpu.CompilerParams(vmem_limit_bytes=44 * 1024 * 1024)

    def forward(earlier, *operands):
        count = len(earlier)
        return pl.pallas_call(
            lambda *refs: attend_kernel(group_size, block, *refs[count:]),
            grid=(kv_heads,),
            in_specs=[pl.BlockSpec(memory_space=pl.ANY)] * count + [raw] + common,
            out_specs=[heads_out, lse_out],
            out_shape=[
                jax.ShapeDtypeStruct((tok_count, kv_heads * group_size * head_size), low),
                jax.ShapeDtypeStruct((kv_heads, group_size, tok_count), full),
            ],
            scratch_shapes=[
                pltpu.VMEM((tok_count, group_size * head_size), low),
                pltpu.VMEM((tok_count, head_size), low),
                pltpu.VMEM((head_size, tok_count), low),
            ],
            compiler_params=limit,
            cost_estimate=pl.CostEstimate(
                flops=pairs, bytes_accessed=0, transcendentals=0
            ),
        )(*earlier, *operands)

    def backward(earlier, *operands):
        count = len(earlier)
        return pl.pallas_call(
            lambda *refs: attend_back_kernel(group_size, block, *refs[count:]),
            grid=(kv_heads,),
            in_specs=[pl.BlockSpec(memory_space=pl.ANY)] * count + [raw, heads, heads, lse] + common,
            out_specs=[raw_out, pl.BlockSpec((1, 2, head_size), lambda g: (g, 0, 0))],
            out_shape=[
                jax.ShapeDtypeStruct((tok_count, kv_heads * wide), low),
                jax.ShapeDtypeStruct((kv_heads, 2, head_size), full),
            ],
            scratch_shapes=[
                pltpu.VMEM((tok_count, (group_size + 1) * head_size), full),
                pltpu.VMEM((tok_count, (group_size + 1) * head_size), full),
                pltpu.VMEM((tok_count, group_size * head_size), low),
                pltpu.VMEM((tok_count, head_size), low),
                pltpu.VMEM((head_size, tok_count), low),
                pltpu.VMEM((tok_count, head_size), low),
                pltpu.VMEM((tok_count, head_size), full),
                pltpu.VMEM((tok_count, head_size), full),
            ],
            compiler_params=limit,
            cost_estimate=pl.CostEstimate(
                flops=pairs, bytes_accessed=0, transcendentals=0
            ),
        )(*earlier, *operands)

    return forward, backward


def sum_cores(partial_of, c_index):
    got = swap(partial_of(1 - c_index).astype(jnp.bfloat16), "tensor")
    return (partial_of(c_index) + got.astype(jnp.float32)).astype(jnp.bfloat16)


def cross_sum(mine):
    return wide_sum(mine, swap(mine, "context")).astype(jnp.bfloat16)


def sum_part(mine, x_index):
    got = swap(half_of(mine, 1 - x_index, 0), "context")
    return wide_sum(half_of(mine, x_index, 0), got)


def dot_rows(left, right):
    return jnp.dot(left, right, preferred_element_type=jnp.float32)


def dot_back(left, right):
    return jnp.einsum("pf,df->pd", left, right, preferred_element_type=jnp.float32)


def dot_grad(left, right):
    return jnp.einsum("pd,pf->df", left, right, preferred_element_type=jnp.float32)


def quarter_shards(
    hidden_in,
    cotangent,
    segment,
    position,
    w_query,
    w_key,
    w_value,
    w_output,
    w_gate,
    w_up,
    w_down,
    attn_gain,
    ffn_gain,
    query_gain,
    key_gain,
):
    x_index, c_index = lax.axis_index("context"), lax.axis_index("tensor")
    fsdp_size = lax.axis_size("fsdp")
    rows_shard = w_query.shape[0]
    model = rows_shard * fsdp_size
    head_size = query_gain.shape[0] * fsdp_size
    q_width, kv_width = w_query.shape[1] // 2, w_key.shape[1] // 2
    ff_width = w_gate.shape[1] // 2
    q_heads, kv_heads = q_width // head_size, kv_width // head_size
    group_size = q_heads // kv_heads
    group_width = group_size * head_size

    def mine(weight, axis):
        return half_of(weight, x_index, axis)

    gains = jnp.concatenate([attn_gain, ffn_gain, query_gain, key_gain])
    gain_rows = jnp.pad(gains[None], ((0, 15), (0, q_width + 2 * kv_width - gains.shape[0])))
    blob_a = pack_call(x_index, kv_heads, head_size, w_query, w_key, w_value, gain_rows)
    blob_o = mine(w_output, 0).T
    blob_g, blob_u = mine(w_gate, 1), mine(w_up, 1)
    blob_d = mine(w_down, 0).T

    def own_part(rows):
        return half_of(half_of(rows, x_index, 0), c_index, 1)

    def wide_half(weight, h):
        return half_of(weight, h, 0)

    def grouped(grads):
        return grads.astype(jnp.bfloat16).reshape(fsdp_size, rows_shard, -1)

    def stacked(pieces):
        return stack_pieces(pieces[0], pieces[1:])

    hidden_other = swap(hidden_in[0], "tensor")
    hidden_other, blob_a = fence(hidden_other, blob_a)

    turned_a = turn_pieces(blob_a)
    far_own_a = flip_pieces(blob_a)
    hidden_wide = pair_join(c_index, hidden_in[0], hidden_other, 1)
    hidden_got = swap(hidden_wide, "context")
    last = len(turned_a) // 2
    far_a = [
        far_own_a if step == 0 else None if step == last else flip_pieces(piece)
        for step, piece in enumerate(turned_a)
    ]
    far_a.pop(last)
    turned_a, far_a, hidden_wide, hidden_got, blob_o, blob_g, blob_u, blob_d = fence(
        turned_a, far_a, hidden_wide, hidden_got, blob_o, blob_g, blob_u, blob_d
    )

    far_last = flip_pieces(turned_a[last])
    turned_o = turn_pieces(blob_o)
    marks = jnp.stack([segment[0], position[0]])
    marks_got = swap(marks, "context")
    hidden_rows = pair_join(x_index, hidden_wide, hidden_got, 0)
    x_rows = hidden_rows.astype(jnp.float32)
    tok_count = x_rows.shape[0]
    recip_one = norm_stats(x_rows)
    far_a, far_last, turned_o, hidden_rows, recip_one, marks_got, blob_g, turned_a, cotangent = (
        fence(
            far_a, far_last, turned_o, hidden_rows, recip_one, marks_got, blob_g, turned_a,
            cotangent,
        )
    )

    near_o = stacked(turned_o)
    far_o = flip_pieces(near_o)
    turned_g = turn_pieces(blob_g)
    dy_got = swap(cotangent[0], "context")
    marks = pair_join(x_index, marks, marks_got, 1)
    segment_all, position_all = marks[0], marks[1]
    half_size = head_size // 2
    freq_table = THETA ** (-jnp.arange(half_size, dtype=jnp.float32) * 2.0 / head_size)
    angle_table = position_all.astype(jnp.float32)[:, None] * freq_table[None, :]
    cosine_half, sine_half = jnp.cos(angle_table), jnp.sin(angle_table)
    cosine_table = jnp.concatenate([cosine_half, cosine_half], axis=1)
    sine_table = jnp.concatenate([-sine_half, sine_half], axis=1)
    all_a = place_rows(turned_a, far_a[:last] + [far_last] + far_a[last:])
    w_qkv = all_a[:, :rows_shard].reshape(model, -1)
    gain_all = all_a[:, rows_shard].astype(jnp.float32)
    gain_part = query_gain.shape[0]
    attn_gain32 = gain_all[:, :rows_shard].reshape(model)
    ffn_gain32 = gain_all[:, rows_shard : 2 * rows_shard].reshape(model)
    qgain32 = gain_all[:, 2 * rows_shard : 2 * rows_shard + gain_part].reshape(head_size)
    kgain32 = gain_all[:, 2 * rows_shard + gain_part : 2 * rows_shard + 2 * gain_part].reshape(
        head_size
    )
    x_rows = hidden_rows.astype(jnp.float32)
    attn_in = (x_rows * recip_one * attn_gain32).astype(jnp.bfloat16)
    qkv_raw = dot_rows(attn_in, w_qkv)
    qkv_raw, far_o, near_o, turned_g, dy_got, blob_u, cosine_table, sine_table = fence(
        qkv_raw, far_o, near_o, turned_g, dy_got, blob_u, cosine_table, sine_table
    )

    near_g = stacked(turned_g)
    far_g = flip_pieces(near_g)
    turned_u = turn_pieces(blob_u)
    shared = (
        cosine_table,
        sine_table,
        qgain32[None],
        kgain32[None],
        segment_all[:, None],
        segment_all[None, :],
    )
    attend, _ = attention_calls(tok_count, head_size, group_size, 0, kv_heads)
    attn_low, log_total = attend((), qkv_raw, *shared)
    all_o = place_rows([near_o], [far_o]).reshape(model, -1)
    attn_low, all_o, far_g, near_g, turned_u, blob_d, dy_got, cotangent = fence(
        attn_low, all_o, far_g, near_g, turned_u, blob_d, dy_got, cotangent
    )

    attn_mine = sum_cores(lambda h: dot_back(attn_low, wide_half(all_o, h)), c_index)
    near_u = stack_pieces(after(turned_u[0], attn_mine), turned_u[1:])
    far_u = flip_pieces(near_u)
    turned_d = turn_pieces(blob_d)
    attn_total = cross_sum(attn_mine)
    all_g = place_rows([near_g], [far_g]).reshape(model, -1)
    dy_column = pair_join(x_index, cotangent[0], dy_got, 0)
    rows_dy = pair_join(c_index, dy_column, swap(dy_column, "tensor"), 1)
    all_u = place_rows([near_u], [far_u]).reshape(model, -1)
    far_own_d = flip_pieces(after(blob_d, far_u))
    attn_total, all_g, all_u, turned_d, far_own_d, rows_dy = fence(
        attn_total, all_g, all_u, turned_d, far_own_d, rows_dy
    )

    attn_other = swap(attn_total, "tensor")
    near_d = stack_pieces(turned_d[1], turned_d[2:])
    far_d = flip_pieces(near_d)
    mid_rows = x_rows + pair_join(c_index, attn_total, attn_other, 1).astype(jnp.float32)
    recip_two = norm_stats(mid_rows)
    normed_two = mid_rows * recip_two
    ffn_in = (normed_two * ffn_gain32).astype(jnp.bfloat16)
    gate_pre, up_pre = dot_rows(ffn_in, all_g), dot_rows(ffn_in, all_u)
    gate_sig = jax.nn.sigmoid(gate_pre)
    hidden_low = (gate_pre * gate_sig * up_pre).astype(jnp.bfloat16)
    stay_d, away_d, apart_d = split_rows(grouped(dot_grad(rows_dy, hidden_low)), apart=True)
    gate_pre, up_pre, far_d, near_d, ffn_in, all_g, all_u, stay_d, away_d, apart_d, hidden_low = fence(
        gate_pre, up_pre, far_d, near_d, ffn_in, all_g, all_u, stay_d, away_d, apart_d, hidden_low
    )

    got_d = flip_pieces(away_d)
    gate_sig = jax.nn.sigmoid(gate_pre)
    gate_act = gate_pre * gate_sig
    all_d = place_rows([turned_d[0], near_d], [far_own_d, far_d]).reshape(model, -1)
    grad_hidden = dot_rows(rows_dy, all_d)
    grad_gate = (grad_hidden * up_pre * gate_sig * (1.0 + gate_pre * (1.0 - gate_sig))).astype(
        jnp.bfloat16
    )
    grad_up_pre = (grad_hidden * gate_act).astype(jnp.bfloat16)
    ffn_mine = sum_cores(
        lambda h: dot_back(grad_gate, wide_half(all_g, h))
        + dot_back(grad_up_pre, wide_half(all_u, h)),
        c_index,
    )
    ffn_total = cross_sum(ffn_mine)
    sent_d = turn_sums(after(stay_d, ffn_mine), got_d)
    stay_g, away_g, apart_g = split_rows(
        grouped(dot_grad(ffn_in, after(grad_gate, ffn_mine))), apart=True
    )
    got_g = flip_pieces(after(away_g, got_d))
    stay_u, away_u, apart_u = split_rows(
        grouped(dot_grad(ffn_in, after(grad_up_pre, ffn_mine))), apart=True
    )
    late_hidden = after(hidden_low, ffn_mine)
    out_away = dot_back(late_hidden, wide_half(all_d, 1 - c_index)).astype(jnp.bfloat16)
    out_stay = dot_back(late_hidden, wide_half(all_d, c_index))
    (
        ffn_total, stay_d, apart_d, sent_d, stay_g, got_g, apart_g, stay_u, away_u, apart_u,
        out_away, out_stay, rows_dy, mid_rows,
    ) = fence(
        ffn_total, stay_d, apart_d, sent_d, stay_g, got_g, apart_g, stay_u, away_u, apart_u,
        out_away, out_stay, rows_dy, mid_rows,
    )

    def finish(stay, got, sent, earlier=()):
        low = wide_sum(stay[0], got, *sent).astype(jnp.bfloat16)
        return low, swap(after(low, *earlier), "context")

    ffn_other = swap(ffn_total, "tensor")
    got_u = flip_pieces(away_u)
    sent_g = turn_sums(stay_g, got_g)
    out_other = swap(after(out_away, ffn_other), "tensor")
    out_mine = wide_sum(out_stay, out_other).astype(jnp.bfloat16)
    grad_ffn_in = pair_join(c_index, ffn_total, ffn_other, 1).astype(jnp.float32)
    normed_two = mid_rows * recip_two
    grad_ffn_gain = jnp.sum(grad_ffn_in * normed_two, axis=0)
    grad_mid = rows_dy.astype(jnp.float32) + norm_back(
        grad_ffn_in * ffn_gain32, normed_two, recip_two
    )
    grad_mid_low = grad_mid.astype(jnp.bfloat16)
    grad_attn = dot_rows(grad_mid_low, all_o).astype(jnp.bfloat16)
    stay_o, away_o = split_rows(grouped(dot_grad(grad_mid_low, attn_low)))
    (
        got_u, stay_u, sent_g, stay_g, sent_d, stay_d, grad_attn, away_o, stay_o, apart_d, apart_g,
        apart_u, attn_in, mid_rows, out_mine,
    ) = fence(
        got_u, stay_u, sent_g, stay_g, sent_d, stay_d, grad_attn, away_o, stay_o, apart_d, apart_g,
        apart_u, attn_in, mid_rows, out_mine,
    )

    got_o = flip_pieces(away_o)
    sent_u = turn_sums(stay_u, got_u)
    half_heads = kv_heads // 2
    _, back_first = attention_calls(tok_count, head_size, group_size, 0, half_heads)
    _, back_second = attention_calls(tok_count, head_size, group_size, half_heads, half_heads)
    back_a, gains_a = back_first((), qkv_raw, attn_low, grad_attn, log_total, *shared)
    stay_a, away_a = split_rows(grouped(dot_grad(attn_in, back_a)))
    got_own_d = flip_pieces(apart_d)
    (
        got_o, stay_o, sent_u, stay_u, sent_g, stay_g, back_a, gains_a, stay_a, away_a, grad_attn,
        attn_in, mid_rows, out_mine, got_own_d, stay_d, sent_d, apart_g, apart_u,
    ) = fence(
        got_o, stay_o, sent_u, stay_u, sent_g, stay_g, back_a, gains_a, stay_a, away_a, grad_attn,
        attn_in, mid_rows, out_mine, got_own_d, stay_d, sent_d, apart_g, apart_u,
    )

    got_a = flip_pieces(away_a)
    sent_o = turn_sums(stay_o, got_o)
    back_b, gains_b = back_second((), qkv_raw, attn_low, grad_attn, log_total, *shared)
    out_got = swap(half_of(out_mine, 1 - x_index, 0), "context")
    (
        got_a, stay_a, sent_o, stay_o, got_o, back_a, back_b, gains_a, gains_b, attn_in, mid_rows,
        out_mine, out_got, apart_g, apart_u, got_own_d, stay_d, sent_d, stay_u, sent_u, stay_g, sent_g,
    ) = fence(
        got_a, stay_a, sent_o, stay_o, got_o, back_a, back_b, gains_a, gains_b, attn_in, mid_rows,
        out_mine, out_got, apart_g, apart_u, got_own_d, stay_d, sent_d, stay_u, sent_u, stay_g, sent_g,
    )

    got_own_g = flip_pieces(apart_g)
    got_own_u = flip_pieces(apart_u)
    own_o, far_o = finish(stay_o, got_o[0], sent_o)
    own_d, far_d = finish(stay_d, got_own_d, sent_d)
    back = jnp.concatenate([back_a, back_b], axis=1)
    normed_one = x_rows * recip_one
    gain_halves = {}

    def attn_part(h):
        part = dot_back(back, wide_half(w_qkv, h))
        gain_halves[len(gain_halves)] = jnp.sum(part * half_of(normed_one, h, 1), axis=0)
        return part

    attn_in_mine = sum_cores(attn_part, c_index)
    grad_attn_gain = pair_join(c_index, gain_halves[1], gain_halves[0], 0)
    head_gains = jnp.sum(gains_a, axis=0) + jnp.sum(gains_b, axis=0)
    first_device = (x_index == 0) & (c_index == 0)
    gain_block = jnp.concatenate(
        [
            grad_attn_gain.reshape(fsdp_size, rows_shard),
            jnp.where(first_device, grad_ffn_gain, 0.0).reshape(fsdp_size, rows_shard),
            head_gains[0].reshape(fsdp_size, gain_part),
            head_gains[1].reshape(fsdp_size, gain_part),
        ],
        axis=1,
    ).astype(jnp.bfloat16)
    gain_block = gain_block.astype(jnp.float32) + swap(gain_block, "tensor").astype(jnp.float32)
    gain_block = jnp.pad(
        gain_block.astype(jnp.bfloat16)[:, None],
        ((0, 0), (0, 15), (0, back_b.shape[1] - gain_block.shape[1])),
    )
    stay_b, away_b = split_rows(grouped(dot_grad(attn_in, back_b)), gain_block)
    (
        stay_a, got_a, attn_in_mine, stay_b, away_b, mid_rows, out_mine, out_got, got_own_g,
        got_own_u, stay_g, sent_g, stay_u, sent_u, own_o, far_o, own_d, far_d,
    ) = fence(
        stay_a, got_a, attn_in_mine, stay_b, away_b, mid_rows, out_mine, out_got, got_own_g,
        got_own_u, stay_g, sent_g, stay_u, sent_u, own_o, far_o, own_d, far_d,
    )

    got_b = flip_pieces(away_b)
    sent_a = turn_sums(stay_a, got_a)
    attn_in_part = sum_part(attn_in_mine, x_index).astype(jnp.bfloat16)
    (
        got_b, stay_b, stay_a, got_a, sent_a, attn_in_part, got_own_g, stay_g, sent_g, got_own_u,
        stay_u, sent_u, mid_rows, out_mine, out_got,
    ) = fence(
        got_b, stay_b, stay_a, got_a, sent_a, attn_in_part, got_own_g, stay_g, sent_g, got_own_u,
        stay_u, sent_u, mid_rows, out_mine, out_got,
    )

    out_part = wide_sum(half_of(out_mine, x_index, 0), out_got)
    block_out = (own_part(mid_rows) + out_part).astype(jnp.bfloat16)[None]
    sent_b = turn_sums(stay_b, got_b)
    attn_in_other = swap(attn_in_part, "tensor")
    own_a, far_a = finish(stay_a, got_a[0], sent_a)
    own_g, far_g = finish(stay_g, got_own_g, sent_g, (far_a,))
    grad_attn_in = pair_join(c_index, attn_in_part, attn_in_other, 1).astype(jnp.float32)
    normed_part = half_of(x_rows * recip_one, x_index, 0)
    grad_input = half_of(grad_mid, x_index, 0) + norm_back(
        grad_attn_in * attn_gain32, normed_part, half_of(recip_one, x_index, 0)
    )
    grad_input_part = half_of(grad_input, c_index, 1)[None]
    own_u, far_u = finish(stay_u, got_own_u, sent_u, (far_g,))
    own_b, far_b = finish(stay_b, got_b[0], sent_b)
    gain_sum = own_b[rows_shard].astype(jnp.float32) + far_b[rows_shard].astype(jnp.float32)

    def outcome(own, far):
        return pair_join(x_index, own, far, 1).astype(jnp.float32)

    def outcome_columns(own, far):
        return pair_join(x_index, own.T, far.T, 0).astype(jnp.float32)

    def picked(first, size):
        wide = group_width + 2 * head_size
        starts = [g * wide + first for g in range(kv_heads // 2)]

        def columns(halves):
            return jnp.concatenate(
                [half[:rows_shard, s : s + size] for half in halves for s in starts], axis=1
            )

        return pair_join(x_index, columns((own_a, own_b)), columns((far_a, far_b)), 1).astype(
            jnp.float32
        )

    return (
        block_out,
        grad_input_part,
        picked(0, group_width),
        picked(group_width, head_size),
        picked(group_width + head_size, head_size),
        outcome_columns(own_o, far_o),
        outcome(own_g, far_g),
        outcome(own_u, far_u),
        outcome_columns(own_d, far_d),
        gain_sum[:rows_shard],
        gain_sum[rows_shard : 2 * rows_shard],
        gain_sum[2 * rows_shard : 2 * rows_shard + gain_part],
        gain_sum[2 * rows_shard + gain_part : 2 * rows_shard + 2 * gain_part],
    )


def fits_quarters(mesh):
    sizes = mesh.shape
    return sizes["context"] == 2 and sizes["tensor"] == 2 and sizes["fsdp"] % 2 == 0


def solution(mesh):
    in_specs = (
        P("fsdp", "context", "tensor"),
        P("fsdp", "context", "tensor"),
        P("fsdp", "context"),
        P("fsdp", "context"),
        P("fsdp", "tensor"),
        P("fsdp", "tensor"),
        P("fsdp", "tensor"),
        P("tensor", "fsdp"),
        P("fsdp", "tensor"),
        P("fsdp", "tensor"),
        P("tensor", "fsdp"),
        P("fsdp"),
        P("fsdp"),
        P("fsdp"),
        P("fsdp"),
    )
    out_specs = (
        P("fsdp", "context", "tensor"),
        P("fsdp", "context", "tensor"),
        P("fsdp", "tensor"),
        P("fsdp", "tensor"),
        P("fsdp", "tensor"),
        P("tensor", "fsdp"),
        P("fsdp", "tensor"),
        P("fsdp", "tensor"),
        P("tensor", "fsdp"),
        P("fsdp"),
        P("fsdp"),
        P("fsdp"),
        P("fsdp"),
    )
    shards = quarter_shards if fits_quarters(mesh) else plain_shards
    return jax.shard_map(shards, mesh=mesh, in_specs=in_specs, out_specs=out_specs, check_vma=False)
```
